32 devices in a mesh: box: 8 (over z, y), field: 4 (over x, core).
Axes of the slice: x: 2, y: 2, z: 4, core: 2. Of those that a mesh axis runs over, the one named last changes fastest.
Arguments:
- incident: bfloat16 [2, 2048, 4096], P(None, 'field', 'box'), may hold values from -6 to 6
- leaf_inverse: bfloat16 [8, 2, 512, 512], P('box', None, 'field'), may hold values from -0.1875 to 0.1875
- contrast: float32 [4096], P('box'), may hold values from 0.2 to 1
- skel_index: int32 [8, 2, 256], replicated, may hold values from 0 to 511
- ranks: int32 [8, 2], replicated, may hold values from 128 to 256, as said below
- top_core: bfloat16 [2, 256, 512], P(None, None, 'box'), may hold values from -0.25 to 0.25
Outputs:
- total_field: float32 [2, 2048, 4096], P(None, 'field', 'box')
The draws below stay inside these ranges and needn't reach their ends.
Inputs may be any that keep to these rules, and one draw needn't show every extreme that they name: At each level some box has rank exactly 256; most ranks lie near 256 // 2.
All inputs are finite; a program needn't handle non-finite values.
Results may differ from the reference program's by a relative error of at most 0.0003.
Values may be sent and summed in bfloat16 or wider, within the bound.
No kernel may reach another device: no remote copies, remote signals or barrier semaphores. Data moves between devices by JAX's collectives and lax.ppermute only.
A program may use at most 64 MiB of HBM per device.

```python
import math
import jax
import jax.numpy as jnp
from jax import lax

SIDE = 8
LEAF = 512
KMAX = 256
KQ = 64
NF = 2048
BOXES = 8
POINTS = 4096


def draw_ranks(key, part):
    key_a, key_b, key_c = jax.random.split(key, 3)
    spread = KMAX - KMAX // 2
    first = jax.random.randint(key_a, (BOXES, 2), 0, spread + 1)
    second = jax.random.randint(key_b, (BOXES, 2), 0, spread + 1)
    drawn = KMAX // 2 + first * second // spread
    chosen = jax.random.randint(key_c, (2,), 0, BOXES)
    drawn = drawn.at[chosen, jnp.arange(2)].set(KMAX)
    return drawn.astype(jnp.int32)


def touch_ends(values, rng, smallest, largest):
    shape = values.shape
    place = [jax.random.randint(jax.random.fold_in(rng, axis), (), 0, shape[axis]) for axis in range(len(shape))]
    values = values.at[tuple(place)].set(smallest)
    longest = shape.index(max(shape))
    place[longest] = (place[longest] + 1) % shape[longest]
    return values.at[tuple(place)].set(largest)


def block_scale(rng, dims, shards, least, high):
    gain = 1.0
    for axis_at, shards_of in shards:
        heights = jax.random.uniform(jax.random.fold_in(jax.random.fold_in(rng, 6), axis_at), (shards_of,), jnp.float32, least / len(shards), high / len(shards))
        gain = gain * jnp.repeat(jnp.exp(heights), dims[axis_at] // shards_of).reshape((-1,) + (1,) * (len(dims) - 1 - axis_at))
    return gain


def bell_draw(rng, dims, scale, most, shards=(), held_as=jnp.bfloat16):
    array = jax.random.normal(rng, dims, jnp.float32) * scale
    if len(shards) > 0:
        array = block_scale(rng, dims, shards, -0.22, 0.18) * array
    return jnp.clip(array, min=-most, max=most).astype(held_as)


def setup_inputs(seed: int = 0) -> dict:
    key_list = jax.random.split(jax.random.key(seed), 7)
    incident = bell_draw(key_list[0], (2, NF, POINTS), 1.0, 6.0, ((1, 4), (2, 8)))
    leaf_inverse = bell_draw(key_list[1], (BOXES, 2, LEAF, LEAF), (2 * LEAF) ** -0.5, 0.1875, ((0, 8), (2, 4)))
    contrast = jnp.clip(jnp.exp(math.log(1.0) - 1.609438 * jax.random.uniform(key_list[2], (POINTS,), jnp.float32) ** block_scale(key_list[2], (POINTS,), ((0, 8),), -0.2, 0.2)), 0.2, 1.0)
    skel_index = touch_ends(jax.random.randint(key_list[3], (BOXES, 2, KMAX), 0, LEAF), jax.random.fold_in(key_list[3], 1), 0, LEAF - 1).astype(jnp.int32)
    ranks = draw_ranks(jax.random.fold_in(key_list[6], 71), 0)
    top_core = bell_draw(key_list[5], (2, KMAX, BOXES * KQ), (2 * KMAX) ** -0.5, 0.25, ((2, 8),))
    return {"incident": incident, "leaf_inverse": leaf_inverse, "contrast": contrast, "skel_index": skel_index, "ranks": ranks, "top_core": top_core}


WAVENUM = 0.7
HIGH = lax.Precision.HIGHEST

def positions(box_at, index_list):
    px = (SIDE * box_at + index_list % SIDE).astype(jnp.float32)
    py = (index_list // SIDE % SIDE).astype(jnp.float32)
    pz = (index_list // (SIDE * SIDE)).astype(jnp.float32)
    return jnp.stack([px, py, pz])

def selector(index_list, rank_now):
    rows = jnp.arange(KMAX, dtype=jnp.int32)[:, None]
    cols = jnp.arange(LEAF, dtype=jnp.int32)[None, :]
    hit = (index_list[:, None] == cols) & (rows < rank_now)
    return hit.astype(jnp.float32)

def kernel_parts(own_pos, far_pos):
    diff = own_pos[:, :, None] - far_pos[:, None, :]
    dist = jnp.sqrt(lax.optimization_barrier(jnp.sum(diff * diff, axis=0)))
    return (jnp.cos(WAVENUM * dist) / dist, jnp.sin(WAVENUM * dist) / dist)

def complex_apply(mat_re, mat_im, vec):
    out_re = jnp.einsum('km,fm->fk', mat_re, vec[0], precision=HIGH) - jnp.einsum('km,fm->fk', mat_im, vec[1], precision=HIGH)
    out_im = jnp.einsum('km,fm->fk', mat_re, vec[1], precision=HIGH) + jnp.einsum('km,fm->fk', mat_im, vec[0], precision=HIGH)
    return jnp.stack([out_re, out_im])

def reference(incident, leaf_inverse, contrast, skel_index, ranks, top_core):
    fields_in = incident.astype(jnp.float32).reshape(2, NF, BOXES, LEAF).transpose(2, 0, 1, 3)

    def leaf_solve(pair):
        mat, vec = pair
        mat = mat.astype(jnp.float32)
        return complex_apply(mat[0], mat[1], vec)
    state = lax.map(leaf_solve, (leaf_inverse, fields_in))
    weights_c = contrast.reshape(BOXES, LEAF)
    box_ids = jnp.arange(BOXES, dtype=jnp.int32)
    for merge_level in range(2):

        def weighted(pair):
            field_b, idx_b, rank_b, cont_b = pair
            sel = selector(idx_b, rank_b)
            skel_vals = jnp.einsum('cfn,kn->cfk', field_b, sel, precision=HIGH)
            skel_q = jnp.dot(sel, cont_b, precision=HIGH)
            return skel_vals * skel_q
        sent = lax.map(weighted, (state, skel_index[:, merge_level], ranks[:, merge_level], weights_c))
        partners = jnp.bitwise_xor(box_ids, 1 << merge_level)
        received = sent[partners]

        def couple(pair):
            field_b, box_at, far_at, far_vals = pair
            idx_b = skel_index[box_at, merge_level]
            idx_p = skel_index[far_at, merge_level]
            sel = selector(idx_b, ranks[box_at, merge_level])
            green_re, green_im = kernel_parts(positions(box_at, idx_b), positions(far_at, idx_p))
            pushed = complex_apply(green_re, green_im, far_vals)
            return field_b - jnp.einsum('cfk,kn->cfn', pushed, sel, precision=HIGH)
        state = lax.map(couple, (state, box_ids, partners, received))
    cores = top_core.astype(jnp.float32).reshape(2, KMAX, BOXES // 4, KMAX)

    def apply_core(pair):
        field_b, box_at = pair
        sel = selector(skel_index[box_at, 1], ranks[box_at, 1])
        coarse = jnp.einsum('cfn,kn->cfk', field_b, sel, precision=HIGH)
        core_q = lax.dynamic_index_in_dim(cores, box_at // 4, 2, keepdims=False)
        pushed = complex_apply(core_q[0], core_q[1], coarse)
        return field_b - jnp.einsum('cfk,kn->cfn', pushed, sel, precision=HIGH)
    state = lax.map(apply_core, (state, box_ids))
    return state.transpose(1, 2, 0, 3).reshape(2, NF, POINTS)
```

```python
import jax
import jax.numpy as jnp
from jax import lax
from jax.experimental import pallas as pl
from jax.experimental.pallas import tpu as pltpu
from jax.sharding import PartitionSpec as P

SIDE = 8
WAVENUM = 0.7
BF = jnp.bfloat16
F32 = jnp.float32
CHUNKS = (128, 128, 128, 128)
TOP = 32766.0
STEPS = 128.0
VMEM = pl.BlockSpec(memory_space=pltpu.VMEM)
SMEM = pl.BlockSpec(memory_space=pltpu.SMEM)
ANY = pl.BlockSpec(memory_space=pl.ANY)
PARAMS = pltpu.CompilerParams(vmem_limit_bytes=40 * 1024 * 1024)


def swap(value, axis, mask):
    return lax.ppermute(value, axis, [(s, s ^ mask) for s in range(lax.axis_size(axis))])


def call(body, name, outs, ins, specs=None, scratch=(), **kw):
    return pl.pallas_call(
        body,
        name=name,
        out_shape=outs,
        in_specs=specs or [VMEM] * len(ins),
        out_specs=kw.pop("out_specs", [VMEM] * len(outs)),
        scratch_shapes=list(scratch),
        compiler_params=PARAMS,
        **kw,
    )(*ins)


def shape(*dims, dtype=F32):
    return jax.ShapeDtypeStruct(dims, dtype)


def nn(a, b):
    return lax.dot_general(a, b, (((1,), (0,)), ((), ())), preferred_element_type=F32)


def nt(a, b):
    return lax.dot_general(a, b, (((1,), (1,)), ((), ())), preferred_element_type=F32)


def halves(v):
    hi = v.astype(BF)
    return hi, (v - hi.astype(F32)).astype(BF)


def iota(dims, axis):
    return lax.broadcasted_iota(jnp.int32, dims, axis)


def to_column(row):
    n = row.shape[1]
    return jnp.sum(jnp.where(iota((n, n), 0) == iota((n, n), 1), row, 0.0), axis=1, keepdims=True)


def to_row(col, width):
    n = col.shape[0]
    return jnp.sum(jnp.where(iota((n, width), 0) == iota((n, width), 1), col, 0.0), axis=0, keepdims=True)


def cos_sin(angle):
    turns = jnp.floor(angle * 0.6366197723675814 + 0.5)
    t = angle - turns * 1.5707855224609375
    t = t - turns * 1.0804334124e-05
    t2 = t * t
    c = 1.0 + t2 * (-0.5 + t2 * (4.1666667e-2 + t2 * (-1.3888889e-3 + t2 * 2.4801587e-5)))
    s = t * (1.0 + t2 * (-1.6666667e-1 + t2 * (8.3333333e-3 + t2 * (-1.9841270e-4 + t2 * 2.7557319e-6))))
    quad = turns.astype(jnp.int32) & 3
    odd = (quad & 1) == 1
    cc = jnp.where(odd, s, c)
    ss = jnp.where(odd, c, s)
    cc = jnp.where((quad == 1) | (quad == 2), -cc, cc)
    ss = jnp.where(quad >= 2, -ss, ss)
    return cc, ss


def place(index, box):
    return (
        (index & (SIDE - 1)).astype(F32) + (box * SIDE).astype(F32),
        ((index >> 3) & (SIDE - 1)).astype(F32),
        (index >> 6).astype(F32),
    )


def plan_body(at_ref, ranks_ref, skel_ref, contrast_ref, e0_ref, e1_ref, q_ref, ghi_ref, glo_ref, g1_ref, j_ref, d_ref):
    box = at_ref[0]
    kmax = skel_ref.shape[1]
    width = contrast_ref.shape[1]
    contrast = contrast_ref[...]
    rows = []
    cols = []
    rank = []
    for level in range(2):
        far = box ^ (1 << level)
        own_row = skel_ref[pl.ds(box * 2 + level, 1), :]
        far_row = skel_ref[pl.ds(far * 2 + level, 1), :]
        own_col = to_column(own_row.astype(F32)).astype(jnp.int32)
        far_col = to_column(far_row.astype(F32)).astype(jnp.int32)
        r = ranks_ref[box * 2 + level]
        rows.append(own_row)
        cols.append(own_col)
        rank.append(r)
        hit = (own_col == iota((kmax, width), 1)) & (iota((kmax, width), 0) < r)
        (e0_ref, e1_ref)[level][...] = hit.astype(F32).astype(BF)
        q_col = jnp.sum(jnp.where(hit, contrast, 0.0), axis=1, keepdims=True)
        q_ref[pl.ds(level, 1), :] = to_row(q_col, kmax)
        ox, oy, oz = place(own_row, box)
        fx, fy, fz = place(far_col, far)
        d2 = (fx - ox) * (fx - ox) + (fy - oy) * (fy - oy) + (fz - oz) * (fz - oz)
        dist = jnp.sqrt(d2)
        inv = 1.0 / dist
        c, s = cos_sin(WAVENUM * dist)
        c = c * inv
        s = s * inv
        if level == 0:
            chi, clo = halves(c)
            shi, slo = halves(s)
            ghi_ref[0:kmax, 0:kmax] = chi
            ghi_ref[0:kmax, kmax:] = shi
            ghi_ref[kmax:, 0:kmax] = -shi
            ghi_ref[kmax:, kmax:] = chi
            glo_ref[0:kmax, 0:kmax] = clo
            glo_ref[0:kmax, kmax:] = slo
            glo_ref[kmax:, 0:kmax] = -slo
            glo_ref[kmax:, kmax:] = clo
        else:
            g1_ref[:, 0:kmax] = c
            g1_ref[:, kmax:] = s
    mine = iota((kmax, kmax), 0)
    other = iota((kmax, kmax), 1)
    j_ref[...] = ((cols[0] == rows[1]) & (mine < rank[0]) & (other < rank[1])).astype(F32).astype(BF)
    d_ref[...] = ((cols[1] == rows[1]) & (mine < rank[1]) & (other < rank[1])).astype(F32).astype(BF)


def core_body(at_ref, own_ref, near_ref, far_ref, g1_ref, d_ref, mc_ref, khi_ref, klo_ref, ct_ref):
    slot = at_ref[0] & 3
    quarter = own_ref.shape[0] // 2
    kmax = own_ref.shape[1]
    pieces = (own_ref[...], near_ref[...], far_ref[0], far_ref[1])
    for mask, piece in enumerate(pieces):
        start = pl.multiple_of((slot ^ mask) * quarter, quarter)
        ct_ref[pl.ds(start, quarter), 0:kmax] = piece[:quarter]
        ct_ref[pl.ds(start, quarter), kmax:] = piece[quarter:]
    cr = ct_ref[:, 0:kmax]
    ci = ct_ref[:, kmax:]
    mc_ref[0:kmax, 0:kmax] = cr
    mc_ref[0:kmax, kmax:] = ci
    mc_ref[kmax:, 0:kmax] = -ci
    mc_ref[kmax:, kmax:] = cr
    dup = d_ref[...]
    gr = g1_ref[:, 0:kmax]
    gi = g1_ref[:, kmax:]
    grh, grl = halves(gr)
    gih, gil = halves(gi)
    dr = nn(grh, dup) + nn(grl, dup)
    di = nn(gih, dup) + nn(gil, dup)
    drh, drl = halves(dr)
    dih, dil = halves(di)
    kr = gr - ((nn(drh, cr) + nn(drl, cr)) - (nn(dih, ci) + nn(dil, ci)))
    ki = gi - ((nn(drh, ci) + nn(drl, ci)) + (nn(dih, cr) + nn(dil, cr)))
    krh, krl = halves(kr)
    kih, kil = halves(ki)
    for ref, a, b in ((khi_ref, krh, kih), (klo_ref, krl, kil)):
        ref[0:kmax, 0:kmax] = a
        ref[0:kmax, kmax:] = b
        ref[kmax:, 0:kmax] = -b
        ref[kmax:, kmax:] = a


def rows_body(at_ref, p0_ref, p1_ref, p2_ref, p3_ref, e_ref, a_ref, b_ref):
    me = at_ref[1]
    n = p0_ref.shape[1]
    width = p0_ref.shape[2]
    kmax = e_ref.shape[0]
    for mask, ref in enumerate((p0_ref, p1_ref, p2_ref, p3_ref)):
        start = pl.multiple_of((me ^ mask) * n, n)
        a_ref[pl.ds(start, n), 0:width] = ref[0]
        a_ref[pl.ds(start, n), width:] = ref[1]
    picked = nn(e_ref[...], a_ref[...]).astype(BF)
    re = picked[:, :width]
    im = picked[:, width:]
    b_ref[0:kmax, 0:width] = re
    b_ref[0:kmax, width:] = -im
    b_ref[kmax:, 0:width] = im
    b_ref[kmax:, width:] = re


def leaf_body(x_ref, a_ref, e_ref, y_ref, v_ref):
    width = x_ref.shape[2]
    kmax = e_ref.shape[0]
    x = jnp.concatenate([x_ref[0], x_ref[1]], axis=1)
    xs = jnp.concatenate([-x_ref[1], x_ref[0]], axis=1)
    a = a_ref[...]
    y_ref[:, 0:width] = nt(jnp.concatenate([x_ref[0], -x_ref[1]], axis=1), a)
    y_ref[:, width:] = nt(jnp.concatenate([x_ref[1], x_ref[0]], axis=1), a)
    picked = nn(e_ref[...], a).astype(BF)
    v_ref[:, 0:kmax] = nt(jnp.concatenate([x_ref[0], -x_ref[1]], axis=1), picked)
    v_ref[:, kmax:] = nt(jnp.concatenate([x_ref[1], x_ref[0]], axis=1), picked)


def pack(w, out_ref):
    n, both = w.shape
    k = both // 2
    most = jnp.max(jnp.abs(w), axis=1, keepdims=True)
    step = jnp.ceil(jnp.log2(jnp.maximum(most, 1e-30)) * STEPS)
    inv = TOP / jnp.exp2(step / STEPS)
    v = jnp.floor(w * inv + 0.5).astype(jnp.int32).astype(jnp.int16)
    out_ref[0:n, :] = v[:, :k]
    out_ref[n : 2 * n, :] = v[:, k:]
    out_ref[2 * n :, :] = jnp.broadcast_to(to_row(step, k), (16, k)).astype(jnp.int32).astype(jnp.int16)


def apply_packed(in_ref, mhi, mlo):
    n = (in_ref.shape[0] - 16) // 2
    k = in_ref.shape[1]
    steps = in_ref[2 * n :, :].astype(jnp.int32).astype(F32)[0:1, :]
    step = jnp.sum(jnp.where(iota((n, k), 0) == iota((n, k), 1), steps, 0.0), axis=1, keepdims=True)
    scale = jnp.exp2(step / STEPS) * (1.0 / TOP)
    v = jnp.concatenate([in_ref[0:n, :], in_ref[n : 2 * n, :]], axis=1).astype(jnp.int32)
    upper = (v + 128) & -256
    lower = (v - upper).astype(F32).astype(BF)
    upper = upper.astype(F32).astype(BF)
    return (nn(upper, mhi) + (nn(lower, mhi) + nn(upper, mlo))) * scale


def first_body(x_ref, b_ref, q_ref, *outs, parts):
    q = q_ref[0:1, :]
    q = jnp.concatenate([q, q], axis=1)
    for ref, (start, n) in zip(outs, parts):
        x = jnp.concatenate([x_ref[0, start : start + n], x_ref[1, start : start + n]], axis=1)
        pack(nt(x, b_ref[...]) * q, ref)


def second_body(in_ref, ghi_ref, glo_ref, v_ref, j_ref, q_ref, out_ref, gs_ref, us_ref, *, start):
    n = (in_ref.shape[0] - 16) // 2
    k = in_ref.shape[1]
    g = apply_packed(in_ref, ghi_ref[...], glo_ref[...])
    hi, lo = halves(g)
    gs_ref[0] = hi
    gs_ref[1] = lo
    j = j_ref[...]
    q = q_ref[1:2, :]
    re = v_ref[start : start + n, :k] - (nn(hi[:, :k], j) + nn(lo[:, :k], j))
    im = v_ref[start : start + n, k:] - (nn(hi[:, k:], j) + nn(lo[:, k:], j))
    u = jnp.concatenate([re, im], axis=1)
    pack(u * jnp.concatenate([q, q], axis=1), out_ref)
    hi, lo = halves(u)
    us_ref[0] = hi
    us_ref[1] = lo


def third_body(gs_ref, us_ref, y_ref, e0_ref, mc_ref, part_ref, p_ref, *, start):
    n = gs_ref.shape[1]
    k = e0_ref.shape[0]
    width = e0_ref.shape[1]
    e = e0_ref[...]
    for i in range(2):
        cols = slice(i * k, i * k + k)
        part_ref[i] = y_ref[start : start + n, i * width : (i + 1) * width] - (
            nn(gs_ref[0, :, cols], e) + nn(gs_ref[1, :, cols], e)
        )
    mc = mc_ref[...]
    p_ref[...] = nn(us_ref[0], mc) + nn(us_ref[1], mc)


def fourth_body(in_ref, khi_ref, klo_ref, part_ref, p_ref, e1_ref, *rest, start):
    out_ref, hold_ref, sem = rest[-3:]
    n = part_ref.shape[1]
    k = e1_ref.shape[0]
    p = p_ref[...] + apply_packed(in_ref, khi_ref[...], klo_ref[...])
    hi, lo = halves(p)
    e = e1_ref[...]
    copies = []
    for i in range(2):
        cols = slice(i * k, i * k + k)
        hold_ref[i] = part_ref[i] - (nn(hi[:, cols], e) + nn(lo[:, cols], e))
        copy = pltpu.make_async_copy(hold_ref.at[i], out_ref.at[i, pl.ds(start, n), :], sem.at[i])
        copy.start()
        copies.append(copy)
    for copy in copies:
        copy.wait()


def body(incident, leaf_inverse, contrast, skel_index, ranks, top_core):
    nf, width = incident.shape[1:]
    boxes, _, kmax = skel_index.shape
    quarter = top_core.shape[2]
    at = jnp.stack([lax.axis_index("box"), lax.axis_index("field")]).astype(jnp.int32)
    own = leaf_inverse[0]
    across = swap(own, "field", 2)
    beside = swap(own, "field", 1)
    core_own = jnp.swapaxes(top_core, 1, 2).reshape(2 * quarter, kmax)
    core_near = swap(core_own, "box", 1)
    core_far = swap(jnp.stack([core_own, core_near]), "box", 2)
    e0, e1, q, ghi, glo, g1, dup01, dup11 = call(
        plan_body,
        "plan",
        [
            shape(kmax, width, dtype=BF),
            shape(kmax, width, dtype=BF),
            shape(8, kmax),
            shape(2 * kmax, 2 * kmax, dtype=BF),
            shape(2 * kmax, 2 * kmax, dtype=BF),
            shape(kmax, 2 * kmax),
            shape(kmax, kmax, dtype=BF),
            shape(kmax, kmax, dtype=BF),
        ],
        [at, ranks.reshape(-1), skel_index.reshape(boxes * 2, kmax), contrast.reshape(1, width)],
        [SMEM, SMEM, VMEM, VMEM],
    )
    beyond = swap(across, "field", 1)
    a_all, b0 = call(
        rows_body,
        "rows",
        [shape(width, 2 * width, dtype=BF), shape(2 * kmax, 2 * width, dtype=BF)],
        [at, own, beside, across, beyond, e0],
        [SMEM] + [VMEM] * 5,
    )
    starts = [sum(CHUNKS[:i]) for i in range(len(CHUNKS))]
    sizes = list(zip(starts, CHUNKS))
    packed = []
    for name, parts in (("send_first", sizes[:1]), ("send_rest", sizes[1:])):
        packed += call(
            lambda *refs, parts=parts: first_body(*refs, parts=parts),
            name,
            [shape(2 * n + 16, kmax, dtype=jnp.int16) for _, n in parts],
            [incident, b0, q],
        )
    got = [swap(v, "box", 1) for v in packed]
    y, v1 = call(leaf_body, "leaf", [shape(nf, 2 * width), shape(nf, 2 * kmax)], [incident, a_all, e1])
    mc, khi, klo = call(
        core_body,
        "core",
        [shape(2 * kmax, 2 * kmax, dtype=BF)] * 3,
        [at, core_own, core_near, core_far, g1, dup11],
        [SMEM] + [VMEM] * 5,
        [pltpu.VMEM((kmax, 2 * kmax), BF)],
    )
    out = None
    late = []
    for i, (start, n) in enumerate(sizes):
        send, gs, us = call(
            lambda *refs, start=start: second_body(*refs, start=start),
            f"second{i}",
            [shape(2 * n + 16, kmax, dtype=jnp.int16), shape(2, n, 2 * kmax, dtype=BF), shape(2, n, 2 * kmax, dtype=BF)],
            [got[i], ghi, glo, v1, dup01, q],
        )
        back = swap(send, "box", 2)
        part, p = call(
            lambda *refs, start=start: third_body(*refs, start=start),
            f"third{i}",
            [shape(2, n, width), shape(n, 2 * kmax)],
            [gs, us, y, e0, mc],
        )
        late.append((back, part, p))
    for i, (start, n) in enumerate(sizes):
        back, part, p = late[i]
        ins = [back, khi, klo, part, p, e1] + ([] if out is None else [out])
        specs = [VMEM] * 6 + ([] if out is None else [ANY])
        (out,) = call(
            lambda *refs, start=start: fourth_body(*refs, start=start),
            f"fourth{i}",
            [shape(2, nf, width)],
            ins,
            specs,
            [pltpu.VMEM((2, n, width), F32), pltpu.SemaphoreType.DMA((2,))],
            out_specs=[ANY],
            input_output_aliases={} if out is None else {6: 0},
        )
    return out


def solution(mesh):
    return jax.shard_map(
        body,
        mesh=mesh,
        in_specs=(P(None, "field", "box"), P("box", None, "field", None), P("box"), P(), P(), P(None, None, "box")),
        out_specs=P(None, "field", "box"),
        check_vma=False,
    )
```

```python
import jax
import jax.numpy as jnp
from jax import lax
from jax.experimental import pallas as pl
from jax.experimental.pallas import tpu as pltpu
from jax.sharding import PartitionSpec as P

SIDE = 8
WAVENUM = 0.7
BF = jnp.bfloat16
F32 = jnp.float32
SHARES = (10, 12, 10)
TOP = 32766.0
STEPS = 128.0
VMEM = pl.BlockSpec(memory_space=pltpu.VMEM)
SMEM = pl.BlockSpec(memory_space=pltpu.SMEM)
ANY = pl.BlockSpec(memory_space=pl.ANY)
PARAMS = pltpu.CompilerParams(vmem_limit_bytes=40 * 1024 * 1024)


def swap(value, axis, mask):
    return lax.ppermute(value, axis, [(s, s ^ mask) for s in range(lax.axis_size(axis))])


def call(body, name, outs, ins, specs=None, scratch=(), cost=1.0, **kw):
    return pl.pallas_call(
        body,
        name=name,
        out_shape=outs,
        in_specs=specs or [VMEM] * len(ins),
        out_specs=kw.pop("out_specs", [VMEM] * len(outs)),
        scratch_shapes=list(scratch),
        compiler_params=PARAMS,
        cost_estimate=pl.CostEstimate(flops=int(cost * 1e9), bytes_accessed=int(cost * 3e6), transcendentals=0),
        **kw,
    )(*ins)


def shape(*dims, dtype=F32):
    return jax.ShapeDtypeStruct(dims, dtype)


def nn(a, b):
    return lax.dot_general(a, b, (((1,), (0,)), ((), ())), preferred_element_type=F32)


def nt(a, b):
    return lax.dot_general(a, b, (((1,), (1,)), ((), ())), preferred_element_type=F32)


def halves(v):
    hi = v.astype(BF)
    return hi, (v - hi.astype(F32)).astype(BF)


def iota(dims, axis):
    return lax.broadcasted_iota(jnp.int32, dims, axis)


def to_column(row):
    n = row.shape[1]
    return jnp.sum(jnp.where(iota((n, n), 0) == iota((n, n), 1), row, 0.0), axis=1, keepdims=True)


def to_row(col, width):
    n = col.shape[0]
    return jnp.sum(jnp.where(iota((n, width), 0) == iota((n, width), 1), col, 0.0), axis=0, keepdims=True)


def cos_sin(angle):
    turns = jnp.floor(angle * 0.6366197723675814 + 0.5)
    t = angle - turns * 1.5707855224609375
    t = t - turns * 1.0804334124e-05
    t2 = t * t
    c = 1.0 + t2 * (-0.5 + t2 * (4.1666667e-2 + t2 * (-1.3888889e-3 + t2 * 2.4801587e-5)))
    s = t * (1.0 + t2 * (-1.6666667e-1 + t2 * (8.3333333e-3 + t2 * (-1.9841270e-4 + t2 * 2.7557319e-6))))
    quad = turns.astype(jnp.int32) & 3
    odd = (quad & 1) == 1
    cc = jnp.where(odd, s, c)
    ss = jnp.where(odd, c, s)
    cc = jnp.where((quad == 1) | (quad == 2), -cc, cc)
    ss = jnp.where(quad >= 2, -ss, ss)
    return cc, ss


def place(index, box):
    return (
        (index & (SIDE - 1)).astype(F32) + (box * SIDE).astype(F32),
        ((index >> 3) & (SIDE - 1)).astype(F32),
        (index >> 6).astype(F32),
    )


def open_body(out_ref):
    out_ref[...] = jnp.zeros(out_ref.shape, out_ref.dtype)


def plan_body(ranks_ref, skel_ref, contrast_ref, own_ref, beside_ref, dep_ref, *refs, parts):
    e0_ref, er_ref, e1_ref, q_ref, ghi_ref, glo_ref, g1_ref, j_ref, d_ref, part_ref = refs
    box = lax.axis_index("box")
    me = lax.axis_index("field")
    kmax = skel_ref.shape[2]
    width = contrast_ref.shape[1]
    contrast = contrast_ref[...]
    ranks = ranks_ref[...].astype(F32)
    ranks = jnp.sum(jnp.where(iota(ranks.shape, 1) == box, ranks, 0.0), axis=1, keepdims=True).astype(jnp.int32)
    rows = []
    cols = []
    rank = []
    for level in range(2):
        far = box ^ (1 << level)
        own_row = skel_ref[box][level : level + 1, :]
        far_row = skel_ref[far][level : level + 1, :]
        own_col = to_column(own_row.astype(F32)).astype(jnp.int32)
        far_col = to_column(far_row.astype(F32)).astype(jnp.int32)
        r = ranks[level : level + 1, :]
        rows.append(own_row)
        cols.append(own_col)
        rank.append(r)
        hit = (own_col == iota((kmax, width), 1)) & (iota((kmax, width), 0) < r)
        (e0_ref, e1_ref)[level][...] = hit.astype(F32).astype(BF)
        if level == 0:
            n = width // parts
            lane = iota((kmax, width), 1)
            turned = (((lane // n) ^ me) * n) + lane % n
            er_ref[...] = ((own_col == turned) & (iota((kmax, width), 0) < r)).astype(F32).astype(BF)
        q_col = jnp.sum(jnp.where(hit, contrast, 0.0), axis=1, keepdims=True)
        q_ref[pl.ds(level, 1), :] = to_row(q_col, kmax)
        ox, oy, oz = place(own_row, box)
        fx, fy, fz = place(far_col, far)
        d2 = (fx - ox) * (fx - ox) + (fy - oy) * (fy - oy) + (fz - oz) * (fz - oz)
        dist = jnp.sqrt(d2)
        inv = 1.0 / dist
        c, s = cos_sin(WAVENUM * dist)
        c = c * inv
        s = s * inv
        if level == 0:
            chi, clo = halves(c)
            shi, slo = halves(s)
            ghi_ref[0:kmax, 0:kmax] = chi
            ghi_ref[0:kmax, kmax:] = shi
            ghi_ref[kmax:, 0:kmax] = -shi
            ghi_ref[kmax:, kmax:] = chi
            glo_ref[0:kmax, 0:kmax] = clo
            glo_ref[0:kmax, kmax:] = slo
            glo_ref[kmax:, 0:kmax] = -slo
            glo_ref[kmax:, kmax:] = clo
        else:
            g1_ref[:, 0:kmax] = c
            g1_ref[:, kmax:] = s
    mine = iota((kmax, kmax), 0)
    other = iota((kmax, kmax), 1)
    j_ref[...] = ((cols[0] == rows[1]) & (mine < rank[0]) & (other < rank[1])).astype(F32).astype(BF)
    d_ref[...] = ((cols[1] == rows[1]) & (mine < rank[1]) & (other < rank[1])).astype(F32).astype(BF)
    n = own_ref.shape[1]
    both = jnp.concatenate(
        [
            jnp.concatenate([own_ref[0], own_ref[1]], axis=1),
            jnp.concatenate([beside_ref[0], beside_ref[1]], axis=1),
        ],
        axis=0,
    )
    part_ref[...] = nn(er_ref[:, : 2 * n], both).astype(BF)


def core_body(own_ref, near_ref, far_ref, g1_ref, d_ref, dep_ref, mc_ref, khi_ref, klo_ref, ct_ref):
    slot = lax.axis_index("box") & 3
    quarter = own_ref.shape[0] // 2
    kmax = own_ref.shape[1]
    pieces = (own_ref[...], near_ref[...], far_ref[0], far_ref[1])
    for mask, piece in enumerate(pieces):
        start = pl.multiple_of((slot ^ mask) * quarter, quarter)
        ct_ref[pl.ds(start, quarter), 0:kmax] = piece[:quarter]
        ct_ref[pl.ds(start, quarter), kmax:] = piece[quarter:]
    cr = ct_ref[:, 0:kmax]
    ci = ct_ref[:, kmax:]
    mc_ref[0:kmax, 0:kmax] = cr
    mc_ref[0:kmax, kmax:] = ci
    mc_ref[kmax:, 0:kmax] = -ci
    mc_ref[kmax:, kmax:] = cr
    dup = d_ref[...]
    gr = g1_ref[:, 0:kmax]
    gi = g1_ref[:, kmax:]
    grh, grl = halves(gr)
    gih, gil = halves(gi)
    dr = nn(grh, dup) + nn(grl, dup)
    di = nn(gih, dup) + nn(gil, dup)
    drh, drl = halves(dr)
    dih, dil = halves(di)
    kr = gr - ((nn(drh, cr) + nn(drl, cr)) - (nn(dih, ci) + nn(dil, ci)))
    ki = gi - ((nn(drh, ci) + nn(drl, ci)) + (nn(dih, cr) + nn(dil, cr)))
    krh, krl = halves(kr)
    kih, kil = halves(ki)
    for ref, a, b in ((khi_ref, krh, kih), (klo_ref, krl, kil)):
        ref[0:kmax, 0:kmax] = a
        ref[0:kmax, kmax:] = b
        ref[kmax:, 0:kmax] = -b
        ref[kmax:, kmax:] = a


def relay_body(in_ref, *rest):
    rest[-1][...] = in_ref[...]


def pair_body(a_ref, b_ref, dep_ref, out_ref):
    out_ref[0] = a_ref[...]
    out_ref[1] = b_ref[...]


def turned_fields(x_ref, start, n):
    re = x_ref[0, start : start + n]
    im = x_ref[1, start : start + n]
    return jnp.concatenate([re, -im], axis=1), jnp.concatenate([im, re], axis=1)


def send(x_ref, picked, q_ref, out_ref, start, n):
    q = q_ref[0:1, :]
    left, right = turned_fields(x_ref, start, n)
    w = jnp.concatenate([nt(left, picked) * q, nt(right, picked) * q], axis=1)
    pack(w, out_ref)


def first_body(part_ref, across_ref, beyond_ref, er_ref, x_ref, q_ref, *outs, start, n):
    picked_ref, out_ref = outs
    rows = across_ref.shape[1]
    both = jnp.concatenate(
        [
            jnp.concatenate([across_ref[0], across_ref[1]], axis=1),
            jnp.concatenate([beyond_ref[0], beyond_ref[1]], axis=1),
        ],
        axis=0,
    )
    picked = (nn(er_ref[:, 2 * rows :], both) + part_ref[...].astype(F32)).astype(BF)
    picked_ref[...] = picked
    send(x_ref, picked, q_ref, out_ref, start, n)


def rest_body(x_ref, picked_ref, q_ref, dep_ref, out_ref, *, start, n):
    send(x_ref, picked_ref[...], q_ref, out_ref, start, n)


def rows_body(x_ref, p0_ref, p1_ref, p2_ref, p3_ref, e_ref, v_ref, a_ref):
    width = x_ref.shape[2]
    kmax = e_ref.shape[0]
    me = lax.axis_index("field")
    n = p0_ref.shape[1]
    for mask, ref in enumerate((p0_ref, p1_ref, p2_ref, p3_ref)):
        start = pl.multiple_of((me ^ mask) * n, n)
        a_ref[pl.ds(start, n), 0:width] = ref[0]
        a_ref[pl.ds(start, n), width:] = ref[1]
    left, right = turned_fields(x_ref, 0, x_ref.shape[1])
    picked = nn(e_ref[...], a_ref[...]).astype(BF)
    v_ref[:, 0:kmax] = nt(left, picked)
    v_ref[:, kmax:] = nt(right, picked)


def leaf_body(x_ref, a_ref, dep_ref, y_ref):
    width = x_ref.shape[2]
    left, right = turned_fields(x_ref, 0, x_ref.shape[1])
    a = a_ref[...]
    y_ref[:, 0:width] = nt(left, a)
    y_ref[:, width:] = nt(right, a)


def pack(w, out_ref):
    n, both = w.shape
    k = both // 2
    most = jnp.max(jnp.abs(w), axis=1, keepdims=True)
    step = jnp.ceil(jnp.log2(jnp.maximum(most, 1e-30)) * STEPS)
    inv = TOP / jnp.exp2(step / STEPS)
    v = jnp.floor(w * inv + 0.5).astype(jnp.int32).astype(jnp.int16)
    out_ref[0:n, :] = v[:, :k]
    out_ref[n : 2 * n, :] = v[:, k:]
    out_ref[2 * n :, :] = jnp.broadcast_to(to_row(step, k), (16, k)).astype(jnp.int32).astype(jnp.int16)


def apply_packed(in_ref, mhi, mlo):
    n = (in_ref.shape[0] - 16) // 2
    k = in_ref.shape[1]
    steps = in_ref[2 * n :, :].astype(jnp.int32).astype(F32)[0:1, :]
    step = jnp.sum(jnp.where(iota((n, k), 0) == iota((n, k), 1), steps, 0.0), axis=1, keepdims=True)
    scale = jnp.exp2(step / STEPS) * (1.0 / TOP)
    v = jnp.concatenate([in_ref[0:n, :], in_ref[n : 2 * n, :]], axis=1).astype(jnp.int32)
    upper = (v + 128) & -256
    lower = (v - upper).astype(F32).astype(BF)
    upper = upper.astype(F32).astype(BF)
    return (nn(upper, mhi) + (nn(lower, mhi) + nn(upper, mlo))) * scale


def second_body(in_ref, ghi_ref, glo_ref, v_ref, j_ref, q_ref, *rest, start):
    out_ref, gs_ref, us_ref = rest[-3:]
    n = (in_ref.shape[0] - 16) // 2
    k = in_ref.shape[1]
    g = apply_packed(in_ref, ghi_ref[...], glo_ref[...])
    hi, lo = halves(g)
    gs_ref[0] = hi
    gs_ref[1] = lo
    j = j_ref[...]
    q = q_ref[1:2, :]
    re = v_ref[start : start + n, :k] - (nn(hi[:, :k], j) + nn(lo[:, :k], j))
    im = v_ref[start : start + n, k:] - (nn(hi[:, k:], j) + nn(lo[:, k:], j))
    u = jnp.concatenate([re, im], axis=1)
    pack(u * jnp.concatenate([q, q], axis=1), out_ref)
    hi, lo = halves(u)
    us_ref[0] = hi
    us_ref[1] = lo


def third_body(gs_ref, us_ref, y_ref, e0_ref, mc_ref, part_ref, p_ref, *, start):
    n = gs_ref.shape[1]
    k = e0_ref.shape[0]
    width = e0_ref.shape[1]
    e = e0_ref[...]
    for i in range(2):
        cols = slice(i * k, i * k + k)
        part_ref[i] = y_ref[start : start + n, i * width : (i + 1) * width] - (
            nn(gs_ref[0, :, cols], e) + nn(gs_ref[1, :, cols], e)
        )
    mc = mc_ref[...]
    p_ref[...] = nn(us_ref[0], mc) + nn(us_ref[1], mc)


def fourth_body(*refs, parts):
    khi_ref, klo_ref, e1_ref = refs[:3]
    chunks = refs[3 : 3 + 3 * len(parts)]
    out_ref, hold_ref, sem = refs[-3:]
    base = parts[0][0]
    e = e1_ref[...]
    khi = khi_ref[...]
    klo = klo_ref[...]
    k = e1_ref.shape[0]
    copies = []
    for c, (start, n) in enumerate(parts):
        in_ref, part_ref, p_ref = chunks[3 * c : 3 * c + 3]
        p = p_ref[...] + apply_packed(in_ref, khi, klo)
        hi, lo = halves(p)
        for i in range(2):
            cols = slice(i * k, i * k + k)
            spot = pl.ds(start - base, n)
            hold_ref[i, spot] = part_ref[i] - (nn(hi[:, cols], e) + nn(lo[:, cols], e))
            copy = pltpu.make_async_copy(hold_ref.at[i, spot], out_ref.at[i, pl.ds(start, n), :], sem.at[2 * c + i])
            copy.start()
            copies.append(copy)
    for copy in copies:
        copy.wait()


def body(incident, leaf_inverse, contrast, skel_index, ranks, top_core):
    nf, width = incident.shape[1:]
    boxes, _, kmax = skel_index.shape
    quarter = top_core.shape[2]
    own = leaf_inverse[0]
    across = swap(own, "field", 2)
    beside = swap(own, "field", 1)
    core_own = jnp.swapaxes(top_core, 1, 2).reshape(2 * quarter, kmax)
    core_near = swap(core_own, "box", 1)
    n = own.shape[1]
    (opened,) = call(open_body, "open", [shape(8, 128)], [], cost=4.0)
    e0, er, e1, q, ghi, glo, g1, dup01, dup11, part = call(
        lambda *refs: plan_body(*refs, parts=lax.axis_size("field")),
        "plan",
        [
            shape(kmax, width, dtype=BF),
            shape(kmax, width, dtype=BF),
            shape(kmax, width, dtype=BF),
            shape(8, kmax),
            shape(2 * kmax, 2 * kmax, dtype=BF),
            shape(2 * kmax, 2 * kmax, dtype=BF),
            shape(kmax, 2 * kmax),
            shape(kmax, kmax, dtype=BF),
            shape(kmax, kmax, dtype=BF),
            shape(kmax, 2 * width, dtype=BF),
        ],
        [ranks.T, skel_index, contrast.reshape(1, width), own, beside, opened],
        [VMEM] * 5 + [ANY],
    )
    x = incident
    (pair,) = call(
        pair_body, "pair", [shape(2, 2 * quarter, kmax, dtype=BF)], [core_own, core_near, part], [VMEM, VMEM, ANY], cost=0.05
    )
    core_far = swap(pair, "box", 2)
    (across,) = call(
        relay_body, "relay", [shape(*across.shape, dtype=BF)], [across, pair], [VMEM, ANY], cost=0.05
    )
    beyond = swap(across, "field", 1)
    chunks = [nf // sum(SHARES) * share for share in SHARES]
    sizes = [(sum(chunks[:i]), n) for i, n in enumerate(chunks)]
    start, n = sizes[0]
    picked, head = call(
        lambda *refs, start=start, n=n: first_body(*refs, start=start, n=n),
        "first",
        [
            shape(kmax, 2 * width, dtype=BF),
            shape(2 * n + 16, kmax, dtype=jnp.int16),
        ],
        [part, across, beyond, er, x, q],
        cost=0.8,
    )

    def ready(i, dep):
        start, n = sizes[i]
        (packed,) = call(
            lambda *refs: rest_body(*refs, start=start, n=n),
            f"ready{i}",
            [shape(2 * n + 16, kmax, dtype=jnp.int16)],
            [x, picked, q, dep],
            [VMEM] * 3 + [ANY],
            cost=0.6,
        )
        return swap(packed, "box", 1)

    got = swap(head, "box", 1)
    v1, a_all = call(
        rows_body,
        "rows",
        [shape(nf, 2 * kmax), shape(width, 2 * width, dtype=BF)],
        [x, own, beside, across, beyond, e1],
    )
    late = []
    coming = ready(1, q)

    def core(dep):
        return call(
            core_body,
            "core",
            [shape(2 * kmax, 2 * kmax, dtype=BF)] * 3,
            [core_own, core_near, core_far, g1, dup11, dep],
            [VMEM] * 5 + [ANY],
            [pltpu.VMEM((kmax, 2 * kmax), BF)],
        )

    def third(i):
        start, n = sizes[i]
        late[i][1:] = call(
            lambda *refs, start=start: third_body(*refs, start=start),
            f"third{i}",
            [shape(2, n, width), shape(n, 2 * kmax)],
            [late[i][1], late[i][2], y, e0, mc],
            cost=0.5,
        )

    for i, (start, n) in enumerate(sizes):
        dep = e1
        if i == 1 and 1:
            dep = mc
        if i == 2 and 2:
            dep = mc if 2 == 1 else late[2 - 2][2]
        back, gs, us = call(
            lambda *refs, start=start: second_body(*refs, start=start),
            f"second{i}",
            [shape(2 * n + 16, kmax, dtype=jnp.int16), shape(2, n, 2 * kmax, dtype=BF), shape(2, n, 2 * kmax, dtype=BF)],
            [got, ghi, glo, v1, dup01, q, dep],
            [VMEM] * 6 + [ANY],
            cost=0.8,
        )
        got = coming
        if 0:
            late.append([swap(back, "box", 2), gs, us])
        if i + 2 < len(sizes):
            coming = ready(i + 2, gs)
        if not 0:
            late.append([swap(back, "box", 2), gs, us])
        if i == 0:
            mc, khi, klo = core(gs)
        if i == 1:
            (y,) = call(leaf_body, "leaf", [shape(nf, 2 * width)], [x, a_all, late[0][0]], [VMEM, VMEM, ANY], cost=1.3)
            for j in range(i + 1):
                third(j)
        if i > 1:
            third(i)
    out = None
    for name, at in (("most", slice(0, -1)), ("last", slice(-1, None))):
        parts = sizes[at]
        ins = [khi, klo, e1] + [a for group in late[at] for a in group]
        specs = [VMEM] * len(ins)
        if out is not None:
            ins.append(out)
            specs.append(ANY)
        (out,) = call(
            lambda *refs, parts=parts: fourth_body(*refs, parts=parts),
            name,
            [shape(2, nf, width)],
            ins,
            specs,
            [pltpu.VMEM((2, sum(n for _, n in parts), width), F32), pltpu.SemaphoreType.DMA((2 * len(parts),))],
            out_specs=[ANY],
            input_output_aliases={} if len(specs) == len(ins) and specs[-1] is VMEM else {len(ins) - 1: 0},
        )
    return out


def solution(mesh):
    return jax.shard_map(
        body,
        mesh=mesh,
        in_specs=(P(None, "field", "box"), P("box", None, "field", None), P("box"), P(), P(), P(None, None, "box")),
        out_specs=P(None, "field", "box"),
        check_vma=False,
    )
```

```python
import jax
import jax.numpy as jnp
from jax import lax
from jax.experimental import pallas as pl
from jax.experimental.pallas import tpu as pltpu
from jax.sharding import PartitionSpec as P

SIDE = 8
WAVENUM = 0.7
BF = jnp.bfloat16
F32 = jnp.float32
SHARES = (10, 11, 11)
TOP = 32766.0
STEPS = 128.0
LANES = 128
VMEM = pl.BlockSpec(memory_space=pltpu.VMEM)
SMEM = pl.BlockSpec(memory_space=pltpu.SMEM)
ANY = pl.BlockSpec(memory_space=pl.ANY)
PARAMS = pltpu.CompilerParams(vmem_limit_bytes=40 * 1024 * 1024)


def swap(value, axis, mask):
    return lax.ppermute(value, axis, [(s, s ^ mask) for s in range(lax.axis_size(axis))])


def call(body, name, outs, ins, specs=None, scratch=(), cost=1.0, **kw):
    return list(
        pl.pallas_call(
        body,
        name=name,
        out_shape=outs,
        in_specs=specs or [VMEM] * len(ins),
        out_specs=kw.pop("out_specs", [VMEM] * len(outs)),
        scratch_shapes=list(scratch),
        compiler_params=PARAMS,
        cost_estimate=pl.CostEstimate(flops=int(cost * 1e9), bytes_accessed=int(cost * 3e6), transcendentals=0),
        **kw,
    )(*ins)
    )


def shape(*dims, dtype=F32):
    return jax.ShapeDtypeStruct(dims, dtype)


def packed_shape(n, kmax):
    return shape(2 * n * kmax // LANES + 16, LANES, dtype=jnp.int16)


def nn(a, b):
    return lax.dot_general(a, b, (((1,), (0,)), ((), ())), preferred_element_type=F32)


def nt(a, b):
    return lax.dot_general(a, b, (((1,), (1,)), ((), ())), preferred_element_type=F32)


def halves(v):
    hi = v.astype(BF)
    return hi, (v - hi.astype(F32)).astype(BF)


def iota(dims, axis):
    return lax.broadcasted_iota(jnp.int32, dims, axis)


def to_column(row):
    n = row.shape[1]
    return jnp.sum(jnp.where(iota((n, n), 0) == iota((n, n), 1), row, 0.0), axis=1, keepdims=True)


def to_row(col, width):
    n = col.shape[0]
    return jnp.sum(jnp.where(iota((n, width), 0) == iota((n, width), 1), col, 0.0), axis=0, keepdims=True)


def cos_sin(angle):
    turns = jnp.floor(angle * 0.6366197723675814 + 0.5)
    t = angle - turns * 1.5707855224609375
    t = t - turns * 1.0804334124e-05
    t2 = t * t
    c = 1.0 + t2 * (-0.5 + t2 * (4.1666667e-2 + t2 * (-1.3888889e-3 + t2 * 2.4801587e-5)))
    s = t * (1.0 + t2 * (-1.6666667e-1 + t2 * (8.3333333e-3 + t2 * (-1.9841270e-4 + t2 * 2.7557319e-6))))
    quad = turns.astype(jnp.int32) & 3
    odd = (quad & 1) == 1
    cc = jnp.where(odd, s, c)
    ss = jnp.where(odd, c, s)
    cc = jnp.where((quad == 1) | (quad == 2), -cc, cc)
    ss = jnp.where(quad >= 2, -ss, ss)
    return cc, ss


def place(index, box):
    return (
        (index & (SIDE - 1)).astype(F32) + (box * SIDE).astype(F32),
        ((index >> 3) & (SIDE - 1)).astype(F32),
        (index >> 6).astype(F32),
    )


def stacked(*refs):
    return jnp.concatenate([jnp.concatenate([ref[0], ref[1]], axis=1) for ref in refs], axis=0)


def open_body(out_ref):
    out_ref[...] = jnp.zeros(out_ref.shape, out_ref.dtype)


def plan_body(ranks_ref, skel_ref, contrast_ref, own_ref, beside_ref, dep_ref, *refs, parts):
    e0_ref, e1_ref, q_ref, ghi_ref, glo_ref, g1_ref, j_ref, d_ref, part_ref = refs
    box = lax.axis_index("box")
    me = lax.axis_index("field")
    kmax = skel_ref.shape[2]
    width = contrast_ref.shape[1]
    contrast = contrast_ref[...]
    ranks = ranks_ref[...].astype(F32)
    ranks = jnp.sum(jnp.where(iota(ranks.shape, 1) == box, ranks, 0.0), axis=1, keepdims=True).astype(jnp.int32)
    n = width // parts
    lane = iota((kmax, width), 1)
    turned = (((lane // n) ^ me) * n) + lane % n
    rows = []
    cols = []
    rank = []
    for level in range(2):
        far = box ^ (1 << level)
        own_row = skel_ref[box][level : level + 1, :]
        far_row = skel_ref[far][level : level + 1, :]
        own_col = to_column(own_row.astype(F32)).astype(jnp.int32)
        far_col = to_column(far_row.astype(F32)).astype(jnp.int32)
        r = ranks[level : level + 1, :]
        rows.append(own_row)
        cols.append(own_col)
        rank.append(r)
        hit = (own_col == turned) & (iota((kmax, width), 0) < r)
        (e0_ref, e1_ref)[level][...] = hit.astype(F32).astype(BF)
        true_hit = (own_col == iota((kmax, width), 1)) & (iota((kmax, width), 0) < r)
        q_col = jnp.sum(jnp.where(true_hit, contrast, 0.0), axis=1, keepdims=True)
        q_ref[pl.ds(level, 1), :] = to_row(q_col, kmax)
        ox, oy, oz = place(own_row, box)
        fx, fy, fz = place(far_col, far)
        d2 = (fx - ox) * (fx - ox) + (fy - oy) * (fy - oy) + (fz - oz) * (fz - oz)
        dist = jnp.sqrt(d2)
        inv = 1.0 / dist
        c, s = cos_sin(WAVENUM * dist)
        c = c * inv
        s = s * inv
        if level == 0:
            chi, clo = halves(c)
            shi, slo = halves(s)
            ghi_ref[0:kmax, 0:kmax] = chi
            ghi_ref[0:kmax, kmax:] = shi
            ghi_ref[kmax:, 0:kmax] = -shi
            ghi_ref[kmax:, kmax:] = chi
            glo_ref[0:kmax, 0:kmax] = clo
            glo_ref[0:kmax, kmax:] = slo
            glo_ref[kmax:, 0:kmax] = -slo
            glo_ref[kmax:, kmax:] = clo
        else:
            g1_ref[:, 0:kmax] = c
            g1_ref[:, kmax:] = s
    mine = iota((kmax, kmax), 0)
    other = iota((kmax, kmax), 1)
    j_ref[...] = ((cols[0] == rows[1]) & (mine < rank[0]) & (other < rank[1])).astype(F32).astype(BF)
    d_ref[...] = ((cols[1] == rows[1]) & (mine < rank[1]) & (other < rank[1])).astype(F32).astype(BF)
    part_ref[...] = nn(e0_ref[:, : 2 * n], stacked(own_ref, beside_ref)).astype(BF)


def core_body(own_ref, near_ref, far_ref, g1_ref, d_ref, dep_ref, mc_ref, khi_ref, klo_ref, ct_ref):
    slot = lax.axis_index("box") & 3
    quarter = own_ref.shape[0] // 2
    kmax = own_ref.shape[1]
    pieces = (own_ref[...], near_ref[...], far_ref[0], far_ref[1])
    for mask, piece in enumerate(pieces):
        start = pl.multiple_of((slot ^ mask) * quarter, quarter)
        ct_ref[pl.ds(start, quarter), 0:kmax] = piece[:quarter]
        ct_ref[pl.ds(start, quarter), kmax:] = piece[quarter:]
    cr = ct_ref[:, 0:kmax]
    ci = ct_ref[:, kmax:]
    mc_ref[0:kmax, 0:kmax] = cr
    mc_ref[0:kmax, kmax:] = ci
    mc_ref[kmax:, 0:kmax] = -ci
    mc_ref[kmax:, kmax:] = cr
    dup = d_ref[...]
    gr = g1_ref[:, 0:kmax]
    gi = g1_ref[:, kmax:]
    grh, grl = halves(gr)
    gih, gil = halves(gi)
    dr = nn(grh, dup) + nn(grl, dup)
    di = nn(gih, dup) + nn(gil, dup)
    drh, drl = halves(dr)
    dih, dil = halves(di)
    kr = gr - ((nn(drh, cr) + nn(drl, cr)) - (nn(dih, ci) + nn(dil, ci)))
    ki = gi - ((nn(drh, ci) + nn(drl, ci)) + (nn(dih, cr) + nn(dil, cr)))
    krh, krl = halves(kr)
    kih, kil = halves(ki)
    for ref, a, b in ((khi_ref, krh, kih), (klo_ref, krl, kil)):
        ref[0:kmax, 0:kmax] = a
        ref[0:kmax, kmax:] = b
        ref[kmax:, 0:kmax] = -b
        ref[kmax:, kmax:] = a


def relay_body(in_ref, *rest):
    rest[-1][...] = in_ref[...]


def pair_body(a_ref, b_ref, dep_ref, out_ref):
    out_ref[0] = a_ref[...]
    out_ref[1] = b_ref[...]


def turned_fields(x_ref, start, n):
    re = x_ref[0, start : start + n]
    im = x_ref[1, start : start + n]
    return jnp.concatenate([re, -im], axis=1), jnp.concatenate([im, re], axis=1)


def send(x_ref, picked, q_ref, out_ref, start, n):
    q = q_ref[0:1, :]
    left, right = turned_fields(x_ref, start, n)
    w = jnp.concatenate([nt(left, picked) * q, nt(right, picked) * q], axis=1)
    pack(w, out_ref)


def first_body(part_ref, across_ref, beyond_ref, e0_ref, x_ref, q_ref, picked_ref, out_ref, *, start, n):
    rows = across_ref.shape[1]
    picked = (nn(e0_ref[:, 2 * rows :], stacked(across_ref, beyond_ref)) + part_ref[...].astype(F32)).astype(BF)
    picked_ref[...] = picked
    send(x_ref, picked, q_ref, out_ref, start, n)


def rest_body(x_ref, picked_ref, q_ref, dep_ref, out_ref, *, start, n):
    send(x_ref, picked_ref[...], q_ref, out_ref, start, n)


def rows_body(x_ref, p0_ref, p1_ref, p2_ref, p3_ref, e_ref, dep_ref, v_ref):
    kmax = e_ref.shape[0]
    left, right = turned_fields(x_ref, 0, x_ref.shape[1])
    picked = nn(e_ref[...], stacked(p0_ref, p1_ref, p2_ref, p3_ref)).astype(BF)
    v_ref[:, 0:kmax] = nt(left, picked)
    v_ref[:, kmax:] = nt(right, picked)


def leaf_body(x_ref, p_ref, q_ref, dep_ref, y_ref):
    left, right = turned_fields(x_ref, 0, x_ref.shape[1])
    a = stacked(p_ref, q_ref)
    y_ref[0] = nt(left, a)
    y_ref[1] = nt(right, a)


def pack(w, out_ref):
    n, both = w.shape
    lanes = out_ref.shape[1]
    most = jnp.max(jnp.abs(w), axis=1, keepdims=True)
    step = jnp.ceil(jnp.log2(jnp.maximum(most, 1e-30)) * STEPS)
    inv = TOP / jnp.exp2(step / STEPS)
    v = jnp.floor(w * inv + 0.5).astype(jnp.int32).astype(jnp.int16)
    for i in range(both // lanes):
        out_ref[i * n : (i + 1) * n, :] = v[:, i * lanes : (i + 1) * lanes]
    groups = -(-n // lanes)
    step = to_row(step, groups * lanes)
    tile = jnp.zeros((16, lanes), F32)
    for i in range(groups):
        tile = jnp.where(iota(tile.shape, 0) == i, step[:, i * lanes : (i + 1) * lanes], tile)
    out_ref[both // lanes * n :, :] = tile.astype(jnp.int32).astype(jnp.int16)


def apply_packed(in_ref, mhi, mlo):
    k = mhi.shape[0]
    lanes = in_ref.shape[1]
    pieces = k // lanes
    n = (in_ref.shape[0] - 16) // pieces
    groups = -(-n // lanes)
    steps = in_ref[pieces * n :, :].astype(jnp.int32).astype(F32)
    steps = jnp.concatenate([steps[i : i + 1, :] for i in range(groups)], axis=1)
    own = iota((n, groups * lanes), 0) == iota((n, groups * lanes), 1)
    step = jnp.sum(jnp.where(own, steps, 0.0), axis=1, keepdims=True)
    scale = jnp.exp2(step / STEPS) * (1.0 / TOP)
    v = jnp.concatenate([in_ref[i * n : (i + 1) * n, :] for i in range(pieces)], axis=1).astype(jnp.int32)
    upper = (v + 128) & -256
    lower = (v - upper).astype(F32).astype(BF)
    upper = upper.astype(F32).astype(BF)
    return (nn(upper, mhi) + (nn(lower, mhi) + nn(upper, mlo))) * scale


def second_body(in_ref, ghi_ref, glo_ref, v_ref, j_ref, q_ref, *rest, start):
    out_ref, gs_ref, us_ref = rest[-3:]
    n = gs_ref.shape[1]
    k = j_ref.shape[0]
    g = apply_packed(in_ref, ghi_ref[...], glo_ref[...])
    hi, lo = halves(g)
    gs_ref[0] = hi
    gs_ref[1] = lo
    j = j_ref[...]
    q = q_ref[1:2, :]
    re = v_ref[start : start + n, :k] - (nn(hi[:, :k], j) + nn(lo[:, :k], j))
    im = v_ref[start : start + n, k:] - (nn(hi[:, k:], j) + nn(lo[:, k:], j))
    u = jnp.concatenate([re, im], axis=1)
    pack(u * jnp.concatenate([q, q], axis=1), out_ref)
    hi, lo = halves(u)
    us_ref[0] = hi
    us_ref[1] = lo


def third_body(gs_ref, us_ref, near_ref, far_ref, e0_ref, mc_ref, part_ref, p_ref, *, start):
    n = gs_ref.shape[1]
    k = e0_ref.shape[0]
    e = e0_ref[...]
    for i in range(2):
        cols = slice(i * k, i * k + k)
        y = jnp.concatenate([near_ref[i, start : start + n], far_ref[i, start : start + n]], axis=1)
        part_ref[i] = y - (nn(gs_ref[0, :, cols], e) + nn(gs_ref[1, :, cols], e))
    mc = mc_ref[...]
    p_ref[...] = nn(us_ref[0], mc) + nn(us_ref[1], mc)


def finish(in_ref, part_ref, p_ref, khi, klo, e):
    k = e.shape[0]
    p = p_ref[...] + apply_packed(in_ref, khi, klo)
    hi, lo = halves(p)
    for i in range(2):
        cols = slice(i * k, i * k + k)
        yield i, part_ref[i] - (nn(hi[:, cols], e) + nn(lo[:, cols], e))


def writer(out_ref, sem, blocks):
    me = lax.axis_index("field")
    copies = []

    def write(src_ref, i, row):
        n = src_ref.shape[2] // blocks
        for m in range(blocks):
            col = pl.multiple_of((me ^ m) * n, n)
            copy = pltpu.make_async_copy(
                src_ref.at[i, :, pl.ds(m * n, n)],
                out_ref.at[i, pl.ds(row, src_ref.shape[1]), pl.ds(col, n)],
                sem.at[len(copies)],
            )
            copy.start()
            copies.append(copy)

    return write, copies


def last_body(khi_ref, klo_ref, e1_ref, in_ref, part_ref, p_ref, *rest, start, blocks):
    out_ref, hold_ref, sem = rest[-3:]
    write, copies = writer(out_ref, sem, blocks)
    for i, value in finish(in_ref, part_ref, p_ref, khi_ref[...], klo_ref[...], e1_ref[...]):
        hold_ref[i] = value
        write(hold_ref, i, start)
    for copy in copies:
        copy.wait()


def body(incident, leaf_inverse, contrast, skel_index, ranks, top_core):
    nf, width = incident.shape[1:]
    boxes, _, kmax = skel_index.shape
    quarter = top_core.shape[2]
    own = leaf_inverse[0]
    across = swap(own, "field", 2)
    beside = swap(own, "field", 1)
    core_own = jnp.swapaxes(top_core, 1, 2).reshape(2 * quarter, kmax)
    core_near = swap(core_own, "box", 1)
    n = n_rows = own.shape[1]
    (opened,) = call(open_body, "open", [shape(8, 128)], [], cost=4.0)
    e0, e1, q, ghi, glo, g1, dup01, dup11, part = call(
        lambda *refs: plan_body(*refs, parts=lax.axis_size("field")),
        "plan",
        [
            shape(kmax, width, dtype=BF),
            shape(kmax, width, dtype=BF),
            shape(8, kmax),
            shape(2 * kmax, 2 * kmax, dtype=BF),
            shape(2 * kmax, 2 * kmax, dtype=BF),
            shape(kmax, 2 * kmax),
            shape(kmax, kmax, dtype=BF),
            shape(kmax, kmax, dtype=BF),
            shape(kmax, 2 * width, dtype=BF),
        ],
        [ranks.T, skel_index, contrast.reshape(1, width), own, beside, opened],
        [VMEM] * 5 + [ANY],
    )
    x = incident
    (near,) = call(
        leaf_body, "near", [shape(2, nf, 2 * n)], [x, own, beside, part], [VMEM] * 3 + [ANY], cost=0.7
    )
    (pair,) = call(
        pair_body, "pair", [shape(2, 2 * quarter, kmax, dtype=BF)], [core_own, core_near, near], [VMEM, VMEM, ANY], cost=0.05
    )
    core_far = swap(pair, "box", 2)
    (across,) = call(
        relay_body, "relay", [shape(*across.shape, dtype=BF)], [across, pair, near], [VMEM, ANY, ANY], cost=0.05
    )
    beyond = swap(across, "field", 1)
    chunks = [nf // sum(SHARES) * share for share in SHARES]
    sizes = [(sum(chunks[:i]), n) for i, n in enumerate(chunks)]
    start, n = sizes[0]
    picked, head = call(
        lambda *refs, start=start, n=n: first_body(*refs, start=start, n=n),
        "first",
        [
            shape(kmax, 2 * width, dtype=BF),
            packed_shape(n, kmax),
        ],
        [part, across, beyond, e0, x, q],
        cost=0.8,
    )

    def ready(i, dep, gate=None):
        start, n = sizes[i]
        (packed,) = call(
            lambda *refs: rest_body(*refs, start=start, n=n),
            f"ready{i}",
            [packed_shape(n, kmax)],
            [x, picked, q, dep],
            [VMEM] * 3 + [ANY],
            cost=0.6,
        )
        if i > 1:
            (packed,) = call(
                relay_body, f"gate{i}", [packed_shape(n, kmax)], [packed, gate], [VMEM, ANY], cost=0.05
            )
        return swap(packed, "box", 1)

    got = swap(head, "box", 1)
    (v1,) = call(
        rows_body,
        "rows",
        [shape(nf, 2 * kmax)],
        [x, own, beside, across, beyond, e1, e0],
        [VMEM] * 6 + [ANY],
    )
    late = []
    coming = ready(1, v1)

    def core(dep):
        return call(
            core_body,
            "core",
            [shape(2 * kmax, 2 * kmax, dtype=BF)] * 3,
            [core_own, core_near, core_far, g1, dup11, dep],
            [VMEM] * 5 + [ANY],
            [pltpu.VMEM((kmax, 2 * kmax), BF)],
        )

    def third(i):
        start, n = sizes[i]
        late[i][1:] = call(
            lambda *refs, start=start: third_body(*refs, start=start),
            f"third{i}",
            [shape(2, n, width), shape(n, 2 * kmax)],
            [late[i][1], late[i][2], near, y, e0, mc],
            cost=0.5,
        )

    for i, (start, n) in enumerate(sizes):
        dep = e1
        if i == 1 and 1:
            dep = mc
        if i >= 2 and 0:
            dep = mc if 0 == 1 else late[i - 0][2]
        back, gs, us = call(
            lambda *refs, start=start: second_body(*refs, start=start),
            f"second{i}",
            [packed_shape(n, kmax), shape(2, n, 2 * kmax, dtype=BF), shape(2, n, 2 * kmax, dtype=BF)],
            [got, ghi, glo, v1, dup01, q, dep],
            [VMEM] * 6 + [ANY],
            cost=0.8,
        )
        got = coming
        if 1:
            late.append([swap(back, "box", 2), gs, us])
        if i + 2 < len(sizes):
            coming = ready(i + 2, e1, gs)
        if not 1:
            late.append([swap(back, "box", 2), gs, us])
        if i == 0:
            mc, khi, klo = core(v1)
        if i == 1:
            (y,) = call(
                leaf_body, "leaf", [shape(2, nf, 2 * n_rows)], [x, across, beyond, gs], [VMEM] * 3 + [ANY], cost=0.7
            )
            for j in range(i + 1):
                third(j)
        if i > 1:
            third(i)
    blocks = lax.axis_size("field")
    out = []
    for i, (start, n) in enumerate(sizes):
        out = call(
            lambda *refs, start=start: last_body(*refs, start=start, blocks=blocks),
            f"last{i}",
            [shape(2, nf, width)],
            [khi, klo, e1] + late[i] + out,
            [VMEM] * 6 + [ANY] * len(out),
            [pltpu.VMEM((2, n, width), F32), pltpu.SemaphoreType.DMA((2 * blocks,))],
            out_specs=[ANY],
            input_output_aliases={6: 0} if out else {},
        )
    return out[0]


def solution(mesh):
    return jax.shard_map(
        body,
        mesh=mesh,
        in_specs=(P(None, "field", "box"), P("box", None, "field", None), P("box"), P(), P(), P(None, None, "box")),
        out_specs=P(None, "field", "box"),
        check_vma=False,
    )
```

```python
import jax
import jax.numpy as jnp
from jax import lax
from jax.experimental import pallas as pl
from jax.experimental.pallas import tpu as pltpu
from jax.sharding import PartitionSpec as P

SIDE = 8
WAVENUM = 0.7
BF = jnp.bfloat16
F32 = jnp.float32
SHARES = (13, 12, 7)
TOP = 32766.0
STEPS = 128.0
LANES = 128
VMEM = pl.BlockSpec(memory_space=pltpu.VMEM)
SMEM = pl.BlockSpec(memory_space=pltpu.SMEM)
ANY = pl.BlockSpec(memory_space=pl.ANY)
PARAMS = pltpu.CompilerParams(vmem_limit_bytes=40 * 1024 * 1024)


def swap(value, axis, mask):
    return lax.ppermute(value, axis, [(s, s ^ mask) for s in range(lax.axis_size(axis))])


def call(body, name, outs, ins, specs=None, scratch=(), cost=1.0, **kw):
    return list(
        pl.pallas_call(
        body,
        name=name,
        out_shape=outs,
        in_specs=specs or [VMEM] * len(ins),
        out_specs=kw.pop("out_specs", [VMEM] * len(outs)),
        scratch_shapes=list(scratch),
        compiler_params=PARAMS,
        cost_estimate=pl.CostEstimate(flops=int(cost * 1e9), bytes_accessed=int(cost * 3e6), transcendentals=0),
        **kw,
    )(*ins)
    )


def shape(*dims, dtype=F32):
    return jax.ShapeDtypeStruct(dims, dtype)


def packed_shape(n, kmax):
    return shape(2 * n * kmax // LANES + 16, LANES, dtype=jnp.int16)


def nn(a, b):
    return lax.dot_general(a, b, (((1,), (0,)), ((), ())), preferred_element_type=F32)


def nt(a, b):
    return lax.dot_general(a, b, (((1,), (1,)), ((), ())), preferred_element_type=F32)


def halves(v):
    hi = v.astype(BF)
    return hi, (v - hi.astype(F32)).astype(BF)


def iota(dims, axis):
    return lax.broadcasted_iota(jnp.int32, dims, axis)


def to_column(row):
    n = row.shape[1]
    return jnp.sum(jnp.where(iota((n, n), 0) == iota((n, n), 1), row, 0.0), axis=1, keepdims=True)


def to_row(col, width):
    n = col.shape[0]
    return jnp.sum(jnp.where(iota((n, width), 0) == iota((n, width), 1), col, 0.0), axis=0, keepdims=True)


def cos_sin(angle):
    turns = jnp.floor(angle * 0.6366197723675814 + 0.5)
    t = angle - turns * 1.5707855224609375
    t = t - turns * 1.0804334124e-05
    t2 = t * t
    c = 1.0 + t2 * (-0.5 + t2 * (4.1666667e-2 + t2 * (-1.3888889e-3 + t2 * 2.4801587e-5)))
    s = t * (1.0 + t2 * (-1.6666667e-1 + t2 * (8.3333333e-3 + t2 * (-1.9841270e-4 + t2 * 2.7557319e-6))))
    quad = turns.astype(jnp.int32) & 3
    odd = (quad & 1) == 1
    cc = jnp.where(odd, s, c)
    ss = jnp.where(odd, c, s)
    cc = jnp.where((quad == 1) | (quad == 2), -cc, cc)
    ss = jnp.where(quad >= 2, -ss, ss)
    return cc, ss


def place(index, box):
    return (
        (index & (SIDE - 1)).astype(F32) + (box * SIDE).astype(F32),
        ((index >> 3) & (SIDE - 1)).astype(F32),
        (index >> 6).astype(F32),
    )


def stacked(*refs):
    return jnp.concatenate([jnp.concatenate([ref[0], ref[1]], axis=1) for ref in refs], axis=0)


def open_body(out_ref):
    out_ref[...] = jnp.zeros(out_ref.shape, out_ref.dtype)


def green(own_row, own_box, far_col, far_box):
    ox, oy, oz = place(own_row, own_box)
    fx, fy, fz = place(far_col, far_box)
    d2 = (fx - ox) * (fx - ox) + (fy - oy) * (fy - oy) + (fz - oz) * (fz - oz)
    dist = jnp.sqrt(d2)
    inv = 1.0 / dist
    c, s = cos_sin(WAVENUM * dist)
    return c * inv, s * inv


def store_complex(ref, re, im):
    k = re.shape[0]
    ref[0:k, 0:k] = re
    ref[0:k, k:] = im
    ref[k:, 0:k] = -im
    ref[k:, k:] = re


def store_halves(hi_ref, lo_ref, re, im):
    rhi, rlo = halves(re)
    ihi, ilo = halves(im)
    store_complex(hi_ref, rhi, ihi)
    store_complex(lo_ref, rlo, ilo)


def matches(col, rank_col, row, rank_row):
    k = col.shape[0]
    hit = (col == row) & (iota((k, k), 0) < rank_col) & (iota((k, k), 1) < rank_row)
    return hit.astype(F32).astype(BF)


def plan_body(ranks_ref, skel_ref, contrast_ref, own_ref, beside_ref, dep_ref, *refs, parts):
    e0_ref, e1_ref, q_ref, ghi_ref, glo_ref, g1_ref, j_ref, d_ref, part_ref, hhi_ref, hlo_ref, jp_ref = refs
    box = lax.axis_index("box")
    me = lax.axis_index("field")
    kmax = skel_ref.shape[2]
    width = contrast_ref.shape[1]
    contrast = contrast_ref[...]
    all_ranks = ranks_ref[...].astype(F32)

    def ranks_of(at):
        mine = jnp.where(iota(all_ranks.shape, 1) == at, all_ranks, 0.0)
        return jnp.sum(mine, axis=1, keepdims=True).astype(jnp.int32)

    def row_of(at, level):
        return skel_ref[at][level : level + 1, :]

    def col_of(at, level):
        return to_column(row_of(at, level).astype(F32)).astype(jnp.int32)

    ranks = ranks_of(box)
    n = width // parts
    lane = iota((kmax, width), 1)
    turned = (((lane // n) ^ me) * n) + lane % n
    cols = []
    for level in range(2):
        far = box ^ (1 << level)
        own_col = col_of(box, level)
        r = ranks[level : level + 1, :]
        cols.append(own_col)
        hit = (own_col == turned) & (iota((kmax, width), 0) < r)
        (e0_ref, e1_ref)[level][...] = hit.astype(F32).astype(BF)
        true_hit = (own_col == iota((kmax, width), 1)) & (iota((kmax, width), 0) < r)
        q_col = jnp.sum(jnp.where(true_hit, contrast, 0.0), axis=1, keepdims=True)
        q_ref[pl.ds(level, 1), :] = to_row(q_col, kmax)
        c, s = green(row_of(box, level), box, col_of(far, level), far)
        if level == 0:
            store_halves(ghi_ref, glo_ref, c, s)
        else:
            g1_ref[:, 0:kmax] = c
            g1_ref[:, kmax:] = s
    j_ref[...] = matches(cols[0], ranks[0:1, :], row_of(box, 1), ranks[1:2, :])
    d_ref[...] = matches(cols[1], ranks[1:2, :], row_of(box, 1), ranks[1:2, :])
    part_ref[...] = nn(e0_ref[:, : 2 * n], stacked(own_ref, beside_ref)).astype(BF)
    mate = box ^ 2
    mate_ranks = ranks_of(mate)
    c, s = green(row_of(mate, 0), mate, col_of(box ^ 3, 0), box ^ 3)
    store_halves(hhi_ref, hlo_ref, c, s)
    jp_ref[...] = matches(col_of(mate, 0), mate_ranks[0:1, :], row_of(mate, 1), mate_ranks[1:2, :])


def core_body(own_ref, near_ref, far_ref, g1_ref, d_ref, dep_ref, mc_ref, khi_ref, klo_ref, ct_ref):
    slot = lax.axis_index("box") & 3
    quarter = own_ref.shape[0] // 2
    kmax = own_ref.shape[1]
    pieces = (own_ref[...], near_ref[...], far_ref[0], far_ref[1])
    for mask, piece in enumerate(pieces):
        start = pl.multiple_of((slot ^ mask) * quarter, quarter)
        ct_ref[pl.ds(start, quarter), 0:kmax] = piece[:quarter]
        ct_ref[pl.ds(start, quarter), kmax:] = piece[quarter:]
    cr = ct_ref[:, 0:kmax]
    ci = ct_ref[:, kmax:]
    mc_ref[0:kmax, 0:kmax] = cr
    mc_ref[0:kmax, kmax:] = ci
    mc_ref[kmax:, 0:kmax] = -ci
    mc_ref[kmax:, kmax:] = cr
    dup = d_ref[...]
    gr = g1_ref[:, 0:kmax]
    gi = g1_ref[:, kmax:]
    grh, grl = halves(gr)
    gih, gil = halves(gi)
    dr = nn(grh, dup) + nn(grl, dup)
    di = nn(gih, dup) + nn(gil, dup)
    drh, drl = halves(dr)
    dih, dil = halves(di)
    kr = gr - ((nn(drh, cr) + nn(drl, cr)) - (nn(dih, ci) + nn(dil, ci)))
    ki = gi - ((nn(drh, ci) + nn(drl, ci)) + (nn(dih, cr) + nn(dil, cr)))
    krh, krl = halves(kr)
    kih, kil = halves(ki)
    for ref, a, b in ((khi_ref, krh, kih), (klo_ref, krl, kil)):
        ref[0:kmax, 0:kmax] = a
        ref[0:kmax, kmax:] = b
        ref[kmax:, 0:kmax] = -b
        ref[kmax:, kmax:] = a


def relay_body(in_ref, *rest):
    rest[-1][...] = in_ref[...]


def pair_body(a_ref, b_ref, dep_ref, out_ref):
    out_ref[0] = a_ref[...]
    out_ref[1] = b_ref[...]


def turned_fields(x_ref, start, n):
    re = x_ref[0, start : start + n]
    im = x_ref[1, start : start + n]
    return jnp.concatenate([re, -im], axis=1), jnp.concatenate([im, re], axis=1)


def send(x_ref, picked, q_ref, out_ref, start, n):
    q = q_ref[0:1, :]
    left, right = turned_fields(x_ref, start, n)
    w = jnp.concatenate([nt(left, picked) * q, nt(right, picked) * q], axis=1)
    pack(w, out_ref)


def first_body(part_ref, across_ref, beyond_ref, e0_ref, x_ref, q_ref, picked_ref, out_ref, *, start, n):
    rows = across_ref.shape[1]
    picked = (nn(e0_ref[:, 2 * rows :], stacked(across_ref, beyond_ref)) + part_ref[...].astype(F32)).astype(BF)
    picked_ref[...] = picked
    send(x_ref, picked, q_ref, out_ref, start, n)


def rest_body(x_ref, picked_ref, q_ref, dep_ref, out_ref, *, start, n):
    send(x_ref, picked_ref[...], q_ref, out_ref, start, n)


def rows_body(x_ref, picked_ref, dep_ref, v_ref):
    kmax = picked_ref.shape[0]
    left, right = turned_fields(x_ref, 0, x_ref.shape[1])
    picked = picked_ref[...]
    v_ref[:, 0:kmax] = nt(left, picked)
    v_ref[:, kmax:] = nt(right, picked)


def ahead_body(x_ref, p0_ref, p1_ref, p2_ref, p3_ref, e1_ref, picked0_ref, q_ref, dep_ref, picked_ref, out_ref, *, start, n):
    half = out_ref.shape[0] // 2
    picked0 = picked0_ref[...]
    picked = nn(e1_ref[...], stacked(p0_ref, p1_ref, p2_ref, p3_ref)).astype(BF)
    picked_ref[...] = picked
    left, right = turned_fields(x_ref, start, n)
    for i, rows in enumerate((picked0, picked)):
        q = q_ref[i : i + 1, :]
        w = jnp.concatenate([nt(left, rows) * q, nt(right, rows) * q], axis=1)
        pack(w, out_ref.at[i * half : (i + 1) * half], q_ref[1:2, :])


def onward_body(own_ref, got_ref, out_ref):
    half = own_ref.shape[0] // 2
    out_ref[0:half] = own_ref[0:half]
    out_ref[half:] = got_ref[0:half]


def pick(hi, lo, sel):
    k = sel.shape[0]
    parts = [nn(hi[:, i : i + k], sel) + nn(lo[:, i : i + k], sel) for i in (0, k)]
    return jnp.concatenate(parts, axis=1)


def around_body(*refs, start):
    (near_in_ref, mate_ref, ghi_ref, glo_ref, hhi_ref, hlo_ref, j_ref, jp_ref) = refs[:8]
    (v_ref, near_ref, far_ref, e0_ref, e1_ref, mc_ref, khi_ref, klo_ref, out_ref) = refs[8:]
    half = near_in_ref.shape[0] // 2
    n = out_ref.shape[1]
    k = j_ref.shape[0]
    lanes = mate_ref.shape[1]
    count = k // lanes
    mhi = khi_ref[...]
    mlo = klo_ref[...]
    t = apply_packed(near_in_ref.at[half : 2 * half], hhi_ref[...], hlo_ref[...])
    tail = mate_ref[half - 16 : half, :].astype(jnp.int32).astype(F32)
    upper = jnp.concatenate([tail[2 + i : 3 + i, :] for i in range(count)], axis=1)
    lower = jnp.concatenate([tail[2 + count + i : 3 + count + i, :] for i in range(count)], axis=1)
    q = (upper + lower * (1.0 / 32768.0)) * (1.0 / 16384.0)
    v, scale = unpack(mate_ref.at[half : 2 * half], 2 * k)
    w = v.astype(F32) * scale - pick(*halves(t), jp_ref[...]) * jnp.concatenate([q, q], axis=1)
    hi, lo = halves(w)
    p = nn(hi, mhi) + (nn(lo, mhi) + nn(hi, mlo))
    g = apply_packed(near_in_ref.at[0:half], ghi_ref[...], glo_ref[...])
    gh, gl = halves(g)
    u = v_ref[start : start + n, :] - pick(gh, gl, j_ref[...])
    uh, ul = halves(u)
    mc = mc_ref[...]
    p = p + (nn(uh, mc) + nn(ul, mc))
    ph, pl_ = halves(p)
    e0 = e0_ref[...]
    e1 = e1_ref[...]
    for i in range(2):
        cols = slice(i * k, i * k + k)
        y = jnp.concatenate([near_ref[i, start : start + n], far_ref[i, start : start + n]], axis=1)
        scattered = (nn(gh[:, cols], e0) + nn(gl[:, cols], e0)) + (nn(ph[:, cols], e1) + nn(pl_[:, cols], e1))
        out_ref[i] = y - scattered


def leaf_body(x_ref, p_ref, q_ref, dep_ref, y_ref):
    left, right = turned_fields(x_ref, 0, x_ref.shape[1])
    a = stacked(p_ref, q_ref)
    y_ref[0] = nt(left, a)
    y_ref[1] = nt(right, a)


def pack(w, out_ref, weight=None):
    n, both = w.shape
    lanes = out_ref.shape[1]
    most = jnp.max(jnp.abs(w), axis=1, keepdims=True)
    step = jnp.ceil(jnp.log2(jnp.maximum(most, 1e-30)) * STEPS)
    inv = TOP / jnp.exp2(step / STEPS)
    v = jnp.floor(w * inv + 0.5).astype(jnp.int32).astype(jnp.int16)
    for i in range(both // lanes):
        out_ref[i * n : (i + 1) * n, :] = v[:, i * lanes : (i + 1) * lanes]
    groups = -(-n // lanes)
    step = to_row(step, groups * lanes)
    tile = jnp.zeros((16, lanes), F32)
    for i in range(groups):
        tile = jnp.where(iota(tile.shape, 0) == i, step[:, i * lanes : (i + 1) * lanes], tile)
    if weight is not None:
        upper = jnp.floor(weight * 16384.0)
        lower = jnp.floor((weight * 16384.0 - upper) * 32768.0)
        count = weight.shape[1] // lanes
        for j, value in enumerate((upper, lower)):
            for i in range(count):
                at = iota(tile.shape, 0) == 2 + j * count + i
                tile = jnp.where(at, value[:, i * lanes : (i + 1) * lanes], tile)
    out_ref[both // lanes * n :, :] = tile.astype(jnp.int32).astype(jnp.int16)


def unpack(in_ref, k):
    lanes = in_ref.shape[1]
    pieces = k // lanes
    n = (in_ref.shape[0] - 16) // pieces
    groups = -(-n // lanes)
    steps = in_ref[pieces * n :, :].astype(jnp.int32).astype(F32)
    steps = jnp.concatenate([steps[i : i + 1, :] for i in range(groups)], axis=1)
    own = iota((n, groups * lanes), 0) == iota((n, groups * lanes), 1)
    step = jnp.sum(jnp.where(own, steps, 0.0), axis=1, keepdims=True)
    scale = jnp.exp2(step / STEPS) * (1.0 / TOP)
    v = jnp.concatenate([in_ref[i * n : (i + 1) * n, :] for i in range(pieces)], axis=1).astype(jnp.int32)
    return v, scale


def apply_packed(in_ref, mhi, mlo):
    v, scale = unpack(in_ref, mhi.shape[0])
    upper = (v + 128) & -256
    lower = (v - upper).astype(F32).astype(BF)
    upper = upper.astype(F32).astype(BF)
    return (nn(upper, mhi) + (nn(lower, mhi) + nn(upper, mlo))) * scale


def second_body(in_ref, ghi_ref, glo_ref, v_ref, j_ref, q_ref, *rest, start):
    out_ref, gs_ref, us_ref = rest[-3:]
    n = gs_ref.shape[1]
    k = j_ref.shape[0]
    g = apply_packed(in_ref, ghi_ref[...], glo_ref[...])
    hi, lo = halves(g)
    gs_ref[0] = hi
    gs_ref[1] = lo
    j = j_ref[...]
    q = q_ref[1:2, :]
    re = v_ref[start : start + n, :k] - (nn(hi[:, :k], j) + nn(lo[:, :k], j))
    im = v_ref[start : start + n, k:] - (nn(hi[:, k:], j) + nn(lo[:, k:], j))
    u = jnp.concatenate([re, im], axis=1)
    pack(u * jnp.concatenate([q, q], axis=1), out_ref)
    hi, lo = halves(u)
    us_ref[0] = hi
    us_ref[1] = lo


def third_body(gs_ref, us_ref, near_ref, far_ref, e0_ref, mc_ref, part_ref, p_ref, *, start):
    n = gs_ref.shape[1]
    k = e0_ref.shape[0]
    e = e0_ref[...]
    for i in range(2):
        cols = slice(i * k, i * k + k)
        y = jnp.concatenate([near_ref[i, start : start + n], far_ref[i, start : start + n]], axis=1)
        part_ref[i] = y - (nn(gs_ref[0, :, cols], e) + nn(gs_ref[1, :, cols], e))
    mc = mc_ref[...]
    p_ref[...] = nn(us_ref[0], mc) + nn(us_ref[1], mc)


def finish(in_ref, part_ref, p_ref, khi, klo, e):
    k = e.shape[0]
    p = p_ref[...] + apply_packed(in_ref, khi, klo)
    hi, lo = halves(p)
    for i in range(2):
        cols = slice(i * k, i * k + k)
        yield i, part_ref[i] - (nn(hi[:, cols], e) + nn(lo[:, cols], e))


def writer(out_ref, sem, blocks):
    me = lax.axis_index("field")
    copies = []

    def write(src_ref, i, row):
        n = src_ref.shape[2] // blocks
        for m in range(blocks):
            col = pl.multiple_of((me ^ m) * n, n)
            copy = pltpu.make_async_copy(
                src_ref.at[i, :, pl.ds(m * n, n)],
                out_ref.at[i, pl.ds(row, src_ref.shape[1]), pl.ds(col, n)],
                sem.at[len(copies)],
            )
            copy.start()
            copies.append(copy)

    return write, copies


def last_body(khi_ref, klo_ref, e1_ref, in_ref, part_ref, p_ref, *rest, start, blocks, done_at):
    out_ref, hold_ref, sem = rest[-3:]
    write, copies = writer(out_ref, sem, blocks)
    if done_at is not None:
        for i in range(2):
            write(rest[0], i, done_at)
    for i, value in finish(in_ref, part_ref, p_ref, khi_ref[...], klo_ref[...], e1_ref[...]):
        hold_ref[i] = value
        write(hold_ref, i, start)
    for copy in copies:
        copy.wait()


def body(incident, leaf_inverse, contrast, skel_index, ranks, top_core):
    nf, width = incident.shape[1:]
    boxes, _, kmax = skel_index.shape
    quarter = top_core.shape[2]
    own = leaf_inverse[0]
    across = swap(own, "field", 2)
    beside = swap(own, "field", 1)
    core_own = jnp.swapaxes(top_core, 1, 2).reshape(2 * quarter, kmax)
    core_near = swap(core_own, "box", 1)
    n = n_rows = own.shape[1]
    (opened,) = call(open_body, "open", [shape(8, 128)], [], cost=4.0)
    e0, e1, q, ghi, glo, g1, dup01, dup11, part, hhi, hlo, dupm = call(
        lambda *refs: plan_body(*refs, parts=lax.axis_size("field")),
        "plan",
        [
            shape(kmax, width, dtype=BF),
            shape(kmax, width, dtype=BF),
            shape(8, kmax),
            shape(2 * kmax, 2 * kmax, dtype=BF),
            shape(2 * kmax, 2 * kmax, dtype=BF),
            shape(kmax, 2 * kmax),
            shape(kmax, kmax, dtype=BF),
            shape(kmax, kmax, dtype=BF),
            shape(kmax, 2 * width, dtype=BF),
            shape(2 * kmax, 2 * kmax, dtype=BF),
            shape(2 * kmax, 2 * kmax, dtype=BF),
            shape(kmax, kmax, dtype=BF),
        ],
        [ranks.T, skel_index, contrast.reshape(1, width), own, beside, opened],
        [VMEM] * 5 + [ANY],
    )
    x = incident
    (near,) = call(
        leaf_body, "near", [shape(2, nf, 2 * n)], [x, own, beside, part], [VMEM] * 3 + [ANY], cost=0.7
    )
    (pair,) = call(
        pair_body, "pair", [shape(2, 2 * quarter, kmax, dtype=BF)], [core_own, core_near, near], [VMEM, VMEM, ANY], cost=0.05
    )
    core_far = swap(pair, "box", 2)
    (across,) = call(
        relay_body, "relay", [shape(*across.shape, dtype=BF)], [across, pair, near], [VMEM, ANY, ANY], cost=0.05
    )
    beyond = swap(across, "field", 1)
    chunks = [nf // sum(SHARES) * share for share in SHARES]
    sizes = [(sum(chunks[:i]), n) for i, n in enumerate(chunks)]
    start, n = sizes[0]
    picked, head = call(
        lambda *refs, start=start, n=n: first_body(*refs, start=start, n=n),
        "first",
        [
            shape(kmax, 2 * width, dtype=BF),
            packed_shape(n, kmax),
        ],
        [part, across, beyond, e0, x, q],
        cost=0.8,
    )

    got = swap(head, "box", 1)
    side_start, side_n = sizes[2]
    picked1, ahead = call(
        lambda *refs: ahead_body(*refs, start=side_start, n=side_n),
        "ahead",
        [shape(kmax, 2 * width, dtype=BF), shape(2 * packed_shape(side_n, kmax).shape[0], LANES, dtype=jnp.int16)],
        [x, own, beside, across, beyond, e1, picked, q, e0],
        [VMEM] * 8 + [ANY],
        cost=1.4,
    )
    mate = swap(ahead, "box", 2)
    start, n = sizes[1]
    (packed,) = call(
        lambda *refs: rest_body(*refs, start=start, n=n),
        "ready",
        [packed_shape(n, kmax)],
        [x, picked, q, ahead],
        [VMEM] * 3 + [ANY],
        cost=0.6,
    )
    coming = swap(packed, "box", 1)
    (v1,) = call(rows_body, "rows", [shape(nf, 2 * kmax)], [x, picked1, picked1], [VMEM] * 2 + [ANY])
    late = []
    for i, (start, n) in enumerate(sizes[:2]):
        back, gs, us = call(
            lambda *refs, start=start: second_body(*refs, start=start),
            f"second{i}",
            [packed_shape(n, kmax), shape(2, n, 2 * kmax, dtype=BF), shape(2, n, 2 * kmax, dtype=BF)],
            [got, ghi, glo, v1, dup01, q, mc if i else e1],
            [VMEM] * 6 + [ANY],
            cost=0.8,
        )
        got = coming
        late.append([swap(back, "box", 2), gs, us])
        if i == 0:
            (onward,) = call(onward_body, "onward", [shape(*ahead.shape, dtype=jnp.int16)], [ahead, mate], cost=0.05)
            sent = onward
            onward = swap(onward, "box", 1)
            mc, khi, klo = call(
                core_body,
                "core",
                [shape(2 * kmax, 2 * kmax, dtype=BF)] * 3,
                [core_own, core_near, core_far, g1, dup11, picked1],
                [VMEM] * 5 + [ANY],
                [pltpu.VMEM((kmax, 2 * kmax), BF)],
            )
    (far,) = call(
        leaf_body, "leaf", [shape(2, nf, 2 * n_rows)], [x, across, beyond, mc], [VMEM] * 3 + [ANY], cost=0.7
    )
    for i, (start, n) in enumerate(sizes[:2]):
        late[i][1:] = call(
            lambda *refs, start=start: third_body(*refs, start=start),
            f"third{i}",
            [shape(2, n, width), shape(n, 2 * kmax)],
            [late[i][1], late[i][2], near, far, e0, mc],
            cost=0.5,
        )
    side = call(
        lambda *refs: around_body(*refs, start=side_start),
        "around",
        [shape(2, side_n, width)],
        [onward, mate, ghi, glo, hhi, hlo, dup01, dupm, v1, near, far, e0, e1, mc, khi, klo],
        cost=2.5,
    )
    blocks = lax.axis_size("field")
    out = []
    for i, (start, n) in enumerate(sizes[:2]):
        ready = side if i == 1 else []
        out = call(
            lambda *refs, start=start, ready=ready: last_body(
                *refs, start=start, blocks=blocks, done_at=side_start if ready else None
            ),
            f"last{i}",
            [shape(2, nf, width)],
            [khi, klo, e1] + late[i] + ready + out,
            [VMEM] * (6 + len(ready)) + [ANY] * len(out),
            [pltpu.VMEM((2, n, width), F32), pltpu.SemaphoreType.DMA(((4 if ready else 2) * blocks,))],
            out_specs=[ANY],
            input_output_aliases={6 + len(ready): 0} if out else {},
        )
    return out[0]


def solution(mesh):
    return jax.shard_map(
        body,
        mesh=mesh,
        in_specs=(P(None, "field", "box"), P("box", None, "field", None), P("box"), P(), P(), P(None, None, "box")),
        out_specs=P(None, "field", "box"),
        check_vma=False,
    )
```

```python
import jax
import jax.numpy as jnp
from jax import lax
from jax.experimental import pallas as pl
from jax.experimental.pallas import tpu as pltpu
from jax.sharding import PartitionSpec as P

SIDE = 8
WAVENUM = 0.7
BF = jnp.bfloat16
F32 = jnp.float32
SHARES = (13, 12, 7)
TOP = 32766.0
STEPS = 128.0
LANES = 128
VMEM = pl.BlockSpec(memory_space=pltpu.VMEM)
SMEM = pl.BlockSpec(memory_space=pltpu.SMEM)
ANY = pl.BlockSpec(memory_space=pl.ANY)
PARAMS = pltpu.CompilerParams(vmem_limit_bytes=40 * 1024 * 1024)


def swap(value, axis, mask):
    return lax.ppermute(value, axis, [(s, s ^ mask) for s in range(lax.axis_size(axis))])


def call(body, name, outs, ins, specs=None, scratch=(), cost=1.0, **kw):
    return list(
        pl.pallas_call(
        body,
        name=name,
        out_shape=outs,
        in_specs=specs or [VMEM] * len(ins),
        out_specs=kw.pop("out_specs", [VMEM] * len(outs)),
        scratch_shapes=list(scratch),
        compiler_params=PARAMS,
        cost_estimate=pl.CostEstimate(flops=int(cost * 1e9), bytes_accessed=int(cost * 3e6), transcendentals=0),
        **kw,
    )(*ins)
    )


def shape(*dims, dtype=F32):
    return jax.ShapeDtypeStruct(dims, dtype)


def packed_shape(n, kmax):
    return shape(2 * n * kmax // LANES + 16, LANES, dtype=jnp.int16)


def nn(a, b):
    return lax.dot_general(a, b, (((1,), (0,)), ((), ())), preferred_element_type=F32)


def nt(a, b):
    return lax.dot_general(a, b, (((1,), (1,)), ((), ())), preferred_element_type=F32)


def halves(v):
    hi = v.astype(BF)
    return hi, (v - hi.astype(F32)).astype(BF)


def iota(dims, axis):
    return lax.broadcasted_iota(jnp.int32, dims, axis)


def to_column(row):
    n = row.shape[1]
    return jnp.sum(jnp.where(iota((n, n), 0) == iota((n, n), 1), row, 0.0), axis=1, keepdims=True)


def to_row(col, width):
    n = col.shape[0]
    return jnp.sum(jnp.where(iota((n, width), 0) == iota((n, width), 1), col, 0.0), axis=0, keepdims=True)


def cos_sin(angle):
    turns = jnp.floor(angle * 0.6366197723675814 + 0.5)
    t = angle - turns * 1.5707855224609375
    t = t - turns * 1.0804334124e-05
    t2 = t * t
    c = 1.0 + t2 * (-0.5 + t2 * (4.1666667e-2 + t2 * (-1.3888889e-3 + t2 * 2.4801587e-5)))
    s = t * (1.0 + t2 * (-1.6666667e-1 + t2 * (8.3333333e-3 + t2 * (-1.9841270e-4 + t2 * 2.7557319e-6))))
    quad = turns.astype(jnp.int32) & 3
    odd = (quad & 1) == 1
    cc = jnp.where(odd, s, c)
    ss = jnp.where(odd, c, s)
    cc = jnp.where((quad == 1) | (quad == 2), -cc, cc)
    ss = jnp.where(quad >= 2, -ss, ss)
    return cc, ss


def place(index, box):
    return (
        (index & (SIDE - 1)).astype(F32) + (box * SIDE).astype(F32),
        ((index >> 3) & (SIDE - 1)).astype(F32),
        (index >> 6).astype(F32),
    )


def stacked(*refs):
    return jnp.concatenate([jnp.concatenate([ref[0], ref[1]], axis=1) for ref in refs], axis=0)


def open_body(out_ref):
    out_ref[...] = jnp.zeros(out_ref.shape, out_ref.dtype)


def green(own_row, own_box, far_col, far_box):
    ox, oy, oz = place(own_row, own_box)
    fx, fy, fz = place(far_col, far_box)
    d2 = (fx - ox) * (fx - ox) + (fy - oy) * (fy - oy) + (fz - oz) * (fz - oz)
    dist = jnp.sqrt(d2)
    inv = 1.0 / dist
    c, s = cos_sin(WAVENUM * dist)
    return c * inv, s * inv


def store_complex(ref, re, im):
    k = re.shape[0]
    ref[0:k, 0:k] = re
    ref[0:k, k:] = im
    ref[k:, 0:k] = -im
    ref[k:, k:] = re


def store_halves(hi_ref, lo_ref, re, im):
    rhi, rlo = halves(re)
    ihi, ilo = halves(im)
    store_complex(hi_ref, rhi, ihi)
    store_complex(lo_ref, rlo, ilo)


def matches(col, rank_col, row, rank_row):
    k = col.shape[0]
    hit = (col == row) & (iota((k, k), 0) < rank_col) & (iota((k, k), 1) < rank_row)
    return hit.astype(F32).astype(BF)


def plan_body(ranks_ref, skel_ref, contrast_ref, own_ref, beside_ref, dep_ref, *refs, parts):
    e0_ref, e1_ref, q_ref, ghi_ref, glo_ref, g1_ref, j_ref, d_ref, part_ref, hhi_ref, hlo_ref, jp_ref = refs
    box = lax.axis_index("box")
    me = lax.axis_index("field")
    kmax = skel_ref.shape[2]
    width = contrast_ref.shape[1]
    contrast = contrast_ref[...]
    all_ranks = ranks_ref[...].astype(F32)

    def ranks_of(at):
        mine = jnp.where(iota(all_ranks.shape, 1) == at, all_ranks, 0.0)
        return jnp.sum(mine, axis=1, keepdims=True).astype(jnp.int32)

    def row_of(at, level):
        return skel_ref[at][level : level + 1, :]

    def col_of(at, level):
        return to_column(row_of(at, level).astype(F32)).astype(jnp.int32)

    ranks = ranks_of(box)
    n = width // parts
    lane = iota((kmax, width), 1)
    turned = (((lane // n) ^ me) * n) + lane % n
    cols = []
    for level in range(2):
        far = box ^ (1 << level)
        own_col = col_of(box, level)
        r = ranks[level : level + 1, :]
        cols.append(own_col)
        hit = (own_col == turned) & (iota((kmax, width), 0) < r)
        (e0_ref, e1_ref)[level][...] = hit.astype(F32).astype(BF)
        true_hit = (own_col == iota((kmax, width), 1)) & (iota((kmax, width), 0) < r)
        q_col = jnp.sum(jnp.where(true_hit, contrast, 0.0), axis=1, keepdims=True)
        q_ref[pl.ds(level, 1), :] = to_row(q_col, kmax)
        c, s = green(row_of(box, level), box, col_of(far, level), far)
        if level == 0:
            store_halves(ghi_ref, glo_ref, c, s)
        else:
            g1_ref[:, 0:kmax] = c
            g1_ref[:, kmax:] = s
    j_ref[...] = matches(cols[0], ranks[0:1, :], row_of(box, 1), ranks[1:2, :])
    d_ref[...] = matches(cols[1], ranks[1:2, :], row_of(box, 1), ranks[1:2, :])
    part_ref[...] = nn(e0_ref[:, : 2 * n], stacked(own_ref, beside_ref)).astype(BF)
    mate = box ^ 2
    mate_ranks = ranks_of(mate)
    c, s = green(row_of(mate, 0), mate, col_of(box ^ 3, 0), box ^ 3)
    store_halves(hhi_ref, hlo_ref, c, s)
    jp_ref[...] = matches(col_of(mate, 0), mate_ranks[0:1, :], row_of(mate, 1), mate_ranks[1:2, :])


def core_body(own_ref, near_ref, far_ref, g1_ref, d_ref, dep_ref, mc_ref, khi_ref, klo_ref, ct_ref):
    slot = lax.axis_index("box") & 3
    quarter = own_ref.shape[0] // 2
    kmax = own_ref.shape[1]
    pieces = (own_ref[...], near_ref[...], far_ref[0], far_ref[1])
    for mask, piece in enumerate(pieces):
        start = pl.multiple_of((slot ^ mask) * quarter, quarter)
        ct_ref[pl.ds(start, quarter), 0:kmax] = piece[:quarter]
        ct_ref[pl.ds(start, quarter), kmax:] = piece[quarter:]
    cr = ct_ref[:, 0:kmax]
    ci = ct_ref[:, kmax:]
    mc_ref[0:kmax, 0:kmax] = cr
    mc_ref[0:kmax, kmax:] = ci
    mc_ref[kmax:, 0:kmax] = -ci
    mc_ref[kmax:, kmax:] = cr
    dup = d_ref[...]
    gr = g1_ref[:, 0:kmax]
    gi = g1_ref[:, kmax:]
    grh, grl = halves(gr)
    gih, gil = halves(gi)
    dr = nn(grh, dup) + nn(grl, dup)
    di = nn(gih, dup) + nn(gil, dup)
    drh, drl = halves(dr)
    dih, dil = halves(di)
    kr = gr - ((nn(drh, cr) + nn(drl, cr)) - (nn(dih, ci) + nn(dil, ci)))
    ki = gi - ((nn(drh, ci) + nn(drl, ci)) + (nn(dih, cr) + nn(dil, cr)))
    krh, krl = halves(kr)
    kih, kil = halves(ki)
    for ref, a, b in ((khi_ref, krh, kih), (klo_ref, krl, kil)):
        ref[0:kmax, 0:kmax] = a
        ref[0:kmax, kmax:] = b
        ref[kmax:, 0:kmax] = -b
        ref[kmax:, kmax:] = a


def relay_body(in_ref, *rest):
    rest[-1][...] = in_ref[...]


def pair_body(a_ref, b_ref, dep_ref, out_ref):
    out_ref[0] = a_ref[...]
    out_ref[1] = b_ref[...]


def turned_fields(x_ref, start, n):
    re = x_ref[0, start : start + n]
    im = x_ref[1, start : start + n]
    return jnp.concatenate([re, -im], axis=1), jnp.concatenate([im, re], axis=1)


def send(x_ref, picked, q_ref, out_ref, start, n):
    q = q_ref[0:1, :]
    left, right = turned_fields(x_ref, start, n)
    w = jnp.concatenate([nt(left, picked) * q, nt(right, picked) * q], axis=1)
    pack(w, out_ref)


def first_body(part_ref, across_ref, beyond_ref, e0_ref, x_ref, q_ref, picked_ref, out_ref, side_ref, *, start, n, side_start):
    rows = across_ref.shape[1]
    picked = (nn(e0_ref[:, 2 * rows :], stacked(across_ref, beyond_ref)) + part_ref[...].astype(F32)).astype(BF)
    picked_ref[...] = picked
    q = q_ref[0:1, :]
    kmax = picked.shape[0]
    side_n = (side_ref.shape[0] - 16) * LANES // (2 * kmax)
    left, right = turned_fields(x_ref, start, n)
    more_left, more_right = turned_fields(x_ref, side_start, side_n)
    left = jnp.concatenate([left, more_left], axis=0)
    right = jnp.concatenate([right, more_right], axis=0)
    w = jnp.concatenate([nt(left, picked) * q, nt(right, picked) * q], axis=1)
    pack(w[:n], out_ref)
    pack(w[n:], side_ref, q_ref[1:2, :])


def rest_body(x_ref, picked_ref, q_ref, dep_ref, out_ref, *, start, n):
    send(x_ref, picked_ref[...], q_ref, out_ref, start, n)


def rows_body(x_ref, picked_ref, dep_ref, v_ref):
    kmax = picked_ref.shape[0]
    left, right = turned_fields(x_ref, 0, x_ref.shape[1])
    picked = picked_ref[...]
    v_ref[:, 0:kmax] = nt(left, picked)
    v_ref[:, kmax:] = nt(right, picked)


def ahead_body(x_ref, p0_ref, p1_ref, p2_ref, p3_ref, e1_ref, side_ref, q_ref, dep_ref, picked_ref, out_ref, *, start, n):
    half = out_ref.shape[0] // 2
    out_ref[0:half] = side_ref[...]
    picked = nn(e1_ref[...], stacked(p0_ref, p1_ref, p2_ref, p3_ref)).astype(BF)
    picked_ref[...] = picked
    left, right = turned_fields(x_ref, start, n)
    q = q_ref[1:2, :]
    w = jnp.concatenate([nt(left, picked) * q, nt(right, picked) * q], axis=1)
    pack(w, out_ref.at[half : 2 * half])


def onward_body(own_ref, got_ref, out_ref):
    half = own_ref.shape[0] // 2
    out_ref[0:half] = own_ref[0:half]
    out_ref[half:] = got_ref[0:half]


def pick(hi, lo, sel):
    k = sel.shape[0]
    parts = [nn(hi[:, i : i + k], sel) + nn(lo[:, i : i + k], sel) for i in (0, k)]
    return jnp.concatenate(parts, axis=1)


def around_body(*refs, start):
    (near_in_ref, mate_ref, ghi_ref, glo_ref, hhi_ref, hlo_ref, j_ref, jp_ref) = refs[:8]
    (v_ref, near_ref, far_ref, e0_ref, e1_ref, mc_ref, khi_ref, klo_ref, out_ref) = refs[8:]
    half = near_in_ref.shape[0] // 2
    n = out_ref.shape[1]
    k = j_ref.shape[0]
    lanes = mate_ref.shape[1]
    count = k // lanes
    mhi = khi_ref[...]
    mlo = klo_ref[...]
    t = apply_packed(near_in_ref.at[half : 2 * half], hhi_ref[...], hlo_ref[...])
    tail = mate_ref[half - 16 : half, :].astype(jnp.int32).astype(F32)
    upper = jnp.concatenate([tail[2 + i : 3 + i, :] for i in range(count)], axis=1)
    lower = jnp.concatenate([tail[2 + count + i : 3 + count + i, :] for i in range(count)], axis=1)
    q = (upper + lower * (1.0 / 32768.0)) * (1.0 / 16384.0)
    v, scale = unpack(mate_ref.at[half : 2 * half], 2 * k)
    w = v.astype(F32) * scale - pick(*halves(t), jp_ref[...]) * jnp.concatenate([q, q], axis=1)
    hi, lo = halves(w)
    p = nn(hi, mhi) + (nn(lo, mhi) + nn(hi, mlo))
    g = apply_packed(near_in_ref.at[0:half], ghi_ref[...], glo_ref[...])
    gh, gl = halves(g)
    u = v_ref[start : start + n, :] - pick(gh, gl, j_ref[...])
    uh, ul = halves(u)
    mc = mc_ref[...]
    p = p + (nn(uh, mc) + nn(ul, mc))
    ph, pl_ = halves(p)
    e0 = e0_ref[...]
    e1 = e1_ref[...]
    for i in range(2):
        cols = slice(i * k, i * k + k)
        y = jnp.concatenate([near_ref[i, start : start + n], far_ref[i, start : start + n]], axis=1)
        scattered = (nn(gh[:, cols], e0) + nn(gl[:, cols], e0)) + (nn(ph[:, cols], e1) + nn(pl_[:, cols], e1))
        out_ref[i] = y - scattered


def leaf_body(x_ref, p_ref, q_ref, dep_ref, y_ref):
    left, right = turned_fields(x_ref, 0, x_ref.shape[1])
    a = stacked(p_ref, q_ref)
    y_ref[0] = nt(left, a)
    y_ref[1] = nt(right, a)


def pack(w, out_ref, weight=None):
    n, both = w.shape
    lanes = out_ref.shape[1]
    most = jnp.max(jnp.abs(w), axis=1, keepdims=True)
    step = jnp.ceil(jnp.log2(jnp.maximum(most, 1e-30)) * STEPS)
    inv = TOP / jnp.exp2(step / STEPS)
    v = jnp.floor(w * inv + 0.5).astype(jnp.int32).astype(jnp.int16)
    for i in range(both // lanes):
        out_ref[i * n : (i + 1) * n, :] = v[:, i * lanes : (i + 1) * lanes]
    groups = -(-n // lanes)
    step = to_row(step, groups * lanes)
    tile = jnp.zeros((16, lanes), F32)
    for i in range(groups):
        tile = jnp.where(iota(tile.shape, 0) == i, step[:, i * lanes : (i + 1) * lanes], tile)
    if weight is not None:
        upper = jnp.floor(weight * 16384.0)
        lower = jnp.floor((weight * 16384.0 - upper) * 32768.0)
        count = weight.shape[1] // lanes
        for j, value in enumerate((upper, lower)):
            for i in range(count):
                at = iota(tile.shape, 0) == 2 + j * count + i
                tile = jnp.where(at, value[:, i * lanes : (i + 1) * lanes], tile)
    out_ref[both // lanes * n :, :] = tile.astype(jnp.int32).astype(jnp.int16)


def unpack(in_ref, k):
    lanes = in_ref.shape[1]
    pieces = k // lanes
    n = (in_ref.shape[0] - 16) // pieces
    groups = -(-n // lanes)
    steps = in_ref[pieces * n :, :].astype(jnp.int32).astype(F32)
    steps = jnp.concatenate([steps[i : i + 1, :] for i in range(groups)], axis=1)
    own = iota((n, groups * lanes), 0) == iota((n, groups * lanes), 1)
    step = jnp.sum(jnp.where(own, steps, 0.0), axis=1, keepdims=True)
    scale = jnp.exp2(step / STEPS) * (1.0 / TOP)
    v = jnp.concatenate([in_ref[i * n : (i + 1) * n, :] for i in range(pieces)], axis=1).astype(jnp.int32)
    return v, scale


def apply_packed(in_ref, mhi, mlo):
    v, scale = unpack(in_ref, mhi.shape[0])
    upper = (v + 128) & -256
    lower = (v - upper).astype(F32).astype(BF)
    upper = upper.astype(F32).astype(BF)
    return (nn(upper, mhi) + (nn(lower, mhi) + nn(upper, mlo))) * scale


def second_body(in_ref, ghi_ref, glo_ref, v_ref, j_ref, q_ref, *rest, start):
    out_ref, gs_ref, us_ref = rest[-3:]
    n = gs_ref.shape[1]
    k = j_ref.shape[0]
    g = apply_packed(in_ref, ghi_ref[...], glo_ref[...])
    hi, lo = halves(g)
    gs_ref[0] = hi
    gs_ref[1] = lo
    j = j_ref[...]
    q = q_ref[1:2, :]
    re = v_ref[start : start + n, :k] - (nn(hi[:, :k], j) + nn(lo[:, :k], j))
    im = v_ref[start : start + n, k:] - (nn(hi[:, k:], j) + nn(lo[:, k:], j))
    u = jnp.concatenate([re, im], axis=1)
    pack(u * jnp.concatenate([q, q], axis=1), out_ref)
    hi, lo = halves(u)
    us_ref[0] = hi
    us_ref[1] = lo


def third_body(gs_ref, us_ref, near_ref, far_ref, e0_ref, mc_ref, dep_ref, part_ref, p_ref, *, start):
    n = gs_ref.shape[1]
    k = e0_ref.shape[0]
    e = e0_ref[...]
    for i in range(2):
        cols = slice(i * k, i * k + k)
        y = jnp.concatenate([near_ref[i, start : start + n], far_ref[i, start : start + n]], axis=1)
        part_ref[i] = y - (nn(gs_ref[0, :, cols], e) + nn(gs_ref[1, :, cols], e))
    mc = mc_ref[...]
    p_ref[...] = nn(us_ref[0], mc) + nn(us_ref[1], mc)


def finish(in_ref, part_ref, p_ref, khi, klo, e):
    k = e.shape[0]
    p = p_ref[...] + apply_packed(in_ref, khi, klo)
    hi, lo = halves(p)
    for i in range(2):
        cols = slice(i * k, i * k + k)
        yield i, part_ref[i] - (nn(hi[:, cols], e) + nn(lo[:, cols], e))


def writer(out_ref, sem, blocks):
    me = lax.axis_index("field")
    copies = []

    def write(src_ref, i, row):
        n = src_ref.shape[2] // blocks
        for m in range(blocks):
            col = pl.multiple_of((me ^ m) * n, n)
            copy = pltpu.make_async_copy(
                src_ref.at[i, :, pl.ds(m * n, n)],
                out_ref.at[i, pl.ds(row, src_ref.shape[1]), pl.ds(col, n)],
                sem.at[len(copies)],
            )
            copy.start()
            copies.append(copy)

    return write, copies


def last_body(khi_ref, klo_ref, e1_ref, in_ref, part_ref, p_ref, *rest, start, blocks, done_at):
    out_ref, hold_ref, sem = rest[-3:]
    write, copies = writer(out_ref, sem, blocks)
    if done_at is not None:
        for i in range(2):
            write(rest[0], i, done_at)
    for i, value in finish(in_ref, part_ref, p_ref, khi_ref[...], klo_ref[...], e1_ref[...]):
        hold_ref[i] = value
        write(hold_ref, i, start)
    for copy in copies:
        copy.wait()


def body(incident, leaf_inverse, contrast, skel_index, ranks, top_core):
    nf, width = incident.shape[1:]
    boxes, _, kmax = skel_index.shape
    quarter = top_core.shape[2]
    own = leaf_inverse[0]
    across = swap(own, "field", 2)
    beside = swap(own, "field", 1)
    core_own = jnp.swapaxes(top_core, 1, 2).reshape(2 * quarter, kmax)
    core_near = swap(core_own, "box", 1)
    n = n_rows = own.shape[1]
    (opened,) = call(open_body, "open", [shape(8, 128)], [], cost=4.0)
    e0, e1, q, ghi, glo, g1, dup01, dup11, part, hhi, hlo, dupm = call(
        lambda *refs: plan_body(*refs, parts=lax.axis_size("field")),
        "plan",
        [
            shape(kmax, width, dtype=BF),
            shape(kmax, width, dtype=BF),
            shape(8, kmax),
            shape(2 * kmax, 2 * kmax, dtype=BF),
            shape(2 * kmax, 2 * kmax, dtype=BF),
            shape(kmax, 2 * kmax),
            shape(kmax, kmax, dtype=BF),
            shape(kmax, kmax, dtype=BF),
            shape(kmax, 2 * width, dtype=BF),
            shape(2 * kmax, 2 * kmax, dtype=BF),
            shape(2 * kmax, 2 * kmax, dtype=BF),
            shape(kmax, kmax, dtype=BF),
        ],
        [ranks.T, skel_index, contrast.reshape(1, width), own, beside, opened],
        [VMEM] * 5 + [ANY],
    )
    x = incident
    (near,) = call(
        leaf_body, "near", [shape(2, nf, 2 * n)], [x, own, beside, part], [VMEM] * 3 + [ANY], cost=0.7
    )
    (pair,) = call(
        pair_body, "pair", [shape(2, 2 * quarter, kmax, dtype=BF)], [core_own, core_near, near], [VMEM, VMEM, ANY], cost=0.05
    )
    core_far = swap(pair, "box", 2)
    (across,) = call(
        relay_body, "relay", [shape(*across.shape, dtype=BF)], [across, pair, near], [VMEM, ANY, ANY], cost=0.05
    )
    beyond = swap(across, "field", 1)
    chunks = [nf // sum(SHARES) * share for share in SHARES]
    sizes = [(sum(chunks[:i]), n) for i, n in enumerate(chunks)]
    start, n = sizes[0]
    side_start, side_n = sizes[2]
    picked, head, side = call(
        lambda *refs, start=start, n=n: first_body(*refs, start=start, n=n, side_start=side_start),
        "first",
        [
            shape(kmax, 2 * width, dtype=BF),
            packed_shape(n, kmax),
            packed_shape(side_n, kmax),
        ],
        [part, across, beyond, e0, x, q],
        cost=0.8,
    )

    got = swap(head, "box", 1)
    picked1, ahead = call(
        lambda *refs: ahead_body(*refs, start=side_start, n=side_n),
        "ahead",
        [shape(kmax, 2 * width, dtype=BF), shape(2 * packed_shape(side_n, kmax).shape[0], LANES, dtype=jnp.int16)],
        [x, own, beside, across, beyond, e1, side, q, e0],
        [VMEM] * 8 + [ANY],
        cost=1.4,
    )
    mate = swap(ahead, "box", 2)
    start, n = sizes[1]
    (packed,) = call(
        lambda *refs: rest_body(*refs, start=start, n=n),
        "ready",
        [packed_shape(n, kmax)],
        [x, picked, q, ahead],
        [VMEM] * 3 + [ANY],
        cost=0.6,
    )
    coming = swap(packed, "box", 1)
    (v1,) = call(rows_body, "rows", [shape(nf, 2 * kmax)], [x, picked1, packed], [VMEM] * 2 + [ANY])
    mc, khi, klo = call(
        core_body,
        "core",
        [shape(2 * kmax, 2 * kmax, dtype=BF)] * 3,
        [core_own, core_near, core_far, g1, dup11, v1],
        [VMEM] * 5 + [ANY],
        [pltpu.VMEM((kmax, 2 * kmax), BF)],
    )
    (far,) = call(
        leaf_body, "leaf", [shape(2, nf, 2 * n_rows)], [x, across, beyond, mc], [VMEM] * 3 + [ANY], cost=0.7
    )
    late = []
    for i, (start, n) in enumerate(sizes[:2]):
        back, gs, us = call(
            lambda *refs, start=start: second_body(*refs, start=start),
            f"second{i}",
            [packed_shape(n, kmax), shape(2, n, 2 * kmax, dtype=BF), shape(2, n, 2 * kmax, dtype=BF)],
            [got, ghi, glo, v1, dup01, q, sent if i else far],
            [VMEM] * 6 + [ANY],
            cost=0.8,
        )
        got = coming
        late.append([swap(back, "box", 2), gs, us])
        if i == 0:
            (onward,) = call(onward_body, "onward", [shape(*ahead.shape, dtype=jnp.int16)], [ahead, mate], cost=0.05)
            sent = onward
            onward = swap(onward, "box", 1)
    for i, (start, n) in enumerate(sizes[:2]):
        late[i][1:] = call(
            lambda *refs, start=start: third_body(*refs, start=start),
            f"third{i}",
            [shape(2, n, width), shape(n, 2 * kmax)],
            [late[i][1], late[i][2], near, far, e0, mc, gs],
            [VMEM] * 6 + [ANY],
            cost=0.5,
        )
    side = call(
        lambda *refs: around_body(*refs, start=side_start),
        "around",
        [shape(2, side_n, width)],
        [onward, mate, ghi, glo, hhi, hlo, dup01, dupm, v1, near, far, e0, e1, mc, khi, klo],
        cost=2.5,
    )
    blocks = lax.axis_size("field")
    out = []
    for i, (start, n) in enumerate(sizes[:2]):
        ready = side if i == 1 else []
        out = call(
            lambda *refs, start=start, ready=ready: last_body(
                *refs, start=start, blocks=blocks, done_at=side_start if ready else None
            ),
            f"last{i}",
            [shape(2, nf, width)],
            [khi, klo, e1] + late[i] + ready + out,
            [VMEM] * (6 + len(ready)) + [ANY] * len(out),
            [pltpu.VMEM((2, n, width), F32), pltpu.SemaphoreType.DMA(((4 if ready else 2) * blocks,))],
            out_specs=[ANY],
            input_output_aliases={6 + len(ready): 0} if out else {},
        )
    return out[0]


def solution(mesh):
    return jax.shard_map(
        body,
        mesh=mesh,
        in_specs=(P(None, "field", "box"), P("box", None, "field", None), P("box"), P(), P(), P(None, None, "box")),
        out_specs=P(None, "field", "box"),
        check_vma=False,
    )
```

```python
import jax
import jax.numpy as jnp
from jax import lax
from jax.experimental import pallas as pl
from jax.experimental.pallas import tpu as pltpu
from jax.sharding import PartitionSpec as P

SIDE = 8
WAVENUM = 0.7
BF = jnp.bfloat16
F32 = jnp.float32
SHARES = (12, 13, 7)
TOP = 32766.0
STEPS = 128.0
LANES = 128
VMEM = pl.BlockSpec(memory_space=pltpu.VMEM)
SMEM = pl.BlockSpec(memory_space=pltpu.SMEM)
ANY = pl.BlockSpec(memory_space=pl.ANY)
PARAMS = pltpu.CompilerParams(vmem_limit_bytes=40 * 1024 * 1024)


def swap(value, axis, mask):
    return lax.ppermute(value, axis, [(s, s ^ mask) for s in range(lax.axis_size(axis))])


def call(body, name, outs, ins, specs=None, scratch=(), cost=1.0, **kw):
    return list(
        pl.pallas_call(
        body,
        name=name,
        out_shape=outs,
        in_specs=specs or [VMEM] * len(ins),
        out_specs=kw.pop("out_specs", [VMEM] * len(outs)),
        scratch_shapes=list(scratch),
        compiler_params=PARAMS,
        cost_estimate=pl.CostEstimate(flops=int(cost * 1e9), bytes_accessed=int(cost * 3e6), transcendentals=0),
        **kw,
    )(*ins)
    )


def shape(*dims, dtype=F32):
    return jax.ShapeDtypeStruct(dims, dtype)


def packed_shape(n, kmax):
    return shape(2 * n * kmax // LANES + 16, LANES, dtype=jnp.int16)


def nn(a, b):
    return lax.dot_general(a, b, (((1,), (0,)), ((), ())), preferred_element_type=F32)


def nt(a, b):
    return lax.dot_general(a, b, (((1,), (1,)), ((), ())), preferred_element_type=F32)


def halves(v):
    hi = v.astype(BF)
    return hi, (v - hi.astype(F32)).astype(BF)


def iota(dims, axis):
    return lax.broadcasted_iota(jnp.int32, dims, axis)


def to_column(row):
    n = row.shape[1]
    return jnp.sum(jnp.where(iota((n, n), 0) == iota((n, n), 1), row, 0.0), axis=1, keepdims=True)


def to_row(col, width):
    n = col.shape[0]
    return jnp.sum(jnp.where(iota((n, width), 0) == iota((n, width), 1), col, 0.0), axis=0, keepdims=True)


def cos_sin(angle):
    turns = jnp.floor(angle * 0.6366197723675814 + 0.5)
    t = angle - turns * 1.5707855224609375
    t = t - turns * 1.0804334124e-05
    t2 = t * t
    c = 1.0 + t2 * (-0.5 + t2 * (4.1666667e-2 + t2 * (-1.3888889e-3 + t2 * 2.4801587e-5)))
    s = t * (1.0 + t2 * (-1.6666667e-1 + t2 * (8.3333333e-3 + t2 * (-1.9841270e-4 + t2 * 2.7557319e-6))))
    quad = turns.astype(jnp.int32) & 3
    odd = (quad & 1) == 1
    cc = jnp.where(odd, s, c)
    ss = jnp.where(odd, c, s)
    cc = jnp.where((quad == 1) | (quad == 2), -cc, cc)
    ss = jnp.where(quad >= 2, -ss, ss)
    return cc, ss


def place(index, box):
    return (
        (index & (SIDE - 1)).astype(F32) + (box * SIDE).astype(F32),
        ((index >> 3) & (SIDE - 1)).astype(F32),
        (index >> 6).astype(F32),
    )


def stacked(*refs):
    return jnp.concatenate([jnp.concatenate([ref[0], ref[1]], axis=1) for ref in refs], axis=0)


def open_body(out_ref):
    out_ref[...] = jnp.zeros(out_ref.shape, out_ref.dtype)


def green(own_row, own_box, far_col, far_box):
    ox, oy, oz = place(own_row, own_box)
    fx, fy, fz = place(far_col, far_box)
    d2 = (fx - ox) * (fx - ox) + (fy - oy) * (fy - oy) + (fz - oz) * (fz - oz)
    dist = jnp.sqrt(d2)
    inv = 1.0 / dist
    c, s = cos_sin(WAVENUM * dist)
    return c * inv, s * inv


def store_complex(ref, re, im):
    k = re.shape[0]
    ref[0:k, 0:k] = re
    ref[0:k, k:] = im
    ref[k:, 0:k] = -im
    ref[k:, k:] = re


def store_halves(hi_ref, lo_ref, re, im):
    rhi, rlo = halves(re)
    ihi, ilo = halves(im)
    store_complex(hi_ref, rhi, ihi)
    store_complex(lo_ref, rlo, ilo)


def matches(col, rank_col, row, rank_row):
    k = col.shape[0]
    hit = (col == row) & (iota((k, k), 0) < rank_col) & (iota((k, k), 1) < rank_row)
    return hit.astype(F32).astype(BF)


def plan_body(ranks_ref, skel_ref, contrast_ref, own_ref, beside_ref, dep_ref, *refs, parts):
    e0_ref, e1_ref, q_ref, ghi_ref, glo_ref, g1_ref, j_ref, d_ref, part_ref, part1_ref, hhi_ref, hlo_ref, jp_ref = refs
    box = lax.axis_index("box")
    me = lax.axis_index("field")
    kmax = skel_ref.shape[2]
    width = contrast_ref.shape[1]
    contrast = contrast_ref[...]
    all_ranks = ranks_ref[...].astype(F32)

    def ranks_of(at):
        mine = jnp.where(iota(all_ranks.shape, 1) == at, all_ranks, 0.0)
        return jnp.sum(mine, axis=1, keepdims=True).astype(jnp.int32)

    def row_of(at, level):
        return skel_ref[at][level : level + 1, :]

    def col_of(at, level):
        return to_column(row_of(at, level).astype(F32)).astype(jnp.int32)

    ranks = ranks_of(box)
    n = width // parts
    lane = iota((kmax, width), 1)
    turned = (((lane // n) ^ me) * n) + lane % n
    cols = []
    for level in range(2):
        far = box ^ (1 << level)
        own_col = col_of(box, level)
        r = ranks[level : level + 1, :]
        cols.append(own_col)
        hit = (own_col == turned) & (iota((kmax, width), 0) < r)
        (e0_ref, e1_ref)[level][...] = hit.astype(F32).astype(BF)
        true_hit = (own_col == iota((kmax, width), 1)) & (iota((kmax, width), 0) < r)
        q_col = jnp.sum(jnp.where(true_hit, contrast, 0.0), axis=1, keepdims=True)
        q_ref[pl.ds(level, 1), :] = to_row(q_col, kmax)
        c, s = green(row_of(box, level), box, col_of(far, level), far)
        if level == 0:
            store_halves(ghi_ref, glo_ref, c, s)
        else:
            g1_ref[:, 0:kmax] = c
            g1_ref[:, kmax:] = s
    j_ref[...] = matches(cols[0], ranks[0:1, :], row_of(box, 1), ranks[1:2, :])
    d_ref[...] = matches(cols[1], ranks[1:2, :], row_of(box, 1), ranks[1:2, :])
    near_rows = stacked(own_ref, beside_ref)
    part_ref[...] = nn(e0_ref[:, : 2 * n], near_rows).astype(BF)
    part1_ref[...] = nn(e1_ref[:, : 2 * n], near_rows).astype(BF)
    mate = box ^ 2
    mate_ranks = ranks_of(mate)
    c, s = green(row_of(mate, 0), mate, col_of(box ^ 3, 0), box ^ 3)
    store_halves(hhi_ref, hlo_ref, c, s)
    jp_ref[...] = matches(col_of(mate, 0), mate_ranks[0:1, :], row_of(mate, 1), mate_ranks[1:2, :])


def core_body(own_ref, near_ref, far_ref, g1_ref, d_ref, dep_ref, mc_ref, khi_ref, klo_ref, ct_ref):
    slot = lax.axis_index("box") & 3
    quarter = own_ref.shape[0] // 2
    kmax = own_ref.shape[1]
    pieces = (own_ref[...], near_ref[...], far_ref[0], far_ref[1])
    for mask, piece in enumerate(pieces):
        start = pl.multiple_of((slot ^ mask) * quarter, quarter)
        ct_ref[pl.ds(start, quarter), 0:kmax] = piece[:quarter]
        ct_ref[pl.ds(start, quarter), kmax:] = piece[quarter:]
    cr = ct_ref[:, 0:kmax]
    ci = ct_ref[:, kmax:]
    mc_ref[0:kmax, 0:kmax] = cr
    mc_ref[0:kmax, kmax:] = ci
    mc_ref[kmax:, 0:kmax] = -ci
    mc_ref[kmax:, kmax:] = cr
    dup = d_ref[...]
    gr = g1_ref[:, 0:kmax]
    gi = g1_ref[:, kmax:]
    grh, grl = halves(gr)
    gih, gil = halves(gi)
    dr = nn(grh, dup) + nn(grl, dup)
    di = nn(gih, dup) + nn(gil, dup)
    drh, drl = halves(dr)
    dih, dil = halves(di)
    kr = gr - ((nn(drh, cr) + nn(drl, cr)) - (nn(dih, ci) + nn(dil, ci)))
    ki = gi - ((nn(drh, ci) + nn(drl, ci)) + (nn(dih, cr) + nn(dil, cr)))
    krh, krl = halves(kr)
    kih, kil = halves(ki)
    for ref, a, b in ((khi_ref, krh, kih), (klo_ref, krl, kil)):
        ref[0:kmax, 0:kmax] = a
        ref[0:kmax, kmax:] = b
        ref[kmax:, 0:kmax] = -b
        ref[kmax:, kmax:] = a


def relay_body(in_ref, *rest):
    rest[-1][...] = in_ref[...]


def pair_body(a_ref, b_ref, dep_ref, out_ref):
    out_ref[0] = a_ref[...]
    out_ref[1] = b_ref[...]


def turned_fields(x_ref, start, n):
    re = x_ref[0, start : start + n]
    im = x_ref[1, start : start + n]
    return jnp.concatenate([re, -im], axis=1), jnp.concatenate([im, re], axis=1)


def send(x_ref, picked, q_ref, out_ref, start, n):
    q = q_ref[0:1, :]
    left, right = turned_fields(x_ref, start, n)
    w = jnp.concatenate([nt(left, picked) * q, nt(right, picked) * q], axis=1)
    pack(w, out_ref)


def first_body(part_ref, across_ref, beyond_ref, e0_ref, x_ref, q_ref, picked_ref, out_ref, side_ref, *, start, n, side_start):
    rows = across_ref.shape[1]
    picked = (nn(e0_ref[:, 2 * rows :], stacked(across_ref, beyond_ref)) + part_ref[...].astype(F32)).astype(BF)
    picked_ref[...] = picked
    q = q_ref[0:1, :]
    kmax = picked.shape[0]
    side_n = (side_ref.shape[0] - 16) * LANES // (2 * kmax)
    left, right = turned_fields(x_ref, start, n)
    more_left, more_right = turned_fields(x_ref, side_start, side_n)
    left = jnp.concatenate([left, more_left], axis=0)
    right = jnp.concatenate([right, more_right], axis=0)
    w = jnp.concatenate([nt(left, picked) * q, nt(right, picked) * q], axis=1)
    pack(w[:n], out_ref)
    pack(w[n:], side_ref, q_ref[1:2, :])


def rest_body(x_ref, picked_ref, q_ref, dep_ref, out_ref, *, start, n):
    send(x_ref, picked_ref[...], q_ref, out_ref, start, n)


def rows_body(x_ref, picked_ref, dep_ref, v_ref):
    kmax = picked_ref.shape[0]
    left, right = turned_fields(x_ref, 0, x_ref.shape[1])
    picked = picked_ref[...]
    v_ref[:, 0:kmax] = nt(left, picked)
    v_ref[:, kmax:] = nt(right, picked)


def ahead_body(x_ref, part_ref, across_ref, beyond_ref, e1_ref, side_ref, q_ref, dep_ref, picked_ref, out_ref, *, start, n):
    half = out_ref.shape[0] // 2
    out_ref[0:half] = side_ref[...]
    rows = across_ref.shape[1]
    picked = (nn(e1_ref[:, 2 * rows :], stacked(across_ref, beyond_ref)) + part_ref[...].astype(F32)).astype(BF)
    picked_ref[...] = picked
    left, right = turned_fields(x_ref, start, n)
    q = q_ref[1:2, :]
    w = jnp.concatenate([nt(left, picked) * q, nt(right, picked) * q], axis=1)
    pack(w, out_ref.at[half : 2 * half])


def onward_body(own_ref, got_ref, out_ref):
    half = own_ref.shape[0] // 2
    out_ref[0:half] = own_ref[0:half]
    out_ref[half:] = got_ref[0:half]


def pick(hi, lo, sel):
    k = sel.shape[0]
    parts = [nn(hi[:, i : i + k], sel) + nn(lo[:, i : i + k], sel) for i in (0, k)]
    return jnp.concatenate(parts, axis=1)


def around_body(*refs, start):
    (near_in_ref, mate_ref, ghi_ref, glo_ref, hhi_ref, hlo_ref, j_ref, jp_ref) = refs[:8]
    (v_ref, near_ref, far_ref, e0_ref, e1_ref, mc_ref, khi_ref, klo_ref, out_ref) = refs[8:]
    half = near_in_ref.shape[0] // 2
    n = out_ref.shape[1]
    k = j_ref.shape[0]
    lanes = mate_ref.shape[1]
    count = k // lanes
    mhi = khi_ref[...]
    mlo = klo_ref[...]
    t = apply_packed(near_in_ref.at[half : 2 * half], hhi_ref[...], hlo_ref[...])
    tail = mate_ref[half - 16 : half, :].astype(jnp.int32).astype(F32)
    upper = jnp.concatenate([tail[2 + i : 3 + i, :] for i in range(count)], axis=1)
    lower = jnp.concatenate([tail[2 + count + i : 3 + count + i, :] for i in range(count)], axis=1)
    q = (upper + lower * (1.0 / 32768.0)) * (1.0 / 16384.0)
    v, scale = unpack(mate_ref.at[half : 2 * half], 2 * k)
    w = v.astype(F32) * scale - pick(*halves(t), jp_ref[...]) * jnp.concatenate([q, q], axis=1)
    hi, lo = halves(w)
    p = nn(hi, mhi) + (nn(lo, mhi) + nn(hi, mlo))
    g = apply_packed(near_in_ref.at[0:half], ghi_ref[...], glo_ref[...])
    gh, gl = halves(g)
    u = v_ref[start : start + n, :] - pick(gh, gl, j_ref[...])
    uh, ul = halves(u)
    mc = mc_ref[...]
    p = p + (nn(uh, mc) + nn(ul, mc))
    ph, pl_ = halves(p)
    e0 = e0_ref[...]
    e1 = e1_ref[...]
    for i in range(2):
        cols = slice(i * k, i * k + k)
        y = jnp.concatenate([near_ref[i, start : start + n], far_ref[i, start : start + n]], axis=1)
        scattered = (nn(gh[:, cols], e0) + nn(gl[:, cols], e0)) + (nn(ph[:, cols], e1) + nn(pl_[:, cols], e1))
        out_ref[i] = y - scattered


def leaf_body(x_ref, p_ref, q_ref, dep_ref, y_ref):
    left, right = turned_fields(x_ref, 0, x_ref.shape[1])
    a = stacked(p_ref, q_ref)
    y_ref[0] = nt(left, a)
    y_ref[1] = nt(right, a)


def pack(w, out_ref, weight=None):
    n, both = w.shape
    lanes = out_ref.shape[1]
    most = jnp.max(jnp.abs(w), axis=1, keepdims=True)
    step = jnp.ceil(jnp.log2(jnp.maximum(most, 1e-30)) * STEPS)
    inv = TOP / jnp.exp2(step / STEPS)
    v = jnp.floor(w * inv + 0.5).astype(jnp.int32).astype(jnp.int16)
    for i in range(both // lanes):
        out_ref[i * n : (i + 1) * n, :] = v[:, i * lanes : (i + 1) * lanes]
    groups = -(-n // lanes)
    step = to_row(step, groups * lanes)
    tile = jnp.zeros((16, lanes), F32)
    for i in range(groups):
        tile = jnp.where(iota(tile.shape, 0) == i, step[:, i * lanes : (i + 1) * lanes], tile)
    if weight is not None:
        upper = jnp.floor(weight * 16384.0)
        lower = jnp.floor((weight * 16384.0 - upper) * 32768.0)
        count = weight.shape[1] // lanes
        for j, value in enumerate((upper, lower)):
            for i in range(count):
                at = iota(tile.shape, 0) == 2 + j * count + i
                tile = jnp.where(at, value[:, i * lanes : (i + 1) * lanes], tile)
    out_ref[both // lanes * n :, :] = tile.astype(jnp.int32).astype(jnp.int16)


def unpack(in_ref, k):
    lanes = in_ref.shape[1]
    pieces = k // lanes
    n = (in_ref.shape[0] - 16) // pieces
    groups = -(-n // lanes)
    steps = in_ref[pieces * n :, :].astype(jnp.int32).astype(F32)
    steps = jnp.concatenate([steps[i : i + 1, :] for i in range(groups)], axis=1)
    own = iota((n, groups * lanes), 0) == iota((n, groups * lanes), 1)
    step = jnp.sum(jnp.where(own, steps, 0.0), axis=1, keepdims=True)
    scale = jnp.exp2(step / STEPS) * (1.0 / TOP)
    v = jnp.concatenate([in_ref[i * n : (i + 1) * n, :] for i in range(pieces)], axis=1).astype(jnp.int32)
    return v, scale


def apply_packed(in_ref, mhi, mlo):
    v, scale = unpack(in_ref, mhi.shape[0])
    upper = (v + 128) & -256
    lower = (v - upper).astype(F32).astype(BF)
    upper = upper.astype(F32).astype(BF)
    return (nn(upper, mhi) + (nn(lower, mhi) + nn(upper, mlo))) * scale


def second_body(in_ref, ghi_ref, glo_ref, v_ref, j_ref, q_ref, *rest, start):
    out_ref, gs_ref, us_ref = rest[-3:]
    n = gs_ref.shape[1]
    k = j_ref.shape[0]
    g = apply_packed(in_ref, ghi_ref[...], glo_ref[...])
    hi, lo = halves(g)
    gs_ref[0] = hi
    gs_ref[1] = lo
    j = j_ref[...]
    q = q_ref[1:2, :]
    re = v_ref[start : start + n, :k] - (nn(hi[:, :k], j) + nn(lo[:, :k], j))
    im = v_ref[start : start + n, k:] - (nn(hi[:, k:], j) + nn(lo[:, k:], j))
    u = jnp.concatenate([re, im], axis=1)
    pack(u * jnp.concatenate([q, q], axis=1), out_ref)
    hi, lo = halves(u)
    us_ref[0] = hi
    us_ref[1] = lo


def third_body(gs_ref, us_ref, near_ref, far_ref, e0_ref, mc_ref, dep_ref, part_ref, p_ref, *, start):
    n = gs_ref.shape[1]
    k = e0_ref.shape[0]
    e = e0_ref[...]
    for i in range(2):
        cols = slice(i * k, i * k + k)
        y = jnp.concatenate([near_ref[i, start : start + n], far_ref[i, start : start + n]], axis=1)
        part_ref[i] = y - (nn(gs_ref[0, :, cols], e) + nn(gs_ref[1, :, cols], e))
    mc = mc_ref[...]
    p_ref[...] = nn(us_ref[0], mc) + nn(us_ref[1], mc)


def finish(in_ref, part_ref, p_ref, khi, klo, e):
    k = e.shape[0]
    p = p_ref[...] + apply_packed(in_ref, khi, klo)
    hi, lo = halves(p)
    for i in range(2):
        cols = slice(i * k, i * k + k)
        yield i, part_ref[i] - (nn(hi[:, cols], e) + nn(lo[:, cols], e))


def writer(out_ref, sem, blocks):
    me = lax.axis_index("field")
    copies = []

    def write(src_ref, i, row):
        n = src_ref.shape[2] // blocks
        for m in range(blocks):
            col = pl.multiple_of((me ^ m) * n, n)
            copy = pltpu.make_async_copy(
                src_ref.at[i, :, pl.ds(m * n, n)],
                out_ref.at[i, pl.ds(row, src_ref.shape[1]), pl.ds(col, n)],
                sem.at[len(copies)],
            )
            copy.start()
            copies.append(copy)

    return write, copies


def last_body(khi_ref, klo_ref, e1_ref, in_ref, part_ref, p_ref, *rest, start, blocks, done_at):
    out_ref, hold_ref, sem = rest[-3:]
    write, copies = writer(out_ref, sem, blocks)
    if done_at is not None:
        for i in range(2):
            write(rest[0], i, done_at)
    for i, value in finish(in_ref, part_ref, p_ref, khi_ref[...], klo_ref[...], e1_ref[...]):
        hold_ref[i] = value
        write(hold_ref, i, start)
    for copy in copies:
        copy.wait()


def body(incident, leaf_inverse, contrast, skel_index, ranks, top_core):
    nf, width = incident.shape[1:]
    boxes, _, kmax = skel_index.shape
    quarter = top_core.shape[2]
    own = leaf_inverse[0]
    across = swap(own, "field", 2)
    beside = swap(own, "field", 1)
    core_own = jnp.swapaxes(top_core, 1, 2).reshape(2 * quarter, kmax)
    core_near = swap(core_own, "box", 1)
    n = n_rows = own.shape[1]
    (opened,) = call(open_body, "open", [shape(8, 128)], [], cost=4.0)
    e0, e1, q, ghi, glo, g1, dup01, dup11, part, part1, hhi, hlo, dupm = call(
        lambda *refs: plan_body(*refs, parts=lax.axis_size("field")),
        "plan",
        [
            shape(kmax, width, dtype=BF),
            shape(kmax, width, dtype=BF),
            shape(8, kmax),
            shape(2 * kmax, 2 * kmax, dtype=BF),
            shape(2 * kmax, 2 * kmax, dtype=BF),
            shape(kmax, 2 * kmax),
            shape(kmax, kmax, dtype=BF),
            shape(kmax, kmax, dtype=BF),
            shape(kmax, 2 * width, dtype=BF),
            shape(kmax, 2 * width, dtype=BF),
            shape(2 * kmax, 2 * kmax, dtype=BF),
            shape(2 * kmax, 2 * kmax, dtype=BF),
            shape(kmax, kmax, dtype=BF),
        ],
        [ranks.T, skel_index, contrast.reshape(1, width), own, beside, opened],
        [VMEM] * 5 + [ANY],
    )
    x = incident
    (near,) = call(
        leaf_body, "near", [shape(2, nf, 2 * n)], [x, own, beside, part], [VMEM] * 3 + [ANY], cost=0.7
    )
    (pair,) = call(
        pair_body, "pair", [shape(2, 2 * quarter, kmax, dtype=BF)], [core_own, core_near, near], [VMEM, VMEM, ANY], cost=0.05
    )
    core_far = swap(pair, "box", 2)
    (across,) = call(
        relay_body, "relay", [shape(*across.shape, dtype=BF)], [across, pair, near], [VMEM, ANY, ANY], cost=0.05
    )
    beyond = swap(across, "field", 1)
    chunks = [nf // sum(SHARES) * share for share in SHARES]
    sizes = [(sum(chunks[:i]), n) for i, n in enumerate(chunks)]
    start, n = sizes[0]
    side_start, side_n = sizes[2]
    picked, head, side = call(
        lambda *refs, start=start, n=n: first_body(*refs, start=start, n=n, side_start=side_start),
        "first",
        [
            shape(kmax, 2 * width, dtype=BF),
            packed_shape(n, kmax),
            packed_shape(side_n, kmax),
        ],
        [part, across, beyond, e0, x, q],
        cost=0.8,
    )

    got = swap(head, "box", 1)
    picked1, ahead = call(
        lambda *refs: ahead_body(*refs, start=side_start, n=side_n),
        "ahead",
        [shape(kmax, 2 * width, dtype=BF), shape(2 * packed_shape(side_n, kmax).shape[0], LANES, dtype=jnp.int16)],
        [x, part1, across, beyond, e1, side, q, e0],
        [VMEM] * 7 + [ANY],
        cost=1.4,
    )
    mate = swap(ahead, "box", 2)
    start, n = sizes[1]
    (packed,) = call(
        lambda *refs: rest_body(*refs, start=start, n=n),
        "ready",
        [packed_shape(n, kmax)],
        [x, picked, q, ahead],
        [VMEM] * 3 + [ANY],
        cost=0.6,
    )
    coming = swap(packed, "box", 1)
    (v1,) = call(rows_body, "rows", [shape(nf, 2 * kmax)], [x, picked1, packed], [VMEM] * 2 + [ANY])
    mc, khi, klo = call(
        core_body,
        "core",
        [shape(2 * kmax, 2 * kmax, dtype=BF)] * 3,
        [core_own, core_near, core_far, g1, dup11, v1],
        [VMEM] * 5 + [ANY],
        [pltpu.VMEM((kmax, 2 * kmax), BF)],
    )
    (far,) = call(
        leaf_body, "leaf", [shape(2, nf, 2 * n_rows)], [x, across, beyond, mc], [VMEM] * 3 + [ANY], cost=0.7
    )
    late = []
    for i, (start, n) in enumerate(sizes[:2]):
        back, gs, us = call(
            lambda *refs, start=start: second_body(*refs, start=start),
            f"second{i}",
            [packed_shape(n, kmax), shape(2, n, 2 * kmax, dtype=BF), shape(2, n, 2 * kmax, dtype=BF)],
            [got, ghi, glo, v1, dup01, q, sent if i else far],
            [VMEM] * 6 + [ANY],
            cost=0.8,
        )
        got = coming
        late.append([swap(back, "box", 2), gs, us])
        if i == 0:
            (onward,) = call(onward_body, "onward", [shape(*ahead.shape, dtype=jnp.int16)], [ahead, mate], cost=0.05)
            sent = onward
            onward = swap(onward, "box", 1)
    for i, (start, n) in enumerate(sizes[:2]):
        late[i][1:] = call(
            lambda *refs, start=start: third_body(*refs, start=start),
            f"third{i}",
            [shape(2, n, width), shape(n, 2 * kmax)],
            [late[i][1], late[i][2], near, far, e0, mc, gs],
            [VMEM] * 6 + [ANY],
            cost=0.5,
        )
    side = call(
        lambda *refs: around_body(*refs, start=side_start),
        "around",
        [shape(2, side_n, width)],
        [onward, mate, ghi, glo, hhi, hlo, dup01, dupm, v1, near, far, e0, e1, mc, khi, klo],
        cost=2.5,
    )
    blocks = lax.axis_size("field")
    out = []
    for i, (start, n) in enumerate(sizes[:2]):
        ready = side if i == 1 else []
        out = call(
            lambda *refs, start=start, ready=ready: last_body(
                *refs, start=start, blocks=blocks, done_at=side_start if ready else None
            ),
            f"last{i}",
            [shape(2, nf, width)],
            [khi, klo, e1] + late[i] + ready + out,
            [VMEM] * (6 + len(ready)) + [ANY] * len(out),
            [pltpu.VMEM((2, n, width), F32), pltpu.SemaphoreType.DMA(((4 if ready else 2) * blocks,))],
            out_specs=[ANY],
            input_output_aliases={6 + len(ready): 0} if out else {},
        )
    return out[0]


def solution(mesh):
    return jax.shard_map(
        body,
        mesh=mesh,
        in_specs=(P(None, "field", "box"), P("box", None, "field", None), P("box"), P(), P(), P(None, None, "box")),
        out_specs=P(None, "field", "box"),
        check_vma=False,
    )
```

```python
import jax
import jax.numpy as jnp
from jax import lax
from jax.experimental import pallas as pl
from jax.experimental.pallas import tpu as pltpu
from jax.sharding import PartitionSpec as P

SIDE = 8
WAVENUM = 0.7
BF = jnp.bfloat16
F32 = jnp.float32
SHARES = (12, 13, 7)
TOP = 32766.0
STEPS = 128.0
LANES = 128
VMEM = pl.BlockSpec(memory_space=pltpu.VMEM)
SMEM = pl.BlockSpec(memory_space=pltpu.SMEM)
ANY = pl.BlockSpec(memory_space=pl.ANY)
PARAMS = pltpu.CompilerParams(vmem_limit_bytes=40 * 1024 * 1024)


def swap(value, axis, mask):
    return lax.ppermute(value, axis, [(s, s ^ mask) for s in range(lax.axis_size(axis))])


def call(body, name, outs, ins, specs=None, scratch=(), cost=1.0, **kw):
    return list(
        pl.pallas_call(
        body,
        name=name,
        out_shape=outs,
        in_specs=specs or [VMEM] * len(ins),
        out_specs=kw.pop("out_specs", [VMEM] * len(outs)),
        scratch_shapes=list(scratch),
        compiler_params=PARAMS,
        cost_estimate=pl.CostEstimate(flops=int(cost * 1e9), bytes_accessed=int(cost * 3e6), transcendentals=0),
        **kw,
    )(*ins)
    )


def shape(*dims, dtype=F32):
    return jax.ShapeDtypeStruct(dims, dtype)


def packed_shape(n, kmax):
    return shape(2 * n * kmax // LANES + 16, LANES, dtype=jnp.int16)


def nn(a, b):
    return lax.dot_general(a, b, (((1,), (0,)), ((), ())), preferred_element_type=F32)


def nt(a, b):
    return lax.dot_general(a, b, (((1,), (1,)), ((), ())), preferred_element_type=F32)


def halves(v):
    hi = v.astype(BF)
    return hi, (v - hi.astype(F32)).astype(BF)


def iota(dims, axis):
    return lax.broadcasted_iota(jnp.int32, dims, axis)


def to_column(row):
    n = row.shape[1]
    return jnp.sum(jnp.where(iota((n, n), 0) == iota((n, n), 1), row, 0.0), axis=1, keepdims=True)


def to_row(col, width):
    n = col.shape[0]
    return jnp.sum(jnp.where(iota((n, width), 0) == iota((n, width), 1), col, 0.0), axis=0, keepdims=True)


def cos_sin(angle):
    turns = jnp.floor(angle * 0.6366197723675814 + 0.5)
    t = angle - turns * 1.5707855224609375
    t = t - turns * 1.0804334124e-05
    t2 = t * t
    c = 1.0 + t2 * (-0.5 + t2 * (4.1666667e-2 + t2 * (-1.3888889e-3 + t2 * 2.4801587e-5)))
    s = t * (1.0 + t2 * (-1.6666667e-1 + t2 * (8.3333333e-3 + t2 * (-1.9841270e-4 + t2 * 2.7557319e-6))))
    quad = turns.astype(jnp.int32) & 3
    odd = (quad & 1) == 1
    cc = jnp.where(odd, s, c)
    ss = jnp.where(odd, c, s)
    cc = jnp.where((quad == 1) | (quad == 2), -cc, cc)
    ss = jnp.where(quad >= 2, -ss, ss)
    return cc, ss


def place(index, box):
    return (
        (index & (SIDE - 1)).astype(F32) + (box * SIDE).astype(F32),
        ((index >> 3) & (SIDE - 1)).astype(F32),
        (index >> 6).astype(F32),
    )


def stacked(*refs):
    return jnp.concatenate([jnp.concatenate([ref[0], ref[1]], axis=1) for ref in refs], axis=0)


def open_body(out_ref):
    out_ref[...] = jnp.zeros(out_ref.shape, out_ref.dtype)


def green(own_row, own_box, far_col, far_box):
    ox, oy, oz = place(own_row, own_box)
    fx, fy, fz = place(far_col, far_box)
    d2 = (fx - ox) * (fx - ox) + (fy - oy) * (fy - oy) + (fz - oz) * (fz - oz)
    dist = jnp.sqrt(d2)
    inv = 1.0 / dist
    c, s = cos_sin(WAVENUM * dist)
    return c * inv, s * inv


def store_complex(ref, re, im):
    k = re.shape[0]
    ref[0:k, 0:k] = re
    ref[0:k, k:] = im
    ref[k:, 0:k] = -im
    ref[k:, k:] = re


def store_halves(hi_ref, lo_ref, re, im):
    rhi, rlo = halves(re)
    ihi, ilo = halves(im)
    store_complex(hi_ref, rhi, ihi)
    store_complex(lo_ref, rlo, ilo)


def matches(col, rank_col, row, rank_row):
    k = col.shape[0]
    hit = (col == row) & (iota((k, k), 0) < rank_col) & (iota((k, k), 1) < rank_row)
    return hit.astype(F32).astype(BF)


def plan_body(ranks_ref, skel_ref, contrast_ref, own_ref, beside_ref, dep_ref, *refs, parts):
    e0_ref, e1_ref, q_ref, ghi_ref, glo_ref, g1_ref, j_ref, d_ref, part_ref, part1_ref, hhi_ref, hlo_ref, jp_ref = refs
    box = lax.axis_index("box")
    me = lax.axis_index("field")
    kmax = skel_ref.shape[2]
    width = contrast_ref.shape[1]
    contrast = contrast_ref[...]
    all_ranks = ranks_ref[...].astype(F32)

    def ranks_of(at):
        mine = jnp.where(iota(all_ranks.shape, 1) == at, all_ranks, 0.0)
        return jnp.sum(mine, axis=1, keepdims=True).astype(jnp.int32)

    def row_of(at, level):
        return skel_ref[at][level : level + 1, :]

    def col_of(at, level):
        return to_column(row_of(at, level).astype(F32)).astype(jnp.int32)

    ranks = ranks_of(box)
    n = width // parts
    lane = iota((kmax, width), 1)
    turned = (((lane // n) ^ me) * n) + lane % n
    cols = []
    for level in range(2):
        far = box ^ (1 << level)
        own_col = col_of(box, level)
        r = ranks[level : level + 1, :]
        cols.append(own_col)
        hit = (own_col == turned) & (iota((kmax, width), 0) < r)
        (e0_ref, e1_ref)[level][...] = hit.astype(F32).astype(BF)
        true_hit = (own_col == iota((kmax, width), 1)) & (iota((kmax, width), 0) < r)
        q_col = jnp.sum(jnp.where(true_hit, contrast, 0.0), axis=1, keepdims=True)
        q_ref[pl.ds(level, 1), :] = to_row(q_col, kmax)
        c, s = green(row_of(box, level), box, col_of(far, level), far)
        if level == 0:
            store_halves(ghi_ref, glo_ref, c, s)
        else:
            g1_ref[:, 0:kmax] = c
            g1_ref[:, kmax:] = s
    j_ref[...] = matches(cols[0], ranks[0:1, :], row_of(box, 1), ranks[1:2, :])
    d_ref[...] = matches(cols[1], ranks[1:2, :], row_of(box, 1), ranks[1:2, :])
    near_rows = stacked(own_ref, beside_ref)
    part_ref[...] = nn(e0_ref[:, : 2 * n], near_rows).astype(BF)
    part1_ref[...] = nn(e1_ref[:, : 2 * n], near_rows).astype(BF)
    mate = box ^ 2
    mate_ranks = ranks_of(mate)
    c, s = green(row_of(mate, 0), mate, col_of(box ^ 3, 0), box ^ 3)
    store_halves(hhi_ref, hlo_ref, c, s)
    jp_ref[...] = matches(col_of(mate, 0), mate_ranks[0:1, :], row_of(mate, 1), mate_ranks[1:2, :])


def core_body(own_ref, near_ref, far_ref, g1_ref, d_ref, dep_ref, mc_ref, khi_ref, klo_ref, ct_ref):
    slot = lax.axis_index("box") & 3
    quarter = own_ref.shape[0] // 2
    kmax = own_ref.shape[1]
    pieces = (own_ref[...], near_ref[...], far_ref[0], far_ref[1])
    for mask, piece in enumerate(pieces):
        start = pl.multiple_of((slot ^ mask) * quarter, quarter)
        ct_ref[pl.ds(start, quarter), 0:kmax] = piece[:quarter]
        ct_ref[pl.ds(start, quarter), kmax:] = piece[quarter:]
    cr = ct_ref[:, 0:kmax]
    ci = ct_ref[:, kmax:]
    mc_ref[0:kmax, 0:kmax] = cr
    mc_ref[0:kmax, kmax:] = ci
    mc_ref[kmax:, 0:kmax] = -ci
    mc_ref[kmax:, kmax:] = cr
    dup = d_ref[...]
    gr = g1_ref[:, 0:kmax]
    gi = g1_ref[:, kmax:]
    grh, grl = halves(gr)
    gih, gil = halves(gi)
    dr = nn(grh, dup) + nn(grl, dup)
    di = nn(gih, dup) + nn(gil, dup)
    drh, drl = halves(dr)
    dih, dil = halves(di)
    kr = gr - ((nn(drh, cr) + nn(drl, cr)) - (nn(dih, ci) + nn(dil, ci)))
    ki = gi - ((nn(drh, ci) + nn(drl, ci)) + (nn(dih, cr) + nn(dil, cr)))
    krh, krl = halves(kr)
    kih, kil = halves(ki)
    for ref, a, b in ((khi_ref, krh, kih), (klo_ref, krl, kil)):
        ref[0:kmax, 0:kmax] = a
        ref[0:kmax, kmax:] = b
        ref[kmax:, 0:kmax] = -b
        ref[kmax:, kmax:] = a


def relay_body(in_ref, *rest):
    rest[-1][...] = in_ref[...]


def pair_body(a_ref, b_ref, dep_ref, out_ref):
    out_ref[0] = a_ref[...]
    out_ref[1] = b_ref[...]


def turned_fields(x_ref, start, n):
    re = x_ref[0, start : start + n]
    im = x_ref[1, start : start + n]
    return jnp.concatenate([re, -im], axis=1), jnp.concatenate([im, re], axis=1)


def send(x_ref, picked, q_ref, out_ref, start, n):
    q = q_ref[0:1, :]
    left, right = turned_fields(x_ref, start, n)
    w = jnp.concatenate([nt(left, picked) * q, nt(right, picked) * q], axis=1)
    pack(w, out_ref)


def first_body(part_ref, across_ref, beyond_ref, e0_ref, x_ref, q_ref, picked_ref, out_ref, side_ref, *, start, n, side_start):
    rows = across_ref.shape[1]
    picked = (nn(e0_ref[:, 2 * rows :], stacked(across_ref, beyond_ref)) + part_ref[...].astype(F32)).astype(BF)
    picked_ref[...] = picked
    q = q_ref[0:1, :]
    kmax = picked.shape[0]
    side_n = (side_ref.shape[0] - 16) * LANES // (2 * kmax)
    left, right = turned_fields(x_ref, start, n)
    more_left, more_right = turned_fields(x_ref, side_start, side_n)
    left = jnp.concatenate([left, more_left], axis=0)
    right = jnp.concatenate([right, more_right], axis=0)
    w = jnp.concatenate([nt(left, picked) * q, nt(right, picked) * q], axis=1)
    pack(w[:n], out_ref)
    pack(w[n:], side_ref, q_ref[1:2, :])


def rest_body(x_ref, picked_ref, q_ref, dep_ref, out_ref, *, start, n):
    send(x_ref, picked_ref[...], q_ref, out_ref, start, n)


def rows_body(x_ref, picked_ref, dep_ref, v_ref):
    kmax = picked_ref.shape[0]
    left, right = turned_fields(x_ref, 0, x_ref.shape[1])
    picked = picked_ref[...]
    v_ref[:, 0:kmax] = nt(left, picked)
    v_ref[:, kmax:] = nt(right, picked)


def ahead_body(x_ref, part_ref, across_ref, beyond_ref, e1_ref, side_ref, q_ref, dep_ref, picked_ref, out_ref, *, start, n):
    half = out_ref.shape[0] // 2
    out_ref[0:half] = side_ref[...]
    rows = across_ref.shape[1]
    picked = (nn(e1_ref[:, 2 * rows :], stacked(across_ref, beyond_ref)) + part_ref[...].astype(F32)).astype(BF)
    picked_ref[...] = picked
    left, right = turned_fields(x_ref, start, n)
    q = q_ref[1:2, :]
    w = jnp.concatenate([nt(left, picked) * q, nt(right, picked) * q], axis=1)
    pack(w, out_ref.at[half : 2 * half])


def onward_body(own_ref, got_ref, out_ref):
    half = own_ref.shape[0] // 2
    out_ref[0:half] = own_ref[0:half]
    out_ref[half:] = got_ref[0:half]


def pick(hi, lo, sel):
    k = sel.shape[0]
    parts = [nn(hi[:, i : i + k], sel) + nn(lo[:, i : i + k], sel) for i in (0, k)]
    return jnp.concatenate(parts, axis=1)


def around_body(*refs, start):
    (near_in_ref, mate_ref, ghi_ref, glo_ref, hhi_ref, hlo_ref, j_ref, jp_ref) = refs[:8]
    (v_ref, near_ref, far_ref, e0_ref, e1_ref, mc_ref, khi_ref, klo_ref, out_ref) = refs[8:]
    half = near_in_ref.shape[0] // 2
    n = out_ref.shape[1]
    k = j_ref.shape[0]
    lanes = mate_ref.shape[1]
    count = k // lanes
    mhi = khi_ref[...]
    mlo = klo_ref[...]
    t = apply_packed(near_in_ref.at[half : 2 * half], hhi_ref[...], hlo_ref[...])
    tail = mate_ref[half - 16 : half, :].astype(jnp.int32).astype(F32)
    upper = jnp.concatenate([tail[2 + i : 3 + i, :] for i in range(count)], axis=1)
    lower = jnp.concatenate([tail[2 + count + i : 3 + count + i, :] for i in range(count)], axis=1)
    q = (upper + lower * (1.0 / 32768.0)) * (1.0 / 16384.0)
    v, scale = unpack(mate_ref.at[half : 2 * half], 2 * k)
    w = v.astype(F32) * scale - pick(*halves(t), jp_ref[...]) * jnp.concatenate([q, q], axis=1)
    hi, lo = halves(w)
    p = nn(hi, mhi) + (nn(lo, mhi) + nn(hi, mlo))
    g = apply_packed(near_in_ref.at[0:half], ghi_ref[...], glo_ref[...])
    gh, gl = halves(g)
    u = v_ref[start : start + n, :] - pick(gh, gl, j_ref[...])
    uh, ul = halves(u)
    mc = mc_ref[...]
    p = p + (nn(uh, mc) + nn(ul, mc))
    ph, pl_ = halves(p)
    e0 = e0_ref[...]
    e1 = e1_ref[...]
    for i in range(2):
        cols = slice(i * k, i * k + k)
        y = jnp.concatenate([near_ref[i, start : start + n], far_ref[i, start : start + n]], axis=1)
        scattered = (nn(gh[:, cols], e0) + nn(gl[:, cols], e0)) + (nn(ph[:, cols], e1) + nn(pl_[:, cols], e1))
        out_ref[i] = y - scattered


def leaf_body(x_ref, p_ref, q_ref, dep_ref, y_ref):
    left, right = turned_fields(x_ref, 0, x_ref.shape[1])
    a = stacked(p_ref, q_ref)
    y_ref[0] = nt(left, a)
    y_ref[1] = nt(right, a)


def pack(w, out_ref, weight=None):
    n, both = w.shape
    lanes = out_ref.shape[1]
    most = jnp.max(jnp.abs(w), axis=1, keepdims=True)
    step = jnp.ceil(jnp.log2(jnp.maximum(most, 1e-30)) * STEPS)
    inv = TOP / jnp.exp2(step / STEPS)
    v = jnp.floor(w * inv + 0.5).astype(jnp.int32).astype(jnp.int16)
    for i in range(both // lanes):
        out_ref[i * n : (i + 1) * n, :] = v[:, i * lanes : (i + 1) * lanes]
    groups = -(-n // lanes)
    step = to_row(step, groups * lanes)
    tile = jnp.zeros((16, lanes), F32)
    for i in range(groups):
        tile = jnp.where(iota(tile.shape, 0) == i, step[:, i * lanes : (i + 1) * lanes], tile)
    if weight is not None:
        upper = jnp.floor(weight * 16384.0)
        lower = jnp.floor((weight * 16384.0 - upper) * 32768.0)
        count = weight.shape[1] // lanes
        for j, value in enumerate((upper, lower)):
            for i in range(count):
                at = iota(tile.shape, 0) == 2 + j * count + i
                tile = jnp.where(at, value[:, i * lanes : (i + 1) * lanes], tile)
    out_ref[both // lanes * n :, :] = tile.astype(jnp.int32).astype(jnp.int16)


def unpack(in_ref, k):
    lanes = in_ref.shape[1]
    pieces = k // lanes
    n = (in_ref.shape[0] - 16) // pieces
    groups = -(-n // lanes)
    steps = in_ref[pieces * n :, :].astype(jnp.int32).astype(F32)
    steps = jnp.concatenate([steps[i : i + 1, :] for i in range(groups)], axis=1)
    own = iota((n, groups * lanes), 0) == iota((n, groups * lanes), 1)
    step = jnp.sum(jnp.where(own, steps, 0.0), axis=1, keepdims=True)
    scale = jnp.exp2(step / STEPS) * (1.0 / TOP)
    v = jnp.concatenate([in_ref[i * n : (i + 1) * n, :] for i in range(pieces)], axis=1).astype(jnp.int32)
    return v, scale


def apply_packed(in_ref, mhi, mlo):
    v, scale = unpack(in_ref, mhi.shape[0])
    upper = (v + 128) & -256
    lower = (v - upper).astype(F32).astype(BF)
    upper = upper.astype(F32).astype(BF)
    return (nn(upper, mhi) + (nn(lower, mhi) + nn(upper, mlo))) * scale


def second_body(in_ref, ghi_ref, glo_ref, v_ref, j_ref, q_ref, *rest, start):
    out_ref, gs_ref, us_ref = rest[-3:]
    n = gs_ref.shape[1]
    k = j_ref.shape[0]
    g = apply_packed(in_ref, ghi_ref[...], glo_ref[...])
    hi, lo = halves(g)
    gs_ref[0] = hi
    gs_ref[1] = lo
    j = j_ref[...]
    q = q_ref[1:2, :]
    re = v_ref[start : start + n, :k] - (nn(hi[:, :k], j) + nn(lo[:, :k], j))
    im = v_ref[start : start + n, k:] - (nn(hi[:, k:], j) + nn(lo[:, k:], j))
    u = jnp.concatenate([re, im], axis=1)
    pack(u * jnp.concatenate([q, q], axis=1), out_ref)
    hi, lo = halves(u)
    us_ref[0] = hi
    us_ref[1] = lo


def third_body(gs_ref, us_ref, near_ref, far_ref, e0_ref, mc_ref, dep_ref, part_ref, p_ref, *, start):
    n = gs_ref.shape[1]
    k = e0_ref.shape[0]
    e = e0_ref[...]
    for i in range(2):
        cols = slice(i * k, i * k + k)
        y = jnp.concatenate([near_ref[i, start : start + n], far_ref[i, start : start + n]], axis=1)
        part_ref[i] = y - (nn(gs_ref[0, :, cols], e) + nn(gs_ref[1, :, cols], e))
    mc = mc_ref[...]
    p_ref[...] = nn(us_ref[0], mc) + nn(us_ref[1], mc)


def finish(in_ref, part_ref, p_ref, khi, klo, e):
    k = e.shape[0]
    p = p_ref[...] + apply_packed(in_ref, khi, klo)
    hi, lo = halves(p)
    for i in range(2):
        cols = slice(i * k, i * k + k)
        yield i, part_ref[i] - (nn(hi[:, cols], e) + nn(lo[:, cols], e))


def writer(out_ref, sem, blocks):
    me = lax.axis_index("field")
    copies = []

    def write(src_ref, i, row):
        n = src_ref.shape[2] // blocks
        for m in range(blocks):
            col = pl.multiple_of((me ^ m) * n, n)
            copy = pltpu.make_async_copy(
                src_ref.at[i, :, pl.ds(m * n, n)],
                out_ref.at[i, pl.ds(row, src_ref.shape[1]), pl.ds(col, n)],
                sem.at[len(copies)],
            )
            copy.start()
            copies.append(copy)

    return write, copies


def last_body(khi_ref, klo_ref, e1_ref, in_ref, part_ref, p_ref, *rest, start, blocks, done_at):
    out_ref, hold_ref, sem = rest[-3:]
    write, copies = writer(out_ref, sem, blocks)
    if done_at is not None:
        write(rest[0], slice(None), done_at)
    for i, value in finish(in_ref, part_ref, p_ref, khi_ref[...], klo_ref[...], e1_ref[...]):
        hold_ref[i] = value
        write(hold_ref, i, start)
    for copy in copies:
        copy.wait()


def body(incident, leaf_inverse, contrast, skel_index, ranks, top_core):
    nf, width = incident.shape[1:]
    boxes, _, kmax = skel_index.shape
    quarter = top_core.shape[2]
    own = leaf_inverse[0]
    across = swap(own, "field", 2)
    beside = swap(own, "field", 1)
    core_own = jnp.swapaxes(top_core, 1, 2).reshape(2 * quarter, kmax)
    core_near = swap(core_own, "box", 1)
    n = n_rows = own.shape[1]
    (opened,) = call(open_body, "open", [shape(8, 128)], [], cost=4.0)
    e0, e1, q, ghi, glo, g1, dup01, dup11, part, part1, hhi, hlo, dupm = call(
        lambda *refs: plan_body(*refs, parts=lax.axis_size("field")),
        "plan",
        [
            shape(kmax, width, dtype=BF),
            shape(kmax, width, dtype=BF),
            shape(8, kmax),
            shape(2 * kmax, 2 * kmax, dtype=BF),
            shape(2 * kmax, 2 * kmax, dtype=BF),
            shape(kmax, 2 * kmax),
            shape(kmax, kmax, dtype=BF),
            shape(kmax, kmax, dtype=BF),
            shape(kmax, 2 * width, dtype=BF),
            shape(kmax, 2 * width, dtype=BF),
            shape(2 * kmax, 2 * kmax, dtype=BF),
            shape(2 * kmax, 2 * kmax, dtype=BF),
            shape(kmax, kmax, dtype=BF),
        ],
        [ranks.T, skel_index, contrast.reshape(1, width), own, beside, opened],
        [VMEM] * 5 + [ANY],
    )
    x = incident
    (near,) = call(
        leaf_body, "near", [shape(2, nf, 2 * n)], [x, own, beside, part], [VMEM] * 3 + [ANY], cost=0.7
    )
    (pair,) = call(
        pair_body, "pair", [shape(2, 2 * quarter, kmax, dtype=BF)], [core_own, core_near, near], [VMEM, VMEM, ANY], cost=0.05
    )
    core_far = swap(pair, "box", 2)
    (across,) = call(
        relay_body, "relay", [shape(*across.shape, dtype=BF)], [across, pair, near], [VMEM, ANY, ANY], cost=0.05
    )
    beyond = swap(across, "field", 1)
    chunks = [nf // sum(SHARES) * share for share in SHARES]
    sizes = [(sum(chunks[:i]), n) for i, n in enumerate(chunks)]
    start, n = sizes[0]
    side_start, side_n = sizes[2]
    picked, head, side = call(
        lambda *refs, start=start, n=n: first_body(*refs, start=start, n=n, side_start=side_start),
        "first",
        [
            shape(kmax, 2 * width, dtype=BF),
            packed_shape(n, kmax),
            packed_shape(side_n, kmax),
        ],
        [part, across, beyond, e0, x, q],
        cost=0.8,
    )

    got = swap(head, "box", 1)
    picked1, ahead = call(
        lambda *refs: ahead_body(*refs, start=side_start, n=side_n),
        "ahead",
        [shape(kmax, 2 * width, dtype=BF), shape(2 * packed_shape(side_n, kmax).shape[0], LANES, dtype=jnp.int16)],
        [x, part1, across, beyond, e1, side, q, e0],
        [VMEM] * 7 + [ANY],
        cost=1.4,
    )
    mate = swap(ahead, "box", 2)
    start, n = sizes[1]
    (packed,) = call(
        lambda *refs: rest_body(*refs, start=start, n=n),
        "ready",
        [packed_shape(n, kmax)],
        [x, picked, q, ahead],
        [VMEM] * 3 + [ANY],
        cost=0.6,
    )
    coming = swap(packed, "box", 1)
    (v1,) = call(rows_body, "rows", [shape(nf, 2 * kmax)], [x, picked1, packed], [VMEM] * 2 + [ANY])
    mc, khi, klo = call(
        core_body,
        "core",
        [shape(2 * kmax, 2 * kmax, dtype=BF)] * 3,
        [core_own, core_near, core_far, g1, dup11, v1],
        [VMEM] * 5 + [ANY],
        [pltpu.VMEM((kmax, 2 * kmax), BF)],
    )
    (far,) = call(
        leaf_body, "leaf", [shape(2, nf, 2 * n_rows)], [x, across, beyond, mc], [VMEM] * 3 + [ANY], cost=0.7
    )
    late = []
    for i, (start, n) in enumerate(sizes[:2]):
        back, gs, us = call(
            lambda *refs, start=start: second_body(*refs, start=start),
            f"second{i}",
            [packed_shape(n, kmax), shape(2, n, 2 * kmax, dtype=BF), shape(2, n, 2 * kmax, dtype=BF)],
            [got, ghi, glo, v1, dup01, q, sent if i else far],
            [VMEM] * 6 + [ANY],
            cost=0.8,
        )
        got = coming
        late.append([swap(back, "box", 2), gs, us])
        if i == 0:
            (onward,) = call(onward_body, "onward", [shape(*ahead.shape, dtype=jnp.int16)], [ahead, mate], cost=0.05)
            sent = onward
            onward = swap(onward, "box", 1)
    for i, (start, n) in enumerate(sizes[:2]):
        late[i][1:] = call(
            lambda *refs, start=start: third_body(*refs, start=start),
            f"third{i}",
            [shape(2, n, width), shape(n, 2 * kmax)],
            [late[i][1], late[i][2], near, far, e0, mc, gs],
            [VMEM] * 6 + [ANY],
            cost=0.5,
        )
    side = call(
        lambda *refs: around_body(*refs, start=side_start),
        "around",
        [shape(2, side_n, width)],
        [onward, mate, ghi, glo, hhi, hlo, dup01, dupm, v1, near, far, e0, e1, mc, khi, klo],
        cost=2.5,
    )
    blocks = lax.axis_size("field")
    out = []
    for i, (start, n) in enumerate(sizes[:2]):
        ready = side if i == 1 else []
        out = call(
            lambda *refs, start=start, ready=ready: last_body(
                *refs, start=start, blocks=blocks, done_at=side_start if ready else None
            ),
            f"last{i}",
            [shape(2, nf, width)],
            [khi, klo, e1] + late[i] + ready + out,
            [VMEM] * (6 + len(ready)) + [ANY] * len(out),
            [pltpu.VMEM((2, n, width), F32), pltpu.SemaphoreType.DMA(((3 if ready else 2) * blocks,))],
            out_specs=[ANY],
            input_output_aliases={6 + len(ready): 0} if out else {},
        )
    return out[0]


def solution(mesh):
    return jax.shard_map(
        body,
        mesh=mesh,
        in_specs=(P(None, "field", "box"), P("box", None, "field", None), P("box"), P(), P(), P(None, None, "box")),
        out_specs=P(None, "field", "box"),
        check_vma=False,
    )
```

```python
import jax
import jax.numpy as jnp
from jax import lax
from jax.experimental import pallas as pl
from jax.experimental.pallas import tpu as pltpu
from jax.sharding import PartitionSpec as P

SIDE = 8
WAVENUM = 0.7
BF = jnp.bfloat16
F32 = jnp.float32
SHARES = (13, 12, 7)
TOP = 32766.0
STEPS = 128.0
LANES = 128
VMEM = pl.BlockSpec(memory_space=pltpu.VMEM)
SMEM = pl.BlockSpec(memory_space=pltpu.SMEM)
ANY = pl.BlockSpec(memory_space=pl.ANY)
PARAMS = pltpu.CompilerParams(vmem_limit_bytes=40 * 1024 * 1024)


def swap(value, axis, mask):
    return lax.ppermute(value, axis, [(s, s ^ mask) for s in range(lax.axis_size(axis))])


def call(body, name, outs, ins, specs=None, scratch=(), cost=1.0, **kw):
    return list(
        pl.pallas_call(
        body,
        name=name,
        out_shape=outs,
        in_specs=specs or [VMEM] * len(ins),
        out_specs=kw.pop("out_specs", [VMEM] * len(outs)),
        scratch_shapes=list(scratch),
        compiler_params=PARAMS,
        cost_estimate=pl.CostEstimate(flops=int(cost * 1e9), bytes_accessed=int(cost * 3e6), transcendentals=0),
        **kw,
    )(*ins)
    )


def shape(*dims, dtype=F32):
    return jax.ShapeDtypeStruct(dims, dtype)


def packed_shape(n, kmax):
    return shape(2 * n * kmax // LANES + 16, LANES, dtype=jnp.int16)


def nn(a, b):
    return lax.dot_general(a, b, (((1,), (0,)), ((), ())), preferred_element_type=F32)


def nt(a, b):
    return lax.dot_general(a, b, (((1,), (1,)), ((), ())), preferred_element_type=F32)


def halves(v):
    hi = v.astype(BF)
    return hi, (v - hi.astype(F32)).astype(BF)


def iota(dims, axis):
    return lax.broadcasted_iota(jnp.int32, dims, axis)


def to_column(row):
    n = row.shape[1]
    return jnp.sum(jnp.where(iota((n, n), 0) == iota((n, n), 1), row, 0.0), axis=1, keepdims=True)


def to_row(col, width):
    n = col.shape[0]
    return jnp.sum(jnp.where(iota((n, width), 0) == iota((n, width), 1), col, 0.0), axis=0, keepdims=True)


def cos_sin(angle):
    turns = jnp.floor(angle * 0.6366197723675814 + 0.5)
    t = angle - turns * 1.5707855224609375
    t = t - turns * 1.0804334124e-05
    t2 = t * t
    c = 1.0 + t2 * (-0.5 + t2 * (4.1666667e-2 + t2 * (-1.3888889e-3 + t2 * 2.4801587e-5)))
    s = t * (1.0 + t2 * (-1.6666667e-1 + t2 * (8.3333333e-3 + t2 * (-1.9841270e-4 + t2 * 2.7557319e-6))))
    quad = turns.astype(jnp.int32) & 3
    odd = (quad & 1) == 1
    cc = jnp.where(odd, s, c)
    ss = jnp.where(odd, c, s)
    cc = jnp.where((quad == 1) | (quad == 2), -cc, cc)
    ss = jnp.where(quad >= 2, -ss, ss)
    return cc, ss


def place(index, box):
    return (
        (index & (SIDE - 1)).astype(F32) + (box * SIDE).astype(F32),
        ((index >> 3) & (SIDE - 1)).astype(F32),
        (index >> 6).astype(F32),
    )


def stacked(*refs):
    return jnp.concatenate([jnp.concatenate([ref[0], ref[1]], axis=1) for ref in refs], axis=0)


def open_body(out_ref):
    out_ref[...] = jnp.zeros(out_ref.shape, out_ref.dtype)


def green(own_row, own_box, far_col, far_box):
    ox, oy, oz = place(own_row, own_box)
    fx, fy, fz = place(far_col, far_box)
    d2 = (fx - ox) * (fx - ox) + (fy - oy) * (fy - oy) + (fz - oz) * (fz - oz)
    dist = jnp.sqrt(d2)
    inv = 1.0 / dist
    c, s = cos_sin(WAVENUM * dist)
    return c * inv, s * inv


def store_complex(ref, re, im):
    k = re.shape[0]
    ref[0:k, 0:k] = re
    ref[0:k, k:] = im
    ref[k:, 0:k] = -im
    ref[k:, k:] = re


def store_halves(hi_ref, lo_ref, re, im):
    rhi, rlo = halves(re)
    ihi, ilo = halves(im)
    store_complex(hi_ref, rhi, ihi)
    store_complex(lo_ref, rlo, ilo)


def matches(col, rank_col, row, rank_row):
    k = col.shape[0]
    hit = (col == row) & (iota((k, k), 0) < rank_col) & (iota((k, k), 1) < rank_row)
    return hit.astype(F32).astype(BF)


def plan_body(ranks_ref, skel_ref, contrast_ref, own_ref, beside_ref, dep_ref, *refs, parts):
    e0_ref, e1_ref, q_ref, ghi_ref, glo_ref, g1_ref, j_ref, d_ref, part_ref, part1_ref, hhi_ref, hlo_ref, jp_ref = refs
    box = lax.axis_index("box")
    me = lax.axis_index("field")
    kmax = skel_ref.shape[2]
    width = contrast_ref.shape[1]
    contrast = contrast_ref[...]
    all_ranks = ranks_ref[...].astype(F32)

    def ranks_of(at):
        mine = jnp.where(iota(all_ranks.shape, 1) == at, all_ranks, 0.0)
        return jnp.sum(mine, axis=1, keepdims=True).astype(jnp.int32)

    def row_of(at, level):
        return skel_ref[at][level : level + 1, :]

    def col_of(at, level):
        return to_column(row_of(at, level).astype(F32)).astype(jnp.int32)

    ranks = ranks_of(box)
    n = width // parts
    lane = iota((kmax, width), 1)
    turned = (((lane // n) ^ me) * n) + lane % n
    cols = []
    for level in range(2):
        far = box ^ (1 << level)
        own_col = col_of(box, level)
        r = ranks[level : level + 1, :]
        cols.append(own_col)
        hit = (own_col == turned) & (iota((kmax, width), 0) < r)
        (e0_ref, e1_ref)[level][...] = hit.astype(F32).astype(BF)
        true_hit = (own_col == iota((kmax, width), 1)) & (iota((kmax, width), 0) < r)
        q_col = jnp.sum(jnp.where(true_hit, contrast, 0.0), axis=1, keepdims=True)
        q_ref[pl.ds(level, 1), :] = to_row(q_col, kmax)
        c, s = green(row_of(box, level), box, col_of(far, level), far)
        if level == 0:
            store_halves(ghi_ref, glo_ref, c, s)
        else:
            g1_ref[:, 0:kmax] = c
            g1_ref[:, kmax:] = s
    j_ref[...] = matches(cols[0], ranks[0:1, :], row_of(box, 1), ranks[1:2, :])
    d_ref[...] = matches(cols[1], ranks[1:2, :], row_of(box, 1), ranks[1:2, :])
    near_rows = stacked(own_ref, beside_ref)
    part_ref[...] = nn(e0_ref[:, : 2 * n], near_rows).astype(BF)
    part1_ref[...] = nn(e1_ref[:, : 2 * n], near_rows).astype(BF)
    mate = box ^ 2
    mate_ranks = ranks_of(mate)
    c, s = green(row_of(mate, 0), mate, col_of(box ^ 3, 0), box ^ 3)
    store_halves(hhi_ref, hlo_ref, c, s)
    jp_ref[...] = matches(col_of(mate, 0), mate_ranks[0:1, :], row_of(mate, 1), mate_ranks[1:2, :])


def core_body(own_ref, near_ref, far_ref, g1_ref, d_ref, dep_ref, mc_ref, khi_ref, klo_ref, ct_ref):
    slot = lax.axis_index("box") & 3
    quarter = own_ref.shape[0] // 2
    kmax = own_ref.shape[1]
    pieces = (own_ref[...], near_ref[...], far_ref[0], far_ref[1])
    for mask, piece in enumerate(pieces):
        start = pl.multiple_of((slot ^ mask) * quarter, quarter)
        ct_ref[pl.ds(start, quarter), 0:kmax] = piece[:quarter]
        ct_ref[pl.ds(start, quarter), kmax:] = piece[quarter:]
    cr = ct_ref[:, 0:kmax]
    ci = ct_ref[:, kmax:]
    mc_ref[0:kmax, 0:kmax] = cr
    mc_ref[0:kmax, kmax:] = ci
    mc_ref[kmax:, 0:kmax] = -ci
    mc_ref[kmax:, kmax:] = cr
    dup = d_ref[...]
    gr = g1_ref[:, 0:kmax]
    gi = g1_ref[:, kmax:]
    grh, grl = halves(gr)
    gih, gil = halves(gi)
    dr = nn(grh, dup) + nn(grl, dup)
    di = nn(gih, dup) + nn(gil, dup)
    drh, drl = halves(dr)
    dih, dil = halves(di)
    kr = gr - ((nn(drh, cr) + nn(drl, cr)) - (nn(dih, ci) + nn(dil, ci)))
    ki = gi - ((nn(drh, ci) + nn(drl, ci)) + (nn(dih, cr) + nn(dil, cr)))
    krh, krl = halves(kr)
    kih, kil = halves(ki)
    for ref, a, b in ((khi_ref, krh, kih), (klo_ref, krl, kil)):
        ref[0:kmax, 0:kmax] = a
        ref[0:kmax, kmax:] = b
        ref[kmax:, 0:kmax] = -b
        ref[kmax:, kmax:] = a


def relay_body(in_ref, *rest):
    rest[-1][...] = in_ref[...]


def pair_body(a_ref, b_ref, dep_ref, out_ref):
    out_ref[0] = a_ref[...]
    out_ref[1] = b_ref[...]


def turned_fields(x_ref, start, n):
    re = x_ref[0, start : start + n]
    im = x_ref[1, start : start + n]
    return jnp.concatenate([re, -im], axis=1), jnp.concatenate([im, re], axis=1)


def send(x_ref, picked, q_ref, out_ref, start, n):
    q = q_ref[0:1, :]
    left, right = turned_fields(x_ref, start, n)
    w = jnp.concatenate([nt(left, picked) * q, nt(right, picked) * q], axis=1)
    pack(w, out_ref)


def first_body(part_ref, across_ref, beyond_ref, e0_ref, x_ref, q_ref, picked_ref, out_ref, side_ref, *, start, n, side_start):
    rows = across_ref.shape[1]
    picked = (nn(e0_ref[:, 2 * rows :], stacked(across_ref, beyond_ref)) + part_ref[...].astype(F32)).astype(BF)
    picked_ref[...] = picked
    q = q_ref[0:1, :]
    kmax = picked.shape[0]
    side_n = (side_ref.shape[0] - 16) * LANES // (2 * kmax)
    left, right = turned_fields(x_ref, start, n)
    more_left, more_right = turned_fields(x_ref, side_start, side_n)
    left = jnp.concatenate([left, more_left], axis=0)
    right = jnp.concatenate([right, more_right], axis=0)
    w = jnp.concatenate([nt(left, picked) * q, nt(right, picked) * q], axis=1)
    pack(w[:n], out_ref)
    pack(w[n:], side_ref, q_ref[1:2, :])


def rest_body(x_ref, picked_ref, q_ref, dep_ref, out_ref, *, start, n):
    send(x_ref, picked_ref[...], q_ref, out_ref, start, n)


def rows_body(x_ref, picked_ref, dep_ref, v_ref):
    kmax = picked_ref.shape[0]
    left, right = turned_fields(x_ref, 0, x_ref.shape[1])
    picked = picked_ref[...]
    v_ref[:, 0:kmax] = nt(left, picked)
    v_ref[:, kmax:] = nt(right, picked)


def ahead_body(x_ref, part_ref, across_ref, beyond_ref, e1_ref, side_ref, q_ref, dep_ref, picked_ref, out_ref, *, start, n):
    half = out_ref.shape[0] // 2
    out_ref[0:half] = side_ref[...]
    rows = across_ref.shape[1]
    picked = (nn(e1_ref[:, 2 * rows :], stacked(across_ref, beyond_ref)) + part_ref[...].astype(F32)).astype(BF)
    picked_ref[...] = picked
    left, right = turned_fields(x_ref, start, n)
    q = q_ref[1:2, :]
    w = jnp.concatenate([nt(left, picked) * q, nt(right, picked) * q], axis=1)
    pack(w, out_ref.at[half : 2 * half])


def onward_body(own_ref, got_ref, out_ref):
    half = own_ref.shape[0] // 2
    out_ref[0:half] = own_ref[0:half]
    out_ref[half:] = got_ref[0:half]


def pick(hi, lo, sel):
    k = sel.shape[0]
    parts = [nn(hi[:, i : i + k], sel) + nn(lo[:, i : i + k], sel) for i in (0, k)]
    return jnp.concatenate(parts, axis=1)


def around_body(*refs, start):
    (near_in_ref, mate_ref, ghi_ref, glo_ref, hhi_ref, hlo_ref, j_ref, jp_ref) = refs[:8]
    (v_ref, near_ref, far_ref, e0_ref, e1_ref, mc_ref, khi_ref, klo_ref, out_ref) = refs[8:]
    half = near_in_ref.shape[0] // 2
    n = out_ref.shape[1]
    k = j_ref.shape[0]
    lanes = mate_ref.shape[1]
    count = k // lanes
    mhi = khi_ref[...]
    mlo = klo_ref[...]
    t = apply_packed(near_in_ref.at[half : 2 * half], hhi_ref[...], hlo_ref[...])
    tail = mate_ref[half - 16 : half, :].astype(jnp.int32).astype(F32)
    upper = jnp.concatenate([tail[2 + i : 3 + i, :] for i in range(count)], axis=1)
    lower = jnp.concatenate([tail[2 + count + i : 3 + count + i, :] for i in range(count)], axis=1)
    q = (upper + lower * (1.0 / 32768.0)) * (1.0 / 16384.0)
    v, scale = unpack(mate_ref.at[half : 2 * half], 2 * k)
    w = v.astype(F32) * scale - pick(*halves(t), jp_ref[...]) * jnp.concatenate([q, q], axis=1)
    hi, lo = halves(w)
    p = nn(hi, mhi) + (nn(lo, mhi) + nn(hi, mlo))
    g = apply_packed(near_in_ref.at[0:half], ghi_ref[...], glo_ref[...])
    gh, gl = halves(g)
    u = v_ref[start : start + n, :] - pick(gh, gl, j_ref[...])
    uh, ul = halves(u)
    mc = mc_ref[...]
    p = p + (nn(uh, mc) + nn(ul, mc))
    ph, pl_ = halves(p)
    e0 = e0_ref[...]
    e1 = e1_ref[...]
    for i in range(2):
        cols = slice(i * k, i * k + k)
        y = jnp.concatenate([near_ref[i, start : start + n], far_ref[i, start : start + n]], axis=1)
        scattered = (nn(gh[:, cols], e0) + nn(gl[:, cols], e0)) + (nn(ph[:, cols], e1) + nn(pl_[:, cols], e1))
        out_ref[i] = y - scattered


def leaf_body(x_ref, p_ref, q_ref, dep_ref, y_ref):
    left, right = turned_fields(x_ref, 0, x_ref.shape[1])
    a = stacked(p_ref, q_ref)
    y_ref[0] = nt(left, a)
    y_ref[1] = nt(right, a)


def pack(w, out_ref, weight=None):
    n, both = w.shape
    lanes = out_ref.shape[1]
    most = jnp.max(jnp.abs(w), axis=1, keepdims=True)
    step = jnp.ceil(jnp.log2(jnp.maximum(most, 1e-30)) * STEPS)
    inv = TOP / jnp.exp2(step / STEPS)
    v = jnp.floor(w * inv + 0.5).astype(jnp.int32).astype(jnp.int16)
    for i in range(both // lanes):
        out_ref[i * n : (i + 1) * n, :] = v[:, i * lanes : (i + 1) * lanes]
    groups = -(-n // lanes)
    step = to_row(step, groups * lanes)
    tile = jnp.zeros((16, lanes), F32)
    for i in range(groups):
        tile = jnp.where(iota(tile.shape, 0) == i, step[:, i * lanes : (i + 1) * lanes], tile)
    if weight is not None:
        upper = jnp.floor(weight * 16384.0)
        lower = jnp.floor((weight * 16384.0 - upper) * 32768.0)
        count = weight.shape[1] // lanes
        for j, value in enumerate((upper, lower)):
            for i in range(count):
                at = iota(tile.shape, 0) == 2 + j * count + i
                tile = jnp.where(at, value[:, i * lanes : (i + 1) * lanes], tile)
    out_ref[both // lanes * n :, :] = tile.astype(jnp.int32).astype(jnp.int16)


def unpack(in_ref, k):
    lanes = in_ref.shape[1]
    pieces = k // lanes
    n = (in_ref.shape[0] - 16) // pieces
    groups = -(-n // lanes)
    steps = in_ref[pieces * n :, :].astype(jnp.int32).astype(F32)
    steps = jnp.concatenate([steps[i : i + 1, :] for i in range(groups)], axis=1)
    own = iota((n, groups * lanes), 0) == iota((n, groups * lanes), 1)
    step = jnp.sum(jnp.where(own, steps, 0.0), axis=1, keepdims=True)
    scale = jnp.exp2(step / STEPS) * (1.0 / TOP)
    v = jnp.concatenate([in_ref[i * n : (i + 1) * n, :] for i in range(pieces)], axis=1).astype(jnp.int32)
    return v, scale


def apply_packed(in_ref, mhi, mlo):
    v, scale = unpack(in_ref, mhi.shape[0])
    upper = (v + 128) & -256
    lower = (v - upper).astype(F32).astype(BF)
    upper = upper.astype(F32).astype(BF)
    return (nn(upper, mhi) + (nn(lower, mhi) + nn(upper, mlo))) * scale


def second_body(in_ref, ghi_ref, glo_ref, v_ref, j_ref, q_ref, *rest, start):
    out_ref, gs_ref, us_ref = rest[-3:]
    n = gs_ref.shape[1]
    k = j_ref.shape[0]
    g = apply_packed(in_ref, ghi_ref[...], glo_ref[...])
    hi, lo = halves(g)
    gs_ref[0] = hi
    gs_ref[1] = lo
    j = j_ref[...]
    q = q_ref[1:2, :]
    re = v_ref[start : start + n, :k] - (nn(hi[:, :k], j) + nn(lo[:, :k], j))
    im = v_ref[start : start + n, k:] - (nn(hi[:, k:], j) + nn(lo[:, k:], j))
    u = jnp.concatenate([re, im], axis=1)
    pack(u * jnp.concatenate([q, q], axis=1), out_ref)
    hi, lo = halves(u)
    us_ref[0] = hi
    us_ref[1] = lo


def third_body(gs_ref, us_ref, near_ref, far_ref, e0_ref, mc_ref, dep_ref, part_ref, p_ref, *, start):
    n = gs_ref.shape[1]
    k = e0_ref.shape[0]
    e = e0_ref[...]
    for i in range(2):
        cols = slice(i * k, i * k + k)
        y = jnp.concatenate([near_ref[i, start : start + n], far_ref[i, start : start + n]], axis=1)
        part_ref[i] = y - (nn(gs_ref[0, :, cols], e) + nn(gs_ref[1, :, cols], e))
    mc = mc_ref[...]
    p_ref[...] = nn(us_ref[0], mc) + nn(us_ref[1], mc)


def finish(in_ref, part_ref, p_ref, khi, klo, e):
    k = e.shape[0]
    p = p_ref[...] + apply_packed(in_ref, khi, klo)
    hi, lo = halves(p)
    for i in range(2):
        cols = slice(i * k, i * k + k)
        yield i, part_ref[i] - (nn(hi[:, cols], e) + nn(lo[:, cols], e))


def writer(out_ref, sem, blocks):
    me = lax.axis_index("field")
    copies = []

    def write(src_ref, i, row):
        n = src_ref.shape[2] // blocks
        for m in range(blocks):
            col = pl.multiple_of((me ^ m) * n, n)
            copy = pltpu.make_async_copy(
                src_ref.at[i, :, pl.ds(m * n, n)],
                out_ref.at[i, pl.ds(row, src_ref.shape[1]), pl.ds(col, n)],
                sem.at[len(copies)],
            )
            copy.start()
            copies.append(copy)

    return write, copies


def last_body(khi_ref, klo_ref, e1_ref, in_ref, part_ref, p_ref, *rest, start, blocks, done_at):
    out_ref, hold_ref, sem = rest[-3:]
    write, copies = writer(out_ref, sem, blocks)
    if done_at is not None:
        write(rest[0], slice(None), done_at)
    for i, value in finish(in_ref, part_ref, p_ref, khi_ref[...], klo_ref[...], e1_ref[...]):
        hold_ref[i] = value
        write(hold_ref, i, start)
    for copy in copies:
        copy.wait()


def body(incident, leaf_inverse, contrast, skel_index, ranks, top_core):
    nf, width = incident.shape[1:]
    boxes, _, kmax = skel_index.shape
    quarter = top_core.shape[2]
    own = leaf_inverse[0]
    across = swap(own, "field", 2)
    beside = swap(own, "field", 1)
    core_own = jnp.swapaxes(top_core, 1, 2).reshape(2 * quarter, kmax)
    core_near = swap(core_own, "box", 1)
    n = n_rows = own.shape[1]
    (opened,) = call(open_body, "open", [shape(8, 128)], [], cost=4.0)
    e0, e1, q, ghi, glo, g1, dup01, dup11, part, part1, hhi, hlo, dupm = call(
        lambda *refs: plan_body(*refs, parts=lax.axis_size("field")),
        "plan",
        [
            shape(kmax, width, dtype=BF),
            shape(kmax, width, dtype=BF),
            shape(8, kmax),
            shape(2 * kmax, 2 * kmax, dtype=BF),
            shape(2 * kmax, 2 * kmax, dtype=BF),
            shape(kmax, 2 * kmax),
            shape(kmax, kmax, dtype=BF),
            shape(kmax, kmax, dtype=BF),
            shape(kmax, 2 * width, dtype=BF),
            shape(kmax, 2 * width, dtype=BF),
            shape(2 * kmax, 2 * kmax, dtype=BF),
            shape(2 * kmax, 2 * kmax, dtype=BF),
            shape(kmax, kmax, dtype=BF),
        ],
        [ranks.T, skel_index, contrast.reshape(1, width), own, beside, opened],
        [VMEM] * 5 + [ANY],
    )
    x = incident
    (near,) = call(
        leaf_body, "near", [shape(2, nf, 2 * n)], [x, own, beside, part], [VMEM] * 3 + [ANY], cost=0.7
    )
    (pair,) = call(
        pair_body, "pair", [shape(2, 2 * quarter, kmax, dtype=BF)], [core_own, core_near, near], [VMEM, VMEM, ANY], cost=0.05
    )
    core_far = swap(pair, "box", 2)
    (across,) = call(
        relay_body, "relay", [shape(*across.shape, dtype=BF)], [across, pair, near], [VMEM, ANY, ANY], cost=0.05
    )
    beyond = swap(across, "field", 1)
    chunks = [nf // sum(SHARES) * share for share in SHARES]
    sizes = [(sum(chunks[:i]), n) for i, n in enumerate(chunks)]
    start, n = sizes[0]
    side_start, side_n = sizes[2]
    picked, head, side = call(
        lambda *refs, start=start, n=n: first_body(*refs, start=start, n=n, side_start=side_start),
        "first",
        [
            shape(kmax, 2 * width, dtype=BF),
            packed_shape(n, kmax),
            packed_shape(side_n, kmax),
        ],
        [part, across, beyond, e0, x, q],
        cost=0.8,
    )

    got = swap(head, "box", 1)
    picked1, ahead = call(
        lambda *refs: ahead_body(*refs, start=side_start, n=side_n),
        "ahead",
        [shape(kmax, 2 * width, dtype=BF), shape(2 * packed_shape(side_n, kmax).shape[0], LANES, dtype=jnp.int16)],
        [x, part1, across, beyond, e1, side, q, head],
        [VMEM] * 7 + [ANY],
        cost=1.4,
    )
    mate = swap(ahead, "box", 2)
    start, n = sizes[1]
    (packed,) = call(
        lambda *refs: rest_body(*refs, start=start, n=n),
        "ready",
        [packed_shape(n, kmax)],
        [x, picked, q, ahead],
        [VMEM] * 3 + [ANY],
        cost=0.6,
    )
    coming = swap(packed, "box", 1)
    (v1,) = call(rows_body, "rows", [shape(nf, 2 * kmax)], [x, picked1, packed], [VMEM] * 2 + [ANY])
    mc, khi, klo = call(
        core_body,
        "core",
        [shape(2 * kmax, 2 * kmax, dtype=BF)] * 3,
        [core_own, core_near, core_far, g1, dup11, v1],
        [VMEM] * 5 + [ANY],
        [pltpu.VMEM((kmax, 2 * kmax), BF)],
    )
    (far,) = call(
        leaf_body, "leaf", [shape(2, nf, 2 * n_rows)], [x, across, beyond, mc], [VMEM] * 3 + [ANY], cost=0.7
    )
    late = []
    for i, (start, n) in enumerate(sizes[:2]):
        back, gs, us = call(
            lambda *refs, start=start: second_body(*refs, start=start),
            f"second{i}",
            [packed_shape(n, kmax), shape(2, n, 2 * kmax, dtype=BF), shape(2, n, 2 * kmax, dtype=BF)],
            [got, ghi, glo, v1, dup01, q, sent if i else far],
            [VMEM] * 6 + [ANY],
            cost=0.8,
        )
        got = coming
        late.append([swap(back, "box", 2), gs, us])
        if i == 0:
            (onward,) = call(onward_body, "onward", [shape(*ahead.shape, dtype=jnp.int16)], [ahead, mate], cost=0.05)
            sent = onward
            onward = swap(onward, "box", 1)
    for i, (start, n) in enumerate(sizes[:2]):
        late[i][1:] = call(
            lambda *refs, start=start: third_body(*refs, start=start),
            f"third{i}",
            [shape(2, n, width), shape(n, 2 * kmax)],
            [late[i][1], late[i][2], near, far, e0, mc, gs],
            [VMEM] * 6 + [ANY],
            cost=0.5,
        )
    side = call(
        lambda *refs: around_body(*refs, start=side_start),
        "around",
        [shape(2, side_n, width)],
        [onward, mate, ghi, glo, hhi, hlo, dup01, dupm, v1, near, far, e0, e1, mc, khi, klo],
        cost=2.5,
    )
    blocks = lax.axis_size("field")
    out = []
    for i, (start, n) in enumerate(sizes[:2]):
        ready = side if i == 1 else []
        out = call(
            lambda *refs, start=start, ready=ready: last_body(
                *refs, start=start, blocks=blocks, done_at=side_start if ready else None
            ),
            f"last{i}",
            [shape(2, nf, width)],
            [khi, klo, e1] + late[i] + ready + out,
            [VMEM] * (6 + len(ready)) + [ANY] * len(out),
            [pltpu.VMEM((2, n, width), F32), pltpu.SemaphoreType.DMA(((3 if ready else 2) * blocks,))],
            out_specs=[ANY],
            input_output_aliases={6 + len(ready): 0} if out else {},
        )
    return out[0]


def solution(mesh):
    return jax.shard_map(
        body,
        mesh=mesh,
        in_specs=(P(None, "field", "box"), P("box", None, "field", None), P("box"), P(), P(), P(None, None, "box")),
        out_specs=P(None, "field", "box"),
        check_vma=False,
    )
```
